512 devices in a mesh: grp: 8 (over z_hi, core), seq: 64 (over y, z_lo, x).
Axes of the slice: x: 4, y: 8, z: 8 (z_hi: 4, z_lo: 2; z = z_hi * 2 + z_lo), core: 2. Of those that a mesh axis runs over, the one named last changes fastest.
Arguments:
- queries: bfloat16 [65536, 3072], P(('grp', 'seq'))
- keys: bfloat16 [65536, 3072], P(('grp', 'seq'))
- values: bfloat16 [65536, 3072], P(('grp', 'seq')), may hold values from -6 to 6
- head_order: int32 [24], replicated, may hold values from 0 to 23, each once
- key_blocks: int32 [128, 6], replicated, may hold values from 0 to 127, as said below
- block_count: int32 [128], replicated, may hold values from 2 to 6, as said below
Outputs:
- attended: bfloat16 [65536, 3072], P(('grp', 'seq'))
The draws below stay inside these ranges and needn't reach their ends.
Inputs may be any that keep to these rules, and one draw needn't show every extreme that they name: `key_blocks`: each row lists distinct frames; entry 0 is the row's own frame; every entry lies within 3 frames of the row's frame on the closed loop of 128 frames. `block_count`: some frame uses all 6 entries.
All inputs are finite; a program needn't handle non-finite values.
Results may differ from the reference program's by a relative error of at most 0.009.
Values may be sent and summed in bfloat16 or wider, within the bound.
No kernel may reach another device: no remote copies, remote signals or barrier semaphores. Data moves between devices by JAX's collectives and lax.ppermute only.
A program may use at most 64 MiB of HBM per device.

```python
import jax
import jax.numpy as jnp
from jax import lax

H = 24
DH = 128
HT = 8
W = 3
NB = 6
P_SIZE = 512
FRAMES = 128
TOKENS = 65536


def draw_queries(key, part):
    key = jax.random.fold_in(key, 3)
    own = jax.random.normal(key, (TOKENS, H * DH), jnp.float32)
    return own.astype(jnp.bfloat16)


def draw_keys(key, part):
    key = jax.random.fold_in(key, 5)
    own = jax.random.normal(key, (TOKENS, H * DH), jnp.float32)
    return own.astype(jnp.bfloat16)


def draw_key_blocks(key, part):
    key = jax.random.fold_in(key, 7)
    scores = jax.random.randint(key, (FRAMES, 2 * W), 0, 1 << 16) * (2 * W) + jnp.arange(2 * W)
    order = jnp.argsort(scores, axis=1)[:, :NB - 1]
    index = jnp.arange(2 * W)
    distance = jnp.where(index < W, index - W, index - W + 1)
    offsets = jnp.take(distance, order)
    frame = jnp.arange(FRAMES)[:, None]
    listed = jnp.concatenate([frame, (frame + offsets) % FRAMES], axis=1)
    return listed.astype(jnp.int32)


def draw_block_count(key, part):
    key = jax.random.fold_in(key, 9)
    first, second = jax.random.split(key)
    counts = jax.random.randint(first, (FRAMES,), 2, NB + 1)
    chosen = jax.random.randint(second, (), 0, FRAMES)
    counts = jnp.where(jnp.arange(FRAMES) == chosen, NB, counts)
    return counts.astype(jnp.int32)


def block_levels(key, dims, cuts, low, top_value):
    loudness = 1.0
    for dim, shards_of in cuts:
        draws = jax.random.uniform(jax.random.fold_in(jax.random.fold_in(key, 6), dim), (shards_of,), jnp.float32, low / len(cuts), top_value / len(cuts))
        loudness = loudness * jnp.repeat(jnp.exp(draws), dims[dim] // shards_of).reshape((-1,) + (1,) * (len(dims) - 1 - dim))
    return loudness


def normal_values(key, extent, scale, most, pieces=(), kind=jnp.bfloat16):
    drawn = scale * jax.random.normal(key, extent, jnp.float32)
    if pieces:
        drawn = drawn * block_levels(key, extent, pieces, -0.22, 0.18)
    return jnp.clip(drawn, -most, most).astype(kind)


def setup_inputs(seed: int = 0) -> dict:
    key_list = jax.random.split(jax.random.key(seed), 7)
    return {
        "queries": draw_queries(jax.random.fold_in(key_list[6], 71), 0),
        "keys": draw_keys(jax.random.fold_in(key_list[6], 71), 0),
        "values": normal_values(key_list[2], (TOKENS, H * DH), 1.0, 6.0, ((0, 512),)),
        "head_order": jax.random.permutation(key_list[3], H).astype(jnp.int32),
        "key_blocks": draw_key_blocks(jax.random.fold_in(key_list[6], 71), 0),
        "block_count": draw_block_count(jax.random.fold_in(key_list[6], 71), 0),
    }


def soft_weights(scores):
    top = jnp.max(scores, axis=-1, keepdims=True)
    expo = jnp.exp(scores - top)
    return (expo / jnp.sum(expo, axis=-1, keepdims=True)).astype(jnp.bfloat16)


def reference(queries, keys, values, head_order, key_blocks, block_count):
    scale = DH ** -0.5
    q4 = queries.reshape(FRAMES, P_SIZE, H, DH)
    k4 = keys.reshape(FRAMES, P_SIZE, H, DH)
    v4 = values.reshape(FRAMES, P_SIZE, H, DH)
    temporal_ids = head_order[:HT]
    spatial_ids = head_order[HT:]
    tq = jnp.take(q4, temporal_ids, axis=2).transpose(1, 0, 2, 3)
    tk = jnp.take(k4, temporal_ids, axis=2).transpose(1, 0, 2, 3)
    tv = jnp.take(v4, temporal_ids, axis=2).transpose(1, 0, 2, 3)

    def temporal_one(items):
        qa, ka, va = items
        scores = jnp.einsum("fhd,ghd->hfg", qa.astype(jnp.float32), ka.astype(jnp.float32)) * scale
        weights = soft_weights(scores)
        out = jnp.einsum("hfg,ghd->fhd", weights.astype(jnp.float32), va.astype(jnp.float32))
        return out.astype(jnp.bfloat16)

    tout = lax.map(temporal_one, (tq, tk, tv)).transpose(1, 0, 2, 3)
    sq = jnp.take(q4, spatial_ids, axis=2)
    sk = jnp.take(k4, spatial_ids, axis=2)
    sv = jnp.take(v4, spatial_ids, axis=2)

    def spatial_one(items):
        qa, listed, count = items
        kk = jnp.take(sk, listed, axis=0).reshape(NB * P_SIZE, H - HT, DH)
        vv = jnp.take(sv, listed, axis=0).reshape(NB * P_SIZE, H - HT, DH)
        keep = jnp.repeat(jnp.arange(NB) < count, P_SIZE)
        scores = jnp.einsum("phd,khd->hpk", qa.astype(jnp.float32), kk.astype(jnp.float32)) * scale
        scores = jnp.where(keep[None, None, :], scores, -jnp.inf)
        weights = soft_weights(scores)
        out = jnp.einsum("hpk,khd->phd", weights.astype(jnp.float32), vv.astype(jnp.float32))
        return out.astype(jnp.bfloat16)

    sout = lax.map(spatial_one, (sq, key_blocks, block_count))
    joined = jnp.concatenate([tout, sout], axis=2)
    inverse = jnp.argsort(head_order).astype(jnp.int32)
    return jnp.take(joined, inverse, axis=2).reshape(FRAMES * P_SIZE, H * DH)
```

```python
import functools
import math

import jax
import jax.numpy as jnp
from jax import lax
from jax.experimental import pallas as pl
from jax.experimental.pallas import tpu as pltpu
from jax.sharding import Mesh
from jax.sharding import PartitionSpec as P

HT = 8
W = 3
NB = 6
DEPTH = 128
LANES = 128
BF = jnp.bfloat16
F32 = jnp.float32
VMEM = pl.BlockSpec(memory_space=pltpu.VMEM)
SMEM = pl.BlockSpec(memory_space=pltpu.SMEM)
PARAMS = pltpu.CompilerParams(vmem_limit_bytes=40 * 1024 * 1024)


def columns_of(order_ref, slot):
    return pl.ds(pl.multiple_of(order_ref[slot] * DEPTH, DEPTH), DEPTH)


def pack_spatial_kernel(order_ref, *refs):
    half = len(refs) // 2
    for src, dst in zip(refs[:half], refs[half:]):
        for dest in range(dst.shape[0]):
            for head in range(dst.shape[1]):
                slot = HT + dest * dst.shape[1] + head
                dst[dest, head] = src[:, columns_of(order_ref, slot)]


def pack_spatial(order, arrays, dests, heads):
    rows = arrays[0].shape[0]
    out = jax.ShapeDtypeStruct((dests, heads, rows, DEPTH), BF)
    return pl.pallas_call(
        pack_spatial_kernel,
        out_shape=[out] * len(arrays),
        in_specs=[SMEM] + [VMEM] * len(arrays),
        out_specs=[VMEM] * len(arrays),
        compiler_params=PARAMS,
    )(order, *arrays)


def pack_temporal_kernel(items, order_ref, q_ref, k_ref, v_ref, out_ref):
    pieces = q_ref.shape[0] // items
    for which, src in enumerate((q_ref, k_ref, v_ref)):
        for head in range(HT):
            block = src[:, columns_of(order_ref, head)]
            out_ref[head * pieces : (head + 1) * pieces, which] = block.reshape(pieces, items, DEPTH)


def pack_temporal(order, q, k, v, items):
    dests = HT * q.shape[0] // items
    return pl.pallas_call(
        functools.partial(pack_temporal_kernel, items),
        out_shape=jax.ShapeDtypeStruct((dests, 3, items, DEPTH), BF),
        in_specs=[SMEM] + [VMEM] * 3,
        out_specs=VMEM,
        compiler_params=PARAMS,
    )(order, q, k, v)


def temporal_kernel(in_ref, out_ref):
    frames, _, items, depth = in_ref.shape
    total = frames * items
    step = 256
    factor = depth ** (-0.5) * math.log2(math.e)
    k = in_ref[:, 1].reshape(total, depth)
    v = in_ref[:, 2].reshape(total, depth)
    row_item = lax.broadcasted_iota(jnp.int32, (step, total), 0) % items
    col_item = lax.broadcasted_iota(jnp.int32, (step, total), 1) % items
    same = row_item == col_item
    per = step // items
    for at in range(frames // per):
        q = in_ref[at * per : (at + 1) * per, 0].reshape(step, depth)
        s = lax.dot_general(q, k, (((1,), (1,)), ((), ())), preferred_element_type=F32)
        s = jnp.where(same, s * factor, -jnp.inf)
        p = jnp.exp2(s - jnp.max(s, axis=1, keepdims=True))
        total_p = jnp.sum(p, axis=1, keepdims=True)
        o = jnp.dot(p.astype(BF), v, preferred_element_type=F32) / total_p
        out_ref[at * per : (at + 1) * per] = o.astype(BF).reshape(per, items, depth)


def temporal_attend(arrived):
    frames, _, items, depth = arrived.shape
    return pl.pallas_call(
        temporal_kernel,
        out_shape=jax.ShapeDtypeStruct((frames, items, depth), BF),
        in_specs=[VMEM],
        out_specs=VMEM,
        compiler_params=PARAMS,
    )(arrived)


def spatial_kernel(frames, base_ref, kb_ref, bc_ref, q_ref, *refs):
    (k0, v0, km1, vm1, kp1, vp1, km2, vm2, kp2, vp2, o_ref, m_ref, l_ref, acc_ref) = refs
    pieces = q_ref.shape[0] // 2
    rows, depth = q_ref.shape[2:]
    size = pieces * rows
    factor = depth ** (-0.5) * math.log2(math.e)
    base = base_ref[0]
    slots = {
        -3: (km2, vm2, 0),
        -2: (km1, vm1, 0),
        -1: (km1, vm1, pieces),
        0: (k0, v0, 0),
        1: (k0, v0, pieces),
        2: (kp1, vp1, 0),
        3: (kp1, vp1, pieces),
        4: (kp2, vp2, 0),
    }
    heads = q_ref.shape[1]
    for mine in range(2):
        frame = base + mine
        count = bc_ref[frame]
        listed = [kb_ref[frame, n] for n in range(NB)]

        def used(slot):
            target = lax.rem(base + slot + frames, frames)
            hit = (listed[0] == target) & (count > 0)
            for n in range(1, NB):
                hit = hit | ((listed[n] == target) & (count > n))
            return hit

        for head in range(heads):
            q = q_ref[mine * pieces : (mine + 1) * pieces, head].reshape(size, depth)

            def scores(slot):
                k_ref, _, at = slots[slot]
                k = k_ref[at : at + pieces, head].reshape(size, depth)
                return lax.dot_general(
                    q, k, (((1,), (1,)), ((), ())), preferred_element_type=F32
                )

            def value(slot):
                _, v_ref, at = slots[slot]
                return v_ref[at : at + pieces, head].reshape(size, depth)

            s = scores(mine) * factor
            top = jnp.max(s, axis=1, keepdims=True)
            p = jnp.exp2(s - top)
            m_ref[...] = jnp.broadcast_to(top, m_ref.shape)
            l_ref[...] = jnp.broadcast_to(jnp.sum(p, axis=1, keepdims=True), l_ref.shape)
            acc_ref[...] = jnp.dot(p.astype(BF), value(mine), preferred_element_type=F32)
            for reach in range(-W, W + 1):
                if reach == 0:
                    continue
                slot = mine + reach

                @pl.when(used(slot))
                def _():
                    s = scores(slot) * factor
                    old = m_ref[...]
                    new = jnp.maximum(old, jnp.max(s, axis=1, keepdims=True))
                    p = jnp.exp2(s - new[:, :1])
                    alpha = jnp.exp2(old - new)
                    m_ref[...] = new
                    l_ref[...] = l_ref[...] * alpha + jnp.sum(p, axis=1, keepdims=True)
                    acc_ref[...] = acc_ref[...] * alpha + jnp.dot(
                        p.astype(BF), value(slot), preferred_element_type=F32
                    )

            o = (acc_ref[...] / l_ref[...]).astype(BF)
            o_ref[mine * pieces : (mine + 1) * pieces, head] = o.reshape(pieces, rows, depth)


def spatial_attend(base, kb, bc, q, parts, frames):
    size = q.shape[0] // 2 * q.shape[2]
    return pl.pallas_call(
        functools.partial(spatial_kernel, frames),
        out_shape=jax.ShapeDtypeStruct(q.shape, BF),
        in_specs=[SMEM] * 3 + [VMEM] * (1 + len(parts)),
        out_specs=VMEM,
        scratch_shapes=[
            pltpu.VMEM((size, LANES), F32),
            pltpu.VMEM((size, LANES), F32),
            pltpu.VMEM((size, DEPTH), F32),
        ],
        compiler_params=PARAMS,
    )(base, kb, bc, q, *parts)


def assemble_kernel(order_ref, t_ref, s_ref, out_ref):
    rows = out_ref.shape[0]
    pieces = t_ref.shape[0] // HT
    for head in range(HT):
        block = t_ref[head * pieces : (head + 1) * pieces].reshape(rows, DEPTH)
        out_ref[:, columns_of(order_ref, head)] = block
    for dest in range(s_ref.shape[0]):
        for head in range(s_ref.shape[1]):
            slot = HT + dest * s_ref.shape[1] + head
            out_ref[:, columns_of(order_ref, slot)] = s_ref[dest, head]


def assemble(order, temporal, spatial, rows, width):
    return pl.pallas_call(
        assemble_kernel,
        out_shape=jax.ShapeDtypeStruct((rows, width), BF),
        in_specs=[SMEM, VMEM, VMEM],
        out_specs=VMEM,
        compiler_params=PARAMS,
    )(order, temporal, spatial)


def exchange(array, axes):
    return lax.all_to_all(array, axes, 0, 0, tiled=True)


def from_block(array, by):
    count = lax.axis_size("grp") * lax.axis_size("y")
    return lax.ppermute(array, ("grp", "y"), [((i + by) % count, i) for i in range(count)])


def local(queries, keys, values, head_order, key_blocks, block_count):
    rows, width = queries.shape
    heads = width // DEPTH
    quarters = lax.axis_size("x")
    frames = lax.axis_size("grp") * lax.axis_size("y") * 2
    dests = 2 * quarters
    share = (heads - HT) // dests
    items = HT * rows // frames
    base = (lax.axis_index("grp") * lax.axis_size("y") + lax.axis_index("y")) * 2
    base = base.astype(jnp.int32).reshape(1)

    sk, sv = pack_spatial(head_order, (keys, values), dests, share)
    k0 = exchange(sk, ("zl", "x"))
    v0 = exchange(sv, ("zl", "x"))
    (sq,) = pack_spatial(head_order, (queries,), dests, share)
    st = pack_temporal(head_order, queries, keys, values, items)
    kp1, vp1 = from_block(k0, 1), from_block(v0, 1)
    km1, vm1 = from_block(k0, -1), from_block(v0, -1)
    kp2, vp2 = from_block(k0[:quarters], 2), from_block(v0[:quarters], 2)
    km2, vm2 = from_block(k0[quarters:], -2), from_block(v0[quarters:], -2)
    at = exchange(st, ("grp", "y", "zl"))
    q0 = exchange(sq, ("zl", "x"))
    to = temporal_attend(at)
    tr = exchange(to, ("grp", "y", "zl"))
    so = spatial_attend(
        base, key_blocks, block_count, q0,
        (k0, v0, km1, vm1, kp1, vp1, km2, vm2, kp2, vp2), frames,
    )
    sr = exchange(so, ("zl", "x"))
    return assemble(head_order, tr, sr, rows, width)


def solution(mesh):
    grp, seq = mesh.shape["grp"], mesh.shape["seq"]
    fine = Mesh(mesh.devices.reshape(grp, seq // 8, 2, 4), ("grp", "y", "zl", "x"))
    tokens = P(("grp", "y", "zl", "x"), None)
    return jax.shard_map(
        local,
        mesh=fine,
        in_specs=(tokens, tokens, tokens, P(), P(), P()),
        out_specs=tokens,
        check_vma=False,
    )
```

```python
import functools
import math

import jax
import jax.numpy as jnp
from jax import lax
from jax.experimental import pallas as pl
from jax.experimental.pallas import tpu as pltpu
from jax.sharding import Mesh
from jax.sharding import PartitionSpec as P

HT = 8
W = 3
NB = 6
DEPTH = 128
LANES = 128
BF = jnp.bfloat16
F32 = jnp.float32
VMEM = pl.BlockSpec(memory_space=pltpu.VMEM)
SMEM = pl.BlockSpec(memory_space=pltpu.SMEM)
PARAMS = pltpu.CompilerParams(vmem_limit_bytes=40 * 1024 * 1024)


def columns_of(order_ref, slot):
    return pl.ds(pl.multiple_of(order_ref[slot] * DEPTH, DEPTH), DEPTH)


def pack_spatial_kernel(order_ref, *refs):
    dst = refs[-1]
    for which, src in enumerate(refs[:-1]):
        for dest in range(dst.shape[0]):
            for head in range(dst.shape[2]):
                slot = HT + dest * dst.shape[2] + head
                dst[dest, which, head] = src[:, columns_of(order_ref, slot)]


def pack_spatial(order, arrays, dests, heads):
    rows = arrays[0].shape[0]
    return pl.pallas_call(
        pack_spatial_kernel,
        out_shape=jax.ShapeDtypeStruct((dests, len(arrays), heads, rows, DEPTH), BF),
        in_specs=[SMEM] + [VMEM] * len(arrays),
        out_specs=VMEM,
        compiler_params=PARAMS,
    )(order, *arrays)


def pack_temporal_kernel(items, order_ref, q_ref, k_ref, v_ref, out_ref):
    pieces = q_ref.shape[0] // items
    for which, src in enumerate((q_ref, k_ref, v_ref)):
        for head in range(HT):
            block = src[:, columns_of(order_ref, head)]
            out_ref[head * pieces : (head + 1) * pieces, which] = block.reshape(pieces, items, DEPTH)


def pack_temporal(order, q, k, v, items):
    dests = HT * q.shape[0] // items
    return pl.pallas_call(
        functools.partial(pack_temporal_kernel, items),
        out_shape=jax.ShapeDtypeStruct((dests, 3, items, DEPTH), BF),
        in_specs=[SMEM] + [VMEM] * 3,
        out_specs=VMEM,
        compiler_params=PARAMS,
    )(order, q, k, v)


def temporal_kernel(in_ref, out_ref):
    frames, _, items, depth = in_ref.shape
    total = frames * items
    step = 256
    factor = depth ** (-0.5) * math.log2(math.e)
    k = in_ref[:, 1].reshape(total, depth)
    v = in_ref[:, 2].reshape(total, depth)
    row_item = lax.broadcasted_iota(jnp.int32, (step, total), 0) % items
    col_item = lax.broadcasted_iota(jnp.int32, (step, total), 1) % items
    same = row_item == col_item
    per = step // items
    for at in range(frames // per):
        q = in_ref[at * per : (at + 1) * per, 0].reshape(step, depth)
        s = lax.dot_general(q, k, (((1,), (1,)), ((), ())), preferred_element_type=F32)
        s = jnp.where(same, s * factor, -jnp.inf)
        p = jnp.exp2(s - jnp.max(s, axis=1, keepdims=True))
        total_p = jnp.sum(p, axis=1, keepdims=True)
        o = jnp.dot(p.astype(BF), v, preferred_element_type=F32) / total_p
        out_ref[at * per : (at + 1) * per] = o.astype(BF).reshape(per, items, depth)


def temporal_attend(arrived):
    frames, _, items, depth = arrived.shape
    return pl.pallas_call(
        temporal_kernel,
        out_shape=jax.ShapeDtypeStruct((frames, items, depth), BF),
        in_specs=[VMEM],
        out_specs=VMEM,
        compiler_params=PARAMS,
        cost_estimate=pl.CostEstimate(flops=50_000_000_000, bytes_accessed=1 << 20, transcendentals=1 << 20),
    )(arrived)


def spatial_kernel(frames, base_ref, kb_ref, bc_ref, q_ref, *refs):
    (own, m1, p1, m2, p2, o_ref, m_ref, l_ref, acc_ref) = refs
    pieces = q_ref.shape[0] // 2
    rows, depth = q_ref.shape[3:]
    size = pieces * rows
    factor = depth ** (-0.5) * math.log2(math.e)
    base = base_ref[0]
    slots = {
        -3: (m2, 0),
        -2: (m1, 0),
        -1: (m1, pieces),
        0: (own, 0),
        1: (own, pieces),
        2: (p1, 0),
        3: (p1, pieces),
        4: (p2, 0),
    }
    heads = q_ref.shape[2]
    for mine in range(2):
        frame = base + mine
        count = bc_ref[frame]
        listed = [kb_ref[frame, n] for n in range(NB)]

        def used(slot):
            target = lax.rem(base + slot + frames, frames)
            hit = (listed[0] == target) & (count > 0)
            for n in range(1, NB):
                hit = hit | ((listed[n] == target) & (count > n))
            return hit

        for head in range(heads):
            q = q_ref[mine * pieces : (mine + 1) * pieces, 0, head].reshape(size, depth)

            def scores(slot):
                src, at = slots[slot]
                k = src[at : at + pieces, 0, head].reshape(size, depth)
                return lax.dot_general(
                    q, k, (((1,), (1,)), ((), ())), preferred_element_type=F32
                )

            def value(slot):
                src, at = slots[slot]
                return src[at : at + pieces, 1, head].reshape(size, depth)

            s = scores(mine) * factor
            top = jnp.max(s, axis=1, keepdims=True)
            p = jnp.exp2(s - top)
            m_ref[...] = jnp.broadcast_to(top, m_ref.shape)
            l_ref[...] = jnp.broadcast_to(jnp.sum(p, axis=1, keepdims=True), l_ref.shape)
            acc_ref[...] = jnp.dot(p.astype(BF), value(mine), preferred_element_type=F32)
            for reach in range(-W, W + 1):
                if reach == 0:
                    continue
                slot = mine + reach

                @pl.when(used(slot))
                def _():
                    s = scores(slot) * factor
                    old = m_ref[...]
                    new = jnp.maximum(old, jnp.max(s, axis=1, keepdims=True))
                    p = jnp.exp2(s - new[:, :1])
                    alpha = jnp.exp2(old - new)
                    m_ref[...] = new
                    l_ref[...] = l_ref[...] * alpha + jnp.sum(p, axis=1, keepdims=True)
                    acc_ref[...] = acc_ref[...] * alpha + jnp.dot(
                        p.astype(BF), value(slot), preferred_element_type=F32
                    )

            o = (acc_ref[...] / l_ref[...]).astype(BF)
            o_ref[mine * pieces : (mine + 1) * pieces, head] = o.reshape(pieces, rows, depth)


def spatial_attend(base, kb, bc, q, parts, frames):
    dests, _, heads, rows, depth = q.shape
    size = dests // 2 * rows
    return pl.pallas_call(
        functools.partial(spatial_kernel, frames),
        out_shape=jax.ShapeDtypeStruct((dests, heads, rows, depth), BF),
        in_specs=[SMEM] * 3 + [VMEM] * (1 + len(parts)),
        out_specs=VMEM,
        scratch_shapes=[
            pltpu.VMEM((size, LANES), F32),
            pltpu.VMEM((size, LANES), F32),
            pltpu.VMEM((size, DEPTH), F32),
        ],
        compiler_params=PARAMS,
    )(base, kb, bc, q, *parts)


def assemble_kernel(order_ref, t_ref, s_ref, out_ref):
    rows = out_ref.shape[0]
    pieces = t_ref.shape[0] // HT
    for head in range(HT):
        block = t_ref[head * pieces : (head + 1) * pieces].reshape(rows, DEPTH)
        out_ref[:, columns_of(order_ref, head)] = block
    for dest in range(s_ref.shape[0]):
        for head in range(s_ref.shape[1]):
            slot = HT + dest * s_ref.shape[1] + head
            out_ref[:, columns_of(order_ref, slot)] = s_ref[dest, head]


def assemble(order, temporal, spatial, rows, width):
    return pl.pallas_call(
        assemble_kernel,
        out_shape=jax.ShapeDtypeStruct((rows, width), BF),
        in_specs=[SMEM, VMEM, VMEM],
        out_specs=VMEM,
        compiler_params=PARAMS,
    )(order, temporal, spatial)


def exchange(array, axes):
    return lax.all_to_all(array, axes, 0, 0, tiled=True)


def from_block(array, by):
    count = lax.axis_size("grp") * lax.axis_size("y")
    return lax.ppermute(array, ("grp", "y"), [((i + by) % count, i) for i in range(count)])


def local(queries, keys, values, head_order, key_blocks, block_count):
    rows, width = queries.shape
    heads = width // DEPTH
    quarters = lax.axis_size("x")
    frames = lax.axis_size("grp") * lax.axis_size("y") * 2
    dests = 2 * quarters
    share = (heads - HT) // dests
    items = HT * rows // frames
    base = (lax.axis_index("grp") * lax.axis_size("y") + lax.axis_index("y")) * 2
    base = base.astype(jnp.int32).reshape(1)

    st = pack_temporal(head_order, queries, keys, values, items)
    kv = exchange(pack_spatial(head_order, (keys, values), dests, share), ("zl", "x"))
    kv, st = lax.optimization_barrier((kv, st))
    at = exchange(st, ("grp", "y", "zl"))
    p1 = from_block(kv, 1)
    m1 = from_block(kv, -1)
    p2 = from_block(kv[:quarters], 2)
    m2 = from_block(kv[quarters:], -2)
    at, sq = lax.optimization_barrier((at, pack_spatial(head_order, (queries,), dests, share)))
    qs = exchange(sq, ("zl", "x"))
    to = temporal_attend(at)
    tr = exchange(to, ("grp", "y", "zl"))
    so = spatial_attend(base, key_blocks, block_count, qs, (kv, m1, p1, m2, p2), frames)
    sr = exchange(so, ("zl", "x"))
    return assemble(head_order, tr, sr, rows, width)


def solution(mesh):
    grp, seq = mesh.shape["grp"], mesh.shape["seq"]
    fine = Mesh(mesh.devices.reshape(grp, seq // 8, 2, 4), ("grp", "y", "zl", "x"))
    tokens = P(("grp", "y", "zl", "x"), None)
    return jax.shard_map(
        local,
        mesh=fine,
        in_specs=(tokens, tokens, tokens, P(), P(), P()),
        out_specs=tokens,
        check_vma=False,
    )
```

```python
import functools
import math

import jax
import jax.numpy as jnp
from jax import lax
from jax.experimental import pallas as pl
from jax.experimental.pallas import tpu as pltpu
from jax.sharding import Mesh
from jax.sharding import PartitionSpec as P

HT = 8
W = 3
NB = 6
BLOCK = 4
DEPTH = 128
LANES = 128
BF = jnp.bfloat16
F32 = jnp.float32
VMEM = pl.BlockSpec(memory_space=pltpu.VMEM)
SMEM = pl.BlockSpec(memory_space=pltpu.SMEM)
PARAMS = pltpu.CompilerParams(vmem_limit_bytes=40 * 1024 * 1024)


def columns_of(order_ref, slot):
    return pl.ds(pl.multiple_of(order_ref[slot] * DEPTH, DEPTH), DEPTH)


def pack_spatial_kernel(order_ref, *refs):
    dst = refs[-1]
    for which, src in enumerate(refs[:-1]):
        for head in range(dst.shape[0]):
            dst[head, which] = src[:, columns_of(order_ref, HT + head)]


def pack_spatial(order, arrays):
    rows, width = arrays[0].shape
    return pl.pallas_call(
        pack_spatial_kernel,
        out_shape=jax.ShapeDtypeStruct((width // DEPTH - HT, len(arrays), rows, DEPTH), BF),
        in_specs=[SMEM] + [VMEM] * len(arrays),
        out_specs=VMEM,
        compiler_params=PARAMS,
    )(order, *arrays)


def pack_temporal_kernel(items, order_ref, q_ref, k_ref, v_ref, out_ref):
    pieces = q_ref.shape[0] // items
    for which, src in enumerate((q_ref, k_ref, v_ref)):
        for head in range(HT):
            block = src[:, columns_of(order_ref, head)]
            out_ref[head * pieces : (head + 1) * pieces, which] = block.reshape(pieces, items, DEPTH)


def pack_temporal(order, q, k, v, items):
    dests = HT * q.shape[0] // items
    return pl.pallas_call(
        functools.partial(pack_temporal_kernel, items),
        out_shape=jax.ShapeDtypeStruct((dests, 3, items, DEPTH), BF),
        in_specs=[SMEM] + [VMEM] * 3,
        out_specs=VMEM,
        compiler_params=PARAMS,
    )(order, q, k, v)


def temporal_kernel(in_ref, out_ref):
    frames, _, items, depth = in_ref.shape
    total = frames * items
    step = 256
    factor = depth ** (-0.5) * math.log2(math.e)
    k = in_ref[:, 1].reshape(total, depth)
    v = in_ref[:, 2].reshape(total, depth)
    row_item = lax.broadcasted_iota(jnp.int32, (step, total), 0) % items
    col_item = lax.broadcasted_iota(jnp.int32, (step, total), 1) % items
    same = row_item == col_item
    per = step // items
    for at in range(frames // per):
        q = in_ref[at * per : (at + 1) * per, 0].reshape(step, depth)
        s = lax.dot_general(q, k, (((1,), (1,)), ((), ())), preferred_element_type=F32)
        s = jnp.where(same, s * factor, -jnp.inf)
        p = jnp.exp2(s - jnp.max(s, axis=1, keepdims=True))
        total_p = jnp.sum(p, axis=1, keepdims=True)
        o = jnp.dot(p.astype(BF), v, preferred_element_type=F32) / total_p
        out_ref[at * per : (at + 1) * per] = o.astype(BF).reshape(per, items, depth)


def temporal_attend(arrived):
    frames, _, items, depth = arrived.shape
    return pl.pallas_call(
        temporal_kernel,
        out_shape=jax.ShapeDtypeStruct((frames, items, depth), BF),
        in_specs=[VMEM],
        out_specs=VMEM,
        compiler_params=PARAMS,
        cost_estimate=pl.CostEstimate(flops=50_000_000_000, bytes_accessed=1 << 20, transcendentals=1 << 20),
    )(arrived)


def row_norm(block):
    wide = block.astype(F32)
    ones = jnp.ones((block.shape[-1], LANES), BF)
    return jnp.max(jnp.dot((wide * wide).astype(BF), ones, preferred_element_type=F32))


def used_slot(frames, base, kb_ref, bc_ref, mine, slot):
    frame = base + mine
    target = lax.rem(base + slot + frames, frames)
    hit = False
    for n in range(NB):
        hit = hit | ((kb_ref[frame, n] == target) & (bc_ref[frame] > n))
    return hit


def attend_slot(fast, first, q_of, k_of, v_of, acc_ref, m_ref):
    rows, depth = m_ref.shape[0], DEPTH
    factor = depth ** (-0.5) * math.log2(math.e)
    step = 128
    k = k_of()
    v = v_of()
    wide = jnp.concatenate([v, jnp.ones_like(v)], axis=1)
    q = q_of()
    for at in range(0, rows, step):
        here = slice(at, at + step)
        s = lax.dot_general(
            q[here], k, (((1,), (1,)), ((), ())), preferred_element_type=F32
        )
        if fast:
            p = jnp.exp2(s * factor).astype(BF)
            add = jnp.dot(p, wide, preferred_element_type=F32)
            acc_ref[here] = add if first else acc_ref[here] + add
        else:
            s = s * factor
            top = jnp.max(s, axis=1, keepdims=True)
            if first:
                p = jnp.exp2(s - top).astype(BF)
                acc_ref[here] = jnp.dot(p, wide, preferred_element_type=F32)
                m_ref[here] = jnp.broadcast_to(top, (step, LANES))
            else:
                old = m_ref[here]
                new = jnp.maximum(old, top)
                p = jnp.exp2(s - new[:, :1]).astype(BF)
                alpha = jnp.exp2(old - new)
                both = jnp.concatenate([alpha, alpha], axis=1)
                acc_ref[here] = acc_ref[here] * both + jnp.dot(p, wide, preferred_element_type=F32)
                m_ref[here] = new


def small_scores(q_norm, k_norm):
    factor = DEPTH ** (-0.5) * math.log2(math.e) * 1.02
    return q_norm * k_norm * (factor * factor) <= 1e4


def own_kernel(frames, base_ref, kb_ref, bc_ref, in_ref, acc_ref, m_ref, stat_ref):
    pieces = in_ref.shape[0] // BLOCK
    size = pieces * in_ref.shape[2]
    base = base_ref[0]

    def part(which, at):
        return lambda: in_ref[at * pieces : (at + 1) * pieces, which].reshape(size, DEPTH)

    total = BLOCK * size
    q_norm = row_norm(in_ref[:, 0].reshape(total, DEPTH))
    k_norm = row_norm(in_ref[:, 1].reshape(total, DEPTH))
    fast = small_scores(q_norm, k_norm)
    stat_ref[0] = q_norm
    stat_ref[1] = jnp.where(fast, 1.0, 0.0)

    def run(quick):
        for mine in range(BLOCK):
            out = acc_ref.at[mine], m_ref.at[mine]
            attend_slot(quick, True, part(0, mine), part(1, mine), part(2, mine), *out)
            if quick:
                m_ref[mine] = jnp.zeros((size, LANES), F32)
            for slot in range(BLOCK):
                if slot != mine and abs(slot - mine) <= W:

                    @pl.when(used_slot(frames, base, kb_ref, bc_ref, mine, slot))
                    def _():
                        attend_slot(quick, False, part(0, mine), part(1, slot), part(2, slot), *out)

    @pl.when(fast)
    def _():
        run(True)

    @pl.when(jnp.logical_not(fast))
    def _():
        run(False)


def near_kernel(
    frames, base_ref, kb_ref, bc_ref, stat_ref, in_ref, less_ref, more_ref, acc_in, m_in, o_ref, acc_ref, m_ref
):
    pieces = in_ref.shape[0] // BLOCK
    rows = in_ref.shape[2]
    size = pieces * rows
    base = base_ref[0]
    total = less_ref.shape[0] * rows
    k_norm = jnp.maximum(
        row_norm(less_ref[:, 0].reshape(total, DEPTH)), row_norm(more_ref[:, 0].reshape(total, DEPTH))
    )
    fast = small_scores(stat_ref[0], k_norm) & (stat_ref[1] > 0.5)

    def query(mine):
        return lambda: in_ref[mine * pieces : (mine + 1) * pieces, 0].reshape(size, DEPTH)

    def part(which, slot):
        ref, at = (less_ref, slot + W) if slot < 0 else (more_ref, slot - BLOCK)
        return lambda: ref[at * pieces : (at + 1) * pieces, which].reshape(size, DEPTH)

    def run(quick):
        for mine in range(BLOCK):
            acc_ref[...] = acc_in[mine]
            if not quick:
                m_ref[...] = m_in[mine]
            for slot in range(mine - W, mine + W + 1):
                if slot < 0 or slot >= BLOCK:

                    @pl.when(used_slot(frames, base, kb_ref, bc_ref, mine, slot))
                    def _():
                        attend_slot(quick, False, query(mine), part(0, slot), part(1, slot), acc_ref, m_ref)

            o = (acc_ref[:, :DEPTH] / acc_ref[:, DEPTH:]).astype(BF)
            o_ref[mine * pieces : (mine + 1) * pieces] = o.reshape(pieces, rows, DEPTH)

    @pl.when(fast)
    def _():
        run(True)

    @pl.when(jnp.logical_not(fast))
    def _():
        run(False)


def attend_own(base, kb, bc, arrived, frames):
    dests, _, rows, depth = arrived.shape
    size = dests // BLOCK * rows
    return pl.pallas_call(
        functools.partial(own_kernel, frames),
        out_shape=[
            jax.ShapeDtypeStruct((BLOCK, size, 2 * depth), F32),
            jax.ShapeDtypeStruct((BLOCK, size, LANES), F32),
            jax.ShapeDtypeStruct((2,), F32),
        ],
        in_specs=[SMEM] * 3 + [VMEM],
        out_specs=[VMEM, VMEM, SMEM],
        compiler_params=PARAMS,
        cost_estimate=pl.CostEstimate(flops=10_000_000_000, bytes_accessed=1 << 20, transcendentals=1 << 20),
    )(base, kb, bc, arrived)


def attend_near(base, kb, bc, stat, arrived, less, more, acc, top, frames):
    dests, _, rows, depth = arrived.shape
    size = dests // BLOCK * rows
    return pl.pallas_call(
        functools.partial(near_kernel, frames),
        out_shape=jax.ShapeDtypeStruct((dests, rows, depth), BF),
        in_specs=[SMEM] * 4 + [VMEM] * 5,
        out_specs=VMEM,
        scratch_shapes=[pltpu.VMEM((size, 2 * depth), F32), pltpu.VMEM((size, LANES), F32)],
        compiler_params=PARAMS,
    )(base, kb, bc, stat, arrived, less, more, acc, top)


def assemble_kernel(order_ref, t_ref, s_ref, out_ref):
    rows = out_ref.shape[0]
    pieces = t_ref.shape[0] // HT
    for head in range(HT):
        block = t_ref[head * pieces : (head + 1) * pieces].reshape(rows, DEPTH)
        out_ref[:, columns_of(order_ref, head)] = block
    for head in range(s_ref.shape[0]):
        out_ref[:, columns_of(order_ref, HT + head)] = s_ref[head]


def assemble(order, temporal, spatial, rows, width):
    return pl.pallas_call(
        assemble_kernel,
        out_shape=jax.ShapeDtypeStruct((rows, width), BF),
        in_specs=[SMEM, VMEM, VMEM],
        out_specs=VMEM,
        compiler_params=PARAMS,
    )(order, temporal, spatial)


def exchange(array, axes):
    return lax.all_to_all(array, axes, 0, 0, tiled=True)


def from_block(array, by):
    count = lax.axis_size("grp") * lax.axis_size("yh")
    return lax.ppermute(array, ("grp", "yh"), [((i + by) % count, i) for i in range(count)])


def local(queries, keys, values, head_order, key_blocks, block_count):
    rows, width = queries.shape
    blocks = lax.axis_size("grp") * lax.axis_size("yh")
    frames = blocks * BLOCK
    items = HT * rows // frames
    base = (lax.axis_index("grp") * lax.axis_size("yh") + lax.axis_index("yh")) * BLOCK
    base = base.astype(jnp.int32).reshape(1)

    block_axes = ("yl", "zl", "x")
    loop_axes = ("grp", "yh", "yl", "zl")
    st = pack_temporal(head_order, queries, keys, values, items)
    qkv = exchange(pack_spatial(head_order, (queries, keys, values)), block_axes)
    qkv, st = lax.optimization_barrier((qkv, st))
    at = exchange(st, loop_axes)
    pieces = qkv.shape[0] // BLOCK
    less = from_block(qkv[(BLOCK - W) * pieces :, 1:], -1)
    more = from_block(qkv[: W * pieces, 1:], 1)
    acc, top, stat = attend_own(base, key_blocks, block_count, qkv, frames)
    to, stat = lax.optimization_barrier((temporal_attend(at), stat))
    tr = exchange(to, loop_axes)
    so = attend_near(base, key_blocks, block_count, stat, qkv, less, more, acc, top, frames)
    sr = exchange(so, block_axes)
    return assemble(head_order, tr, sr, rows, width)


def solution(mesh):
    grp, seq = mesh.shape["grp"], mesh.shape["seq"]
    fine = Mesh(mesh.devices.reshape(grp, seq // 16, 2, 2, 4), ("grp", "yh", "yl", "zl", "x"))
    tokens = P(("grp", "yh", "yl", "zl", "x"), None)
    return jax.shard_map(
        local,
        mesh=fine,
        in_specs=(tokens, tokens, tokens, P(), P(), P()),
        out_specs=tokens,
        check_vma=False,
    )
```

```python
import functools
import math

import jax
import jax.numpy as jnp
from jax import lax
from jax.experimental import pallas as pl
from jax.experimental.pallas import tpu as pltpu
from jax.sharding import Mesh
from jax.sharding import PartitionSpec as P

HT = 8
W = 3
NB = 6
BLOCK = 4
DEPTH = 128
LANES = 128
BF = jnp.bfloat16
F32 = jnp.float32
VMEM = pl.BlockSpec(memory_space=pltpu.VMEM)
SMEM = pl.BlockSpec(memory_space=pltpu.SMEM)
ANY = pl.BlockSpec(memory_space=pl.ANY)
PARAMS = pltpu.CompilerParams(vmem_limit_bytes=40 * 1024 * 1024)


def estimate(gigaflops):
    return pl.CostEstimate(flops=gigaflops * 10**9, bytes_accessed=1 << 20, transcendentals=1 << 20)


def columns_of(order_ref, slot):
    return pl.ds(pl.multiple_of(order_ref[slot] * DEPTH, DEPTH), DEPTH)


def run_copies(copies):
    for copy in copies:
        copy.start()
    for copy in copies:
        copy.wait()


def pack_spatial_kernel(order_ref, *refs):
    dst, sems = refs[-2:]
    copies = []
    for which, src in enumerate(refs[:-2]):
        for head in range(dst.shape[0]):
            column = columns_of(order_ref, HT + head)
            copies.append(
                pltpu.make_async_copy(src.at[:, column], dst.at[head, which], sems.at[which, head])
            )
    run_copies(copies)


def pack_spatial(order, arrays):
    rows, width = arrays[0].shape
    heads = width // DEPTH - HT
    return pl.pallas_call(
        pack_spatial_kernel,
        out_shape=jax.ShapeDtypeStruct((heads, len(arrays), rows, DEPTH), BF),
        in_specs=[SMEM] + [ANY] * len(arrays),
        out_specs=ANY,
        scratch_shapes=[pltpu.SemaphoreType.DMA((len(arrays), heads))],
        compiler_params=PARAMS,
    )(order, *arrays)


def pack_temporal_kernel(order_ref, *refs):
    dst, sems = refs[-2:]
    pieces = refs[0].shape[0]
    copies = []
    for which, src in enumerate(refs[:-2]):
        for head in range(HT):
            copies.append(
                pltpu.make_async_copy(
                    src.at[:, :, columns_of(order_ref, head)],
                    dst.at[pl.ds(head * pieces, pieces), which],
                    sems.at[which, head],
                )
            )
    run_copies(copies)


def pack_temporal(order, arrays, items):
    rows, width = arrays[0].shape
    pieces = rows // items
    return pl.pallas_call(
        pack_temporal_kernel,
        out_shape=jax.ShapeDtypeStruct((HT * pieces, len(arrays), items, DEPTH), BF),
        in_specs=[SMEM] + [ANY] * len(arrays),
        out_specs=ANY,
        scratch_shapes=[pltpu.SemaphoreType.DMA((len(arrays), HT))],
        compiler_params=PARAMS,
        cost_estimate=estimate(10),
    )(order, *[array.reshape(pieces, items, width) for array in arrays])


def temporal_kernel(in_ref, out_ref):
    frames, _, items, depth = in_ref.shape
    total = frames * items
    step = 256
    factor = depth ** (-0.5) * math.log2(math.e)
    k = in_ref[:, 1].reshape(total, depth)
    v = in_ref[:, 2].reshape(total, depth)
    row_item = lax.broadcasted_iota(jnp.int32, (step, total), 0) % items
    col_item = lax.broadcasted_iota(jnp.int32, (step, total), 1) % items
    same = row_item == col_item
    per = step // items
    for at in range(frames // per):
        q = in_ref[at * per : (at + 1) * per, 0].reshape(step, depth)
        s = lax.dot_general(q, k, (((1,), (1,)), ((), ())), preferred_element_type=F32)
        s = jnp.where(same, s * factor, -jnp.inf)
        p = jnp.exp2(s - jnp.max(s, axis=1, keepdims=True))
        total_p = jnp.sum(p, axis=1, keepdims=True)
        o = jnp.dot(p.astype(BF), v, preferred_element_type=F32) / total_p
        out_ref[at * per : (at + 1) * per] = o.astype(BF).reshape(per, items, depth)


def temporal_attend(arrived):
    frames, _, items, depth = arrived.shape
    return pl.pallas_call(
        temporal_kernel,
        out_shape=jax.ShapeDtypeStruct((frames, items, depth), BF),
        in_specs=[VMEM],
        out_specs=VMEM,
        compiler_params=PARAMS,
        cost_estimate=estimate(50),
    )(arrived)


def row_norm(block):
    wide = block.astype(F32)
    ones = jnp.ones((block.shape[-1], LANES), BF)
    return jnp.max(jnp.dot((wide * wide).astype(BF), ones, preferred_element_type=F32))


def used_slot(frames, base, kb_ref, bc_ref, mine, slot):
    frame = base + mine
    target = lax.rem(base + slot + frames, frames)
    hit = False
    for n in range(NB):
        hit = hit | ((kb_ref[frame, n] == target) & (bc_ref[frame] > n))
    return hit


def score_factor():
    return DEPTH ** (-0.5) * math.log2(math.e)


def products(q, k):
    return lax.dot_general(q, k, (((1,), (1,)), ((), ())), preferred_element_type=F32)


def add_frames(acc, q, pairs):
    for k, v, hit in pairs:
        p = jnp.exp2(products(q, k) * score_factor()).astype(BF)
        weight = jnp.where(hit, 1.0, 0.0).astype(BF)
        wide = jnp.concatenate([v * weight, jnp.full(v.shape, weight)], axis=1)
        add = jnp.dot(p, wide, preferred_element_type=F32)
        acc = add if acc is None else acc + add
    return acc


def fold_frame(first, q, k, v, acc_ref, m_ref):
    wide = jnp.concatenate([v, jnp.ones_like(v)], axis=1)
    s = products(q, k) * score_factor()
    top = jnp.max(s, axis=1, keepdims=True)
    if first:
        p = jnp.exp2(s - top).astype(BF)
        acc_ref[...] = jnp.dot(p, wide, preferred_element_type=F32)
        m_ref[...] = jnp.broadcast_to(top, m_ref.shape)
    else:
        old = m_ref[...]
        new = jnp.maximum(old, top)
        p = jnp.exp2(s - new[:, :1]).astype(BF)
        alpha = jnp.exp2(old - new)
        both = jnp.concatenate([alpha, alpha], axis=1)
        acc_ref[...] = acc_ref[...] * both + jnp.dot(p, wide, preferred_element_type=F32)
        m_ref[...] = new


def small_scores(q_norm, k_norm):
    factor = score_factor() * 1.02
    return q_norm * k_norm * (factor * factor) <= 1e4


def own_kernel(frames, base_ref, kb_ref, bc_ref, in_ref, acc_ref, m_ref, stat_ref):
    pieces = in_ref.shape[0] // BLOCK
    size = pieces * in_ref.shape[2]
    base = base_ref[0]

    def part(which, at):
        return lambda: in_ref[at * pieces : (at + 1) * pieces, which].reshape(size, DEPTH)

    total = BLOCK * size
    q_norm = row_norm(in_ref[:, 0].reshape(total, DEPTH))
    k_norm = row_norm(in_ref[:, 1].reshape(total, DEPTH))
    fast = small_scores(q_norm, k_norm)
    stat_ref[0] = q_norm
    stat_ref[1] = jnp.where(fast, 1.0, 0.0)

    def used(mine, slot):
        return used_slot(frames, base, kb_ref, bc_ref, mine, slot)

    @pl.when(fast)
    def _():
        for mine in range(BLOCK):
            pairs = [
                (part(1, slot)(), part(2, slot)(), used(mine, slot))
                for slot in range(BLOCK)
                if abs(slot - mine) <= W
            ]
            acc_ref[mine] = add_frames(None, part(0, mine)(), pairs)
            m_ref[mine] = jnp.zeros((size, LANES), F32)

    @pl.when(jnp.logical_not(fast))
    def _():
        for mine in range(BLOCK):
            out = acc_ref.at[mine], m_ref.at[mine]
            fold_frame(True, part(0, mine)(), part(1, mine)(), part(2, mine)(), *out)
            for slot in range(BLOCK):
                if slot != mine and abs(slot - mine) <= W:

                    @pl.when(used(mine, slot))
                    def _():
                        fold_frame(False, part(0, mine)(), part(1, slot)(), part(2, slot)(), *out)


def near_kernel(
    frames, base_ref, kb_ref, bc_ref, stat_ref, in_ref, less_ref, more_ref, acc_in, m_in, o_ref, acc_ref, m_ref
):
    pieces = in_ref.shape[0] // BLOCK
    rows = in_ref.shape[2]
    size = pieces * rows
    base = base_ref[0]
    total = less_ref.shape[0] * rows
    k_norm = jnp.maximum(
        row_norm(less_ref[:, 0].reshape(total, DEPTH)), row_norm(more_ref[:, 0].reshape(total, DEPTH))
    )
    fast = small_scores(stat_ref[0], k_norm) & (stat_ref[1] > 0.5)

    def query(mine):
        return lambda: in_ref[mine * pieces : (mine + 1) * pieces, 0].reshape(size, DEPTH)

    def part(which, slot):
        ref, at = (less_ref, slot + W) if slot < 0 else (more_ref, slot - BLOCK)
        return lambda: ref[at * pieces : (at + 1) * pieces, which].reshape(size, DEPTH)

    def used(mine, slot):
        return used_slot(frames, base, kb_ref, bc_ref, mine, slot)

    def near(mine):
        return [slot for slot in range(mine - W, mine + W + 1) if slot < 0 or slot >= BLOCK]

    def finish(mine, acc):
        o = (acc[:, :DEPTH] / acc[:, DEPTH:]).astype(BF)
        o_ref[mine * pieces : (mine + 1) * pieces] = o.reshape(pieces, rows, DEPTH)

    @pl.when(fast)
    def _():
        for mine in range(BLOCK):
            pairs = [(part(0, slot)(), part(1, slot)(), used(mine, slot)) for slot in near(mine)]
            finish(mine, add_frames(acc_in[mine], query(mine)(), pairs))

    @pl.when(jnp.logical_not(fast))
    def _():
        for mine in range(BLOCK):
            acc_ref[...] = acc_in[mine]
            m_ref[...] = m_in[mine]
            for slot in near(mine):

                @pl.when(used(mine, slot))
                def _():
                    fold_frame(False, query(mine)(), part(0, slot)(), part(1, slot)(), acc_ref, m_ref)

            finish(mine, acc_ref[...])


def attend_own(base, kb, bc, arrived, frames):
    dests, _, rows, depth = arrived.shape
    size = dests // BLOCK * rows
    return pl.pallas_call(
        functools.partial(own_kernel, frames),
        out_shape=[
            jax.ShapeDtypeStruct((BLOCK, size, 2 * depth), F32),
            jax.ShapeDtypeStruct((BLOCK, size, LANES), F32),
            jax.ShapeDtypeStruct((2,), F32),
        ],
        in_specs=[SMEM] * 3 + [VMEM],
        out_specs=[VMEM, VMEM, SMEM],
        compiler_params=PARAMS,
        cost_estimate=estimate(10),
    )(base, kb, bc, arrived)


def attend_near(base, kb, bc, stat, arrived, less, more, acc, top, frames):
    dests, _, rows, depth = arrived.shape
    size = dests // BLOCK * rows
    return pl.pallas_call(
        functools.partial(near_kernel, frames),
        out_shape=jax.ShapeDtypeStruct((dests, rows, depth), BF),
        in_specs=[SMEM] * 4 + [VMEM] * 5,
        out_specs=VMEM,
        scratch_shapes=[pltpu.VMEM((size, 2 * depth), F32), pltpu.VMEM((size, LANES), F32)],
        compiler_params=PARAMS,
    )(base, kb, bc, stat, arrived, less, more, acc, top)


def assemble_kernel(order_ref, t_ref, s_ref, out_ref):
    rows = out_ref.shape[0]
    pieces = t_ref.shape[0] // HT
    for head in range(HT):
        block = t_ref[head * pieces : (head + 1) * pieces].reshape(rows, DEPTH)
        out_ref[:, columns_of(order_ref, head)] = block
    for head in range(s_ref.shape[0]):
        out_ref[:, columns_of(order_ref, HT + head)] = s_ref[head]


def assemble(order, temporal, spatial, rows, width):
    return pl.pallas_call(
        assemble_kernel,
        out_shape=jax.ShapeDtypeStruct((rows, width), BF),
        in_specs=[SMEM, VMEM, VMEM],
        out_specs=VMEM,
        compiler_params=PARAMS,
    )(order, temporal, spatial)


def exchange(array, axes):
    return lax.all_to_all(array, axes, 0, 0, tiled=True)


def from_block(array, by):
    count = lax.axis_size("grp") * lax.axis_size("yh")
    return lax.ppermute(array, ("grp", "yh"), [((i + by) % count, i) for i in range(count)])


def local(queries, keys, values, head_order, key_blocks, block_count):
    rows, width = queries.shape
    blocks = lax.axis_size("grp") * lax.axis_size("yh")
    frames = blocks * BLOCK
    items = HT * rows // frames
    base = (lax.axis_index("grp") * lax.axis_size("yh") + lax.axis_index("yh")) * BLOCK
    base = base.astype(jnp.int32).reshape(1)

    block_axes = ("yl", "zl", "x")
    loop_axes = ("grp", "yh", "yl", "zl")
    st = pack_temporal(head_order, (queries, keys, values), items)
    qkv = exchange(pack_spatial(head_order, (queries, keys, values)), block_axes)
    pieces = qkv.shape[0] // BLOCK
    less = from_block(qkv[(BLOCK - W) * pieces :, 1:], -1)
    more = from_block(qkv[: W * pieces, 1:], 1)
    qkv, st = lax.optimization_barrier((qkv, st))
    at = exchange(st, loop_axes)
    acc, top, stat = attend_own(base, key_blocks, block_count, qkv, frames)
    to, stat = lax.optimization_barrier((temporal_attend(at), stat))
    tr = exchange(to, loop_axes)
    so = attend_near(base, key_blocks, block_count, stat, qkv, less, more, acc, top, frames)
    sr = exchange(so, block_axes)
    return assemble(head_order, tr, sr, rows, width)


def solution(mesh):
    grp, seq = mesh.shape["grp"], mesh.shape["seq"]
    fine = Mesh(mesh.devices.reshape(grp, seq // 16, 2, 2, 4), ("grp", "yh", "yl", "zl", "x"))
    tokens = P(("grp", "yh", "yl", "zl", "x"), None)
    return jax.shard_map(
        local,
        mesh=fine,
        in_specs=(tokens, tokens, tokens, P(), P(), P()),
        out_specs=tokens,
        check_vma=False,
    )
```

```python
import functools
import math

import jax
import jax.numpy as jnp
from jax import lax
from jax.experimental import pallas as pl
from jax.experimental.pallas import tpu as pltpu
from jax.sharding import Mesh
from jax.sharding import PartitionSpec as P

HT = 8
W = 3
NB = 6
BLOCK = 4
DEPTH = 128
LANES = 128
BF = jnp.bfloat16
F32 = jnp.float32
VMEM = pl.BlockSpec(memory_space=pltpu.VMEM)
SMEM = pl.BlockSpec(memory_space=pltpu.SMEM)
ANY = pl.BlockSpec(memory_space=pl.ANY)
PARAMS = pltpu.CompilerParams(vmem_limit_bytes=40 * 1024 * 1024)
PACK_PARAMS = pltpu.CompilerParams(vmem_limit_bytes=58 * 1024 * 1024)


def estimate(gigaflops):
    return pl.CostEstimate(flops=gigaflops * 10**9, bytes_accessed=1 << 20, transcendentals=1 << 20)


def columns_of(order_ref, slot):
    return pl.ds(pl.multiple_of(order_ref[slot] * DEPTH, DEPTH), DEPTH)


def run_copies(copies):
    for copy in copies:
        copy.start()
    for copy in copies:
        copy.wait()


def pack_spatial_kernel(order_ref, *refs):
    dst, sems = refs[-2:]
    copies = []
    for which, src in enumerate(refs[:-2]):
        for head in range(dst.shape[0]):
            column = columns_of(order_ref, HT + head)
            copies.append(
                pltpu.make_async_copy(src.at[:, column], dst.at[head, which], sems.at[which, head])
            )
    run_copies(copies)


def pack_spatial(order, arrays):
    rows, width = arrays[0].shape
    heads = width // DEPTH - HT
    return pl.pallas_call(
        pack_spatial_kernel,
        out_shape=jax.ShapeDtypeStruct((heads, len(arrays), rows, DEPTH), BF),
        in_specs=[SMEM] + [ANY] * len(arrays),
        out_specs=ANY,
        scratch_shapes=[pltpu.SemaphoreType.DMA((len(arrays), heads))],
        compiler_params=PACK_PARAMS,
    )(order, *arrays)


def pack_temporal_kernel(order_ref, *refs):
    dst, sems = refs[-2:]
    pieces = refs[0].shape[0]
    copies = []
    for which, src in enumerate(refs[:-2]):
        for head in range(HT):
            copies.append(
                pltpu.make_async_copy(
                    src.at[:, :, columns_of(order_ref, head)],
                    dst.at[pl.ds(head * pieces, pieces), which],
                    sems.at[which, head],
                )
            )
    run_copies(copies)


def pack_temporal(order, arrays, items):
    rows, width = arrays[0].shape
    pieces = rows // items
    return pl.pallas_call(
        pack_temporal_kernel,
        out_shape=jax.ShapeDtypeStruct((HT * pieces, len(arrays), items, DEPTH), BF),
        in_specs=[SMEM] + [ANY] * len(arrays),
        out_specs=ANY,
        scratch_shapes=[pltpu.SemaphoreType.DMA((len(arrays), HT))],
        compiler_params=PACK_PARAMS,
        cost_estimate=estimate(10),
    )(order, *[array.reshape(pieces, items, width) for array in arrays])


def temporal_kernel(in_ref, out_ref):
    frames, _, items, depth = in_ref.shape
    total = frames * items
    step = 256
    factor = depth ** (-0.5) * math.log2(math.e)
    k = in_ref[:, 1].reshape(total, depth)
    v = in_ref[:, 2].reshape(total, depth)
    row_item = lax.broadcasted_iota(jnp.int32, (step, total), 0) % items
    col_item = lax.broadcasted_iota(jnp.int32, (step, total), 1) % items
    same = row_item == col_item
    per = step // items
    for at in range(frames // per):
        q = in_ref[at * per : (at + 1) * per, 0].reshape(step, depth)
        s = lax.dot_general(q, k, (((1,), (1,)), ((), ())), preferred_element_type=F32)
        s = jnp.where(same, s * factor, -jnp.inf)
        p = jnp.exp2(s - jnp.max(s, axis=1, keepdims=True))
        total_p = jnp.sum(p, axis=1, keepdims=True)
        o = jnp.dot(p.astype(BF), v, preferred_element_type=F32) / total_p
        out_ref[at * per : (at + 1) * per] = o.astype(BF).reshape(per, items, depth)


def temporal_attend(arrived):
    frames, _, items, depth = arrived.shape
    return pl.pallas_call(
        temporal_kernel,
        out_shape=jax.ShapeDtypeStruct((frames, items, depth), BF),
        in_specs=[VMEM],
        out_specs=VMEM,
        compiler_params=PARAMS,
        cost_estimate=estimate(50),
    )(arrived)


def row_norm(blocks):
    ones = jnp.ones((DEPTH, LANES), BF)
    best = None
    for block in blocks:
        norms = jnp.dot(block * block, ones, preferred_element_type=F32)
        most = jnp.max(norms.reshape(-1, 8, LANES), axis=0)
        best = most if best is None else jnp.maximum(best, most)
    return jnp.max(best)


def used_slot(frames, base, kb_ref, bc_ref, mine, slot):
    frame = base + mine
    target = lax.rem(base + slot + frames, frames)
    hit = False
    for n in range(NB):
        hit = hit | ((kb_ref[frame, n] == target) & (bc_ref[frame] > n))
    return hit


def score_factor():
    return DEPTH ** (-0.5) * math.log2(math.e)


def products(q, k):
    return lax.dot_general(q, k, (((1,), (1,)), ((), ())), preferred_element_type=F32)


def add_frames(acc, q, pairs):
    for k, v, hit in pairs:
        p = jnp.exp2(products(q, k) * score_factor()).astype(BF)
        weight = jnp.where(hit, 1.0, 0.0).astype(BF)
        wide = jnp.concatenate([v * weight, jnp.full(v.shape, weight)], axis=1)
        add = jnp.dot(p, wide, preferred_element_type=F32)
        acc = add if acc is None else acc + add
    return acc


def fold_frame(q, k, v, acc_ref, m_ref):
    wide = jnp.concatenate([v, jnp.ones_like(v)], axis=1)
    s = products(q, k) * score_factor()
    old = m_ref[...]
    new = jnp.maximum(old, jnp.max(s, axis=1, keepdims=True))
    p = jnp.exp2(s - new[:, :1]).astype(BF)
    alpha = jnp.exp2(old - new)
    both = jnp.concatenate([alpha, alpha], axis=1)
    acc_ref[...] = acc_ref[...] * both + jnp.dot(p, wide, preferred_element_type=F32)
    m_ref[...] = new


def small_scores(q_norm, k_norm):
    factor = score_factor() * 1.02
    return q_norm * k_norm * (factor * factor) <= 1e4


def frame_at(ref, which, at, pieces):
    block = ref[pl.ds(at * pieces, pieces), which]
    return block.reshape(pieces * block.shape[1], DEPTH)


def own_kernel(frames, base_ref, kb_ref, bc_ref, in_ref, acc_ref, m_ref, stat_ref):
    pieces = in_ref.shape[0] // BLOCK
    size = pieces * in_ref.shape[2]
    base = base_ref[0]
    part = functools.partial(frame_at, in_ref, pieces=pieces)
    q_norm = row_norm([part(0, at) for at in range(BLOCK)])
    k_norm = row_norm([part(1, at) for at in range(BLOCK)])
    fast = small_scores(q_norm, k_norm)
    stat_ref[0] = q_norm
    stat_ref[1] = jnp.where(fast, 1.0, 0.0)

    def used(mine, slot):
        return used_slot(frames, base, kb_ref, bc_ref, mine, slot)

    @pl.when(fast)
    def _():
        def frame(mine, carry):
            pairs = [(part(1, slot), part(2, slot), used(mine, slot)) for slot in range(BLOCK)]
            acc_ref[mine] = add_frames(None, part(0, mine), pairs)
            m_ref[mine] = jnp.zeros((size, LANES), F32)
            return carry

        lax.fori_loop(0, BLOCK, frame, 0)

    @pl.when(jnp.logical_not(fast))
    def _():
        def pair(at, carry):
            mine, slot = at // BLOCK, lax.rem(at, BLOCK)

            @pl.when(slot == 0)
            def _():
                acc_ref[mine] = jnp.zeros((size, 2 * DEPTH), F32)
                m_ref[mine] = jnp.full((size, LANES), -jnp.inf, F32)

            @pl.when(used(mine, slot))
            def _():
                fold_frame(part(0, mine), part(1, slot), part(2, slot), acc_ref.at[mine], m_ref.at[mine])

            return carry

        lax.fori_loop(0, BLOCK * BLOCK, pair, 0)


def near_kernel(
    frames, base_ref, kb_ref, bc_ref, stat_ref, in_ref, less_ref, more_ref, acc_in, m_in, o_ref,
    acc_ref, m_ref, near_ref, sems
):
    pieces = in_ref.shape[0] // BLOCK
    rows = in_ref.shape[2]
    base = base_ref[0]
    run_copies(
        [
            pltpu.make_async_copy(less_ref, near_ref.at[pl.ds(0, W * pieces)], sems.at[0]),
            pltpu.make_async_copy(more_ref, near_ref.at[pl.ds(W * pieces, W * pieces)], sems.at[1]),
        ]
    )
    part = functools.partial(frame_at, near_ref, pieces=pieces)
    k_norm = row_norm([part(0, at) for at in range(2 * W)])
    fast = small_scores(stat_ref[0], k_norm) & (stat_ref[1] > 0.5)

    def query(mine):
        return frame_at(in_ref, 0, mine, pieces)

    def used(mine, at):
        slot = jnp.where(at < W, at - W, at - W + BLOCK)
        return used_slot(frames, base, kb_ref, bc_ref, mine, slot)

    def finish(mine, acc):
        o = (acc[:, :DEPTH] / acc[:, DEPTH:]).astype(BF)
        o_ref[pl.ds(mine * pieces, pieces)] = o.reshape(pieces, rows, DEPTH)

    @pl.when(fast)
    def _():
        def frame(mine, carry):
            pairs = [
                (part(0, mine + j), part(1, mine + j), used(mine, mine + j)) for j in range(W)
            ]
            finish(mine, add_frames(acc_in[mine], query(mine), pairs))
            return carry

        lax.fori_loop(0, BLOCK, frame, 0)

    @pl.when(jnp.logical_not(fast))
    def _():
        def frame(mine, carry):
            acc_ref[...] = acc_in[mine]
            m_ref[...] = m_in[mine]

            def pair(j, inner):
                @pl.when(used(mine, mine + j))
                def _():
                    fold_frame(query(mine), part(0, mine + j), part(1, mine + j), acc_ref, m_ref)

                return inner

            lax.fori_loop(0, W, pair, 0)
            finish(mine, acc_ref[...])
            return carry

        lax.fori_loop(0, BLOCK, frame, 0)


def attend_own(base, kb, bc, arrived, frames):
    dests, _, rows, depth = arrived.shape
    size = dests // BLOCK * rows
    return pl.pallas_call(
        functools.partial(own_kernel, frames),
        out_shape=[
            jax.ShapeDtypeStruct((BLOCK, size, 2 * depth), F32),
            jax.ShapeDtypeStruct((BLOCK, size, LANES), F32),
            jax.ShapeDtypeStruct((2,), F32),
        ],
        in_specs=[SMEM] * 3 + [VMEM],
        out_specs=[VMEM, VMEM, SMEM],
        compiler_params=PARAMS,
        cost_estimate=estimate(10),
    )(base, kb, bc, arrived)


def attend_near(base, kb, bc, stat, arrived, less, more, acc, top, frames):
    dests, _, rows, depth = arrived.shape
    size = dests // BLOCK * rows
    return pl.pallas_call(
        functools.partial(near_kernel, frames),
        out_shape=jax.ShapeDtypeStruct((dests, rows, depth), BF),
        in_specs=[SMEM] * 4 + [VMEM, ANY, ANY, VMEM, VMEM],
        out_specs=VMEM,
        scratch_shapes=[
            pltpu.VMEM((size, 2 * depth), F32),
            pltpu.VMEM((size, LANES), F32),
            pltpu.VMEM((2 * less.shape[0], *less.shape[1:]), BF),
            pltpu.SemaphoreType.DMA((2,)),
        ],
        compiler_params=PARAMS,
    )(base, kb, bc, stat, arrived, less, more, acc, top)


def assemble_kernel(order_ref, t_ref, s_ref, out_ref):
    rows = out_ref.shape[0]
    pieces = t_ref.shape[0] // HT
    for head in range(HT):
        block = t_ref[head * pieces : (head + 1) * pieces].reshape(rows, DEPTH)
        out_ref[:, columns_of(order_ref, head)] = block
    for head in range(s_ref.shape[0]):
        out_ref[:, columns_of(order_ref, HT + head)] = s_ref[head]


def assemble(order, temporal, spatial, rows, width):
    return pl.pallas_call(
        assemble_kernel,
        out_shape=jax.ShapeDtypeStruct((rows, width), BF),
        in_specs=[SMEM, VMEM, VMEM],
        out_specs=VMEM,
        compiler_params=PARAMS,
    )(order, temporal, spatial)


def exchange(array, axes):
    return lax.all_to_all(array, axes, 0, 0, tiled=True)


def from_block(array, by):
    count = lax.axis_size("grp") * lax.axis_size("yh")
    return lax.ppermute(array, ("grp", "yh"), [((i + by) % count, i) for i in range(count)])


def local(queries, keys, values, head_order, key_blocks, block_count):
    rows, width = queries.shape
    blocks = lax.axis_size("grp") * lax.axis_size("yh")
    frames = blocks * BLOCK
    items = HT * rows // frames
    base = (lax.axis_index("grp") * lax.axis_size("yh") + lax.axis_index("yh")) * BLOCK
    base = base.astype(jnp.int32).reshape(1)

    block_axes = ("yl", "zl", "x")
    loop_axes = ("grp", "yh", "yl", "zl")
    st = pack_temporal(head_order, (queries, keys, values), items)
    qkv = exchange(pack_spatial(head_order, (queries, keys, values)), block_axes)
    pieces = qkv.shape[0] // BLOCK
    less = from_block(qkv[(BLOCK - W) * pieces :, 1:], -1)
    more = from_block(qkv[: W * pieces, 1:], 1)
    qkv, st = lax.optimization_barrier((qkv, st))
    at = exchange(st, loop_axes)
    acc, top, stat = attend_own(base, key_blocks, block_count, qkv, frames)
    to, stat = lax.optimization_barrier((temporal_attend(at), stat))
    tr = exchange(to, loop_axes)
    so = attend_near(base, key_blocks, block_count, stat, qkv, less, more, acc, top, frames)
    sr = exchange(so, block_axes)
    return assemble(head_order, tr, sr, rows, width)


def solution(mesh):
    grp, seq = mesh.shape["grp"], mesh.shape["seq"]
    fine = Mesh(mesh.devices.reshape(grp, seq // 16, 2, 2, 4), ("grp", "yh", "yl", "zl", "x"))
    tokens = P(("grp", "yh", "yl", "zl", "x"), None)
    return jax.shard_map(
        local,
        mesh=fine,
        in_specs=(tokens, tokens, tokens, P(), P(), P()),
        out_specs=tokens,
        check_vma=False,
    )
```

```python
import functools
import math

import jax
import jax.numpy as jnp
from jax import lax
from jax.experimental import pallas as pl
from jax.experimental.pallas import tpu as pltpu
from jax.sharding import Mesh
from jax.sharding import PartitionSpec as P

HT = 8
W = 3
NB = 6
BLOCK = 4
DEPTH = 128
LANES = 128
BF = jnp.bfloat16
F32 = jnp.float32
VMEM = pl.BlockSpec(memory_space=pltpu.VMEM)
SMEM = pl.BlockSpec(memory_space=pltpu.SMEM)
ANY = pl.BlockSpec(memory_space=pl.ANY)
PARAMS = pltpu.CompilerParams(vmem_limit_bytes=40 * 1024 * 1024)
PACK_PARAMS = pltpu.CompilerParams(vmem_limit_bytes=58 * 1024 * 1024)


def estimate(gigaflops):
    return pl.CostEstimate(flops=gigaflops * 10**9, bytes_accessed=1 << 20, transcendentals=1 << 20)


def columns_of(order_ref, slot):
    return pl.ds(pl.multiple_of(order_ref[slot] * DEPTH, DEPTH), DEPTH)


def run_copies(copies):
    for copy in copies:
        copy.start()
    for copy in copies:
        copy.wait()


def pack_spatial_kernel(order_ref, *refs):
    dst, sems = refs[-2:]
    copies = []
    for which, src in enumerate(refs[:-2]):
        for head in range(dst.shape[0]):
            column = columns_of(order_ref, HT + head)
            copies.append(
                pltpu.make_async_copy(src.at[:, column], dst.at[head, which], sems.at[which, head])
            )
    run_copies(copies)


def pack_spatial(order, arrays):
    rows, width = arrays[0].shape
    heads = width // DEPTH - HT
    return pl.pallas_call(
        pack_spatial_kernel,
        out_shape=jax.ShapeDtypeStruct((heads, len(arrays), rows, DEPTH), BF),
        in_specs=[SMEM] + [ANY] * len(arrays),
        out_specs=VMEM,
        scratch_shapes=[pltpu.SemaphoreType.DMA((len(arrays), heads))],
        compiler_params=PACK_PARAMS,
    )(order, *arrays)


def pack_temporal_kernel(order_ref, y_ref, q_ref, k_ref, v_ref, *outs):
    _, side, _, items, _ = outs[0].shape
    for away, out in enumerate(outs):
        to = lax.rem(y_ref[0] + away, len(outs))
        here = pl.ds(pl.multiple_of(to * (side * items), side * items), side * items)
        for which, src in enumerate((q_ref, k_ref, v_ref)):
            for head in range(HT):
                block = src[here, columns_of(order_ref, head)]
                out[head, :, which] = block.reshape(side, items, DEPTH)


def pack_temporal(order, y, arrays, items, steps):
    side = arrays[0].shape[0] // items // steps
    out = jax.ShapeDtypeStruct((HT, side, len(arrays), items, DEPTH), BF)
    return pl.pallas_call(
        pack_temporal_kernel,
        out_shape=[out] * steps,
        in_specs=[SMEM, SMEM] + [VMEM] * len(arrays),
        out_specs=[VMEM] * steps,
        compiler_params=PARAMS,
    )(order, y, *arrays)


def regroup_kernel(*refs):
    dst = refs[-1]
    for away, src in enumerate(refs[:-1]):
        dst[:, away] = src[...].reshape(dst.shape[0], *dst.shape[2:])


def regroup(parts):
    heads, side, *rest = parts[0].shape
    return pl.pallas_call(
        regroup_kernel,
        out_shape=jax.ShapeDtypeStruct((heads * side, len(parts), *rest), BF),
        in_specs=[VMEM] * len(parts),
        out_specs=VMEM,
        compiler_params=PARAMS,
    )(*parts)


def temporal_kernel(y_ref, in_ref, out_ref):
    planes, steps, _, items, depth = in_ref.shape
    total = planes * steps * items
    per = 4
    step = per * steps * items
    side = 2
    k = in_ref[:, :, 1].reshape(total, depth)
    v = in_ref[:, :, 2].reshape(total, depth)
    row_item = lax.broadcasted_iota(jnp.int32, (step, total), 0) % items
    col_item = lax.broadcasted_iota(jnp.int32, (step, total), 1) % items
    same = row_item == col_item
    for at in range(planes // per):
        q = in_ref[at * per : (at + 1) * per, :, 0].reshape(step, depth)
        s = jnp.where(same, products(q, k) * score_factor(), -jnp.inf)
        p = jnp.exp2(s - jnp.max(s, axis=1, keepdims=True))
        total_p = jnp.sum(p, axis=1, keepdims=True)
        o = jnp.dot(p.astype(BF), v, preferred_element_type=F32) / total_p
        o = o.astype(BF).reshape(per, steps, items, depth)
        for plane in range(per):
            grp, low = divmod(at * per + plane, side)
            for away in range(steps):
                y = lax.rem(y_ref[0] + steps - away, steps)
                out_ref[(grp * steps + y) * side + low] = o[plane, away]


def temporal_attend(y, arrived):
    planes, steps, _, items, depth = arrived.shape
    return pl.pallas_call(
        temporal_kernel,
        out_shape=jax.ShapeDtypeStruct((planes * steps, items, depth), BF),
        in_specs=[SMEM, VMEM],
        out_specs=VMEM,
        compiler_params=PARAMS,
        cost_estimate=estimate(50),
    )(y, arrived)


def row_norm(blocks):
    ones = jnp.ones((DEPTH, LANES), BF)
    best = None
    for block in blocks:
        norms = jnp.dot(block * block, ones, preferred_element_type=F32)
        most = jnp.max(norms.reshape(-1, 8, LANES), axis=0)
        best = most if best is None else jnp.maximum(best, most)
    return jnp.max(best)


def used_slot(frames, base, kb_ref, bc_ref, mine, slot):
    frame = base + mine
    target = lax.rem(base + slot + frames, frames)
    hit = False
    for n in range(NB):
        hit = hit | ((kb_ref[frame, n] == target) & (bc_ref[frame] > n))
    return hit


def score_factor():
    return DEPTH ** (-0.5) * math.log2(math.e)


def products(q, k):
    return lax.dot_general(q, k, (((1,), (1,)), ((), ())), preferred_element_type=F32)


def add_frames(acc, q, pairs):
    for k, v, hit in pairs:
        p = jnp.exp2(products(q, k) * score_factor()).astype(BF)
        weight = jnp.where(hit, 1.0, 0.0).astype(BF)
        wide = jnp.concatenate([v * weight, jnp.full(v.shape, weight)], axis=1)
        add = jnp.dot(p, wide, preferred_element_type=F32)
        acc = add if acc is None else acc + add
    return acc


def fold_frame(q, k, v, acc_ref, m_ref):
    wide = jnp.concatenate([v, jnp.ones_like(v)], axis=1)
    s = products(q, k) * score_factor()
    old = m_ref[...]
    new = jnp.maximum(old, jnp.max(s, axis=1, keepdims=True))
    p = jnp.exp2(s - new[:, :1]).astype(BF)
    alpha = jnp.exp2(old - new)
    both = jnp.concatenate([alpha, alpha], axis=1)
    acc_ref[...] = acc_ref[...] * both + jnp.dot(p, wide, preferred_element_type=F32)
    m_ref[...] = new


def small_scores(q_norm, k_norm):
    factor = score_factor() * 1.02
    return q_norm * k_norm * (factor * factor) <= 1e4


def frame_at(ref, which, at, pieces):
    block = ref[pl.ds(at * pieces, pieces), which]
    return block.reshape(pieces * block.shape[1], DEPTH)


def own_kernel(frames, base_ref, kb_ref, bc_ref, in_ref, acc_ref, m_ref, stat_ref):
    pieces = in_ref.shape[0] // BLOCK
    size = pieces * in_ref.shape[2]
    base = base_ref[0]
    part = functools.partial(frame_at, in_ref, pieces=pieces)
    q_norm = row_norm([part(0, at) for at in range(BLOCK)])
    k_norm = row_norm([part(1, at) for at in range(BLOCK)])
    fast = small_scores(q_norm, k_norm)
    stat_ref[0] = q_norm
    stat_ref[1] = jnp.where(fast, 1.0, 0.0)

    def used(mine, slot):
        return used_slot(frames, base, kb_ref, bc_ref, mine, slot)

    @pl.when(fast)
    def _():
        def frame(mine, carry):
            pairs = [(part(1, slot), part(2, slot), used(mine, slot)) for slot in range(BLOCK)]
            acc_ref[mine] = add_frames(None, part(0, mine), pairs)
            m_ref[mine] = jnp.zeros((size, LANES), F32)
            return carry

        lax.fori_loop(0, BLOCK, frame, 0)

    @pl.when(jnp.logical_not(fast))
    def _():
        def pair(at, carry):
            mine, slot = at // BLOCK, lax.rem(at, BLOCK)

            @pl.when(slot == 0)
            def _():
                acc_ref[mine] = jnp.zeros((size, 2 * DEPTH), F32)
                m_ref[mine] = jnp.full((size, LANES), -jnp.inf, F32)

            @pl.when(used(mine, slot))
            def _():
                fold_frame(part(0, mine), part(1, slot), part(2, slot), acc_ref.at[mine], m_ref.at[mine])

            return carry

        lax.fori_loop(0, BLOCK * BLOCK, pair, 0)


def near_kernel(
    frames, base_ref, kb_ref, bc_ref, stat_ref, in_ref, less_ref, more_ref, acc_in, m_in, o_ref,
    acc_ref, m_ref, near_ref, sems
):
    pieces = in_ref.shape[0] // BLOCK
    rows = in_ref.shape[2]
    base = base_ref[0]
    run_copies(
        [
            pltpu.make_async_copy(less_ref, near_ref.at[pl.ds(0, W * pieces)], sems.at[0]),
            pltpu.make_async_copy(more_ref, near_ref.at[pl.ds(W * pieces, W * pieces)], sems.at[1]),
        ]
    )
    part = functools.partial(frame_at, near_ref, pieces=pieces)
    k_norm = row_norm([part(0, at) for at in range(2 * W)])
    fast = small_scores(stat_ref[0], k_norm) & (stat_ref[1] > 0.5)

    def query(mine):
        return frame_at(in_ref, 0, mine, pieces)

    def used(mine, at):
        slot = jnp.where(at < W, at - W, at - W + BLOCK)
        return used_slot(frames, base, kb_ref, bc_ref, mine, slot)

    def finish(mine, acc):
        o = (acc[:, :DEPTH] / acc[:, DEPTH:]).astype(BF)
        o_ref[pl.ds(mine * pieces, pieces)] = o.reshape(pieces, rows, DEPTH)

    @pl.when(fast)
    def _():
        def frame(mine, carry):
            pairs = [
                (part(0, mine + j), part(1, mine + j), used(mine, mine + j)) for j in range(W)
            ]
            finish(mine, add_frames(acc_in[mine], query(mine), pairs))
            return carry

        lax.fori_loop(0, BLOCK, frame, 0)

    @pl.when(jnp.logical_not(fast))
    def _():
        def frame(mine, carry):
            acc_ref[...] = acc_in[mine]
            m_ref[...] = m_in[mine]

            def pair(j, inner):
                @pl.when(used(mine, mine + j))
                def _():
                    fold_frame(query(mine), part(0, mine + j), part(1, mine + j), acc_ref, m_ref)

                return inner

            lax.fori_loop(0, W, pair, 0)
            finish(mine, acc_ref[...])
            return carry

        lax.fori_loop(0, BLOCK, frame, 0)


def attend_own(base, kb, bc, arrived, frames):
    dests, _, rows, depth = arrived.shape
    size = dests // BLOCK * rows
    return pl.pallas_call(
        functools.partial(own_kernel, frames),
        out_shape=[
            jax.ShapeDtypeStruct((BLOCK, size, 2 * depth), F32),
            jax.ShapeDtypeStruct((BLOCK, size, LANES), F32),
            jax.ShapeDtypeStruct((2,), F32),
        ],
        in_specs=[SMEM] * 3 + [VMEM],
        out_specs=[VMEM, VMEM, SMEM],
        compiler_params=PARAMS,
        cost_estimate=estimate(10),
    )(base, kb, bc, arrived)


def attend_near(base, kb, bc, stat, arrived, less, more, acc, top, frames):
    dests, _, rows, depth = arrived.shape
    size = dests // BLOCK * rows
    return pl.pallas_call(
        functools.partial(near_kernel, frames),
        out_shape=jax.ShapeDtypeStruct((dests, rows, depth), BF),
        in_specs=[SMEM] * 4 + [VMEM, ANY, ANY, VMEM, VMEM],
        out_specs=VMEM,
        scratch_shapes=[
            pltpu.VMEM((size, 2 * depth), F32),
            pltpu.VMEM((size, LANES), F32),
            pltpu.VMEM((2 * less.shape[0], *less.shape[1:]), BF),
            pltpu.SemaphoreType.DMA((2,)),
        ],
        compiler_params=PARAMS,
    )(base, kb, bc, stat, arrived, less, more, acc, top)


def assemble_kernel(order_ref, t_ref, s_ref, out_ref):
    rows = out_ref.shape[0]
    pieces = t_ref.shape[0] // HT
    for head in range(HT):
        block = t_ref[head * pieces : (head + 1) * pieces].reshape(rows, DEPTH)
        out_ref[:, columns_of(order_ref, head)] = block
    for head in range(s_ref.shape[0]):
        out_ref[:, columns_of(order_ref, HT + head)] = s_ref[head]


def assemble(order, temporal, spatial, rows, width):
    return pl.pallas_call(
        assemble_kernel,
        out_shape=jax.ShapeDtypeStruct((rows, width), BF),
        in_specs=[SMEM, VMEM, VMEM],
        out_specs=VMEM,
        compiler_params=PARAMS,
    )(order, temporal, spatial)


def exchange(array, axes):
    return lax.all_to_all(array, axes, 0, 0, tiled=True)


def from_block(array, by):
    count = lax.axis_size("grp") * lax.axis_size("yh")
    return lax.ppermute(array, ("grp", "yh"), [((i + by) % count, i) for i in range(count)])


def along_y(array, by):
    count = lax.axis_size("yh") * lax.axis_size("yl")
    if by == 0:
        return array
    return lax.ppermute(array, ("yh", "yl"), [(i, (i + by) % count) for i in range(count)])


def local(queries, keys, values, head_order, key_blocks, block_count):
    rows, width = queries.shape
    blocks = lax.axis_size("grp") * lax.axis_size("yh")
    frames = blocks * BLOCK
    items = HT * rows // frames
    base = (lax.axis_index("grp") * lax.axis_size("yh") + lax.axis_index("yh")) * BLOCK
    base = base.astype(jnp.int32).reshape(1)

    block_axes = ("yl", "zl", "x")
    loop_axes = ("grp", "yh", "yl", "zl")
    steps = lax.axis_size("yh") * lax.axis_size("yl")
    y = (lax.axis_index("yh") * lax.axis_size("yl") + lax.axis_index("yl")).astype(jnp.int32).reshape(1)
    st = pack_temporal(head_order, y, (queries, keys, values), items, steps)
    st = [along_y(part, away) for away, part in enumerate(st)]
    qkv = exchange(pack_spatial(head_order, (queries, keys, values)), block_axes)
    pieces = qkv.shape[0] // BLOCK
    less = from_block(qkv[(BLOCK - W) * pieces :, 1:], -1)
    more = from_block(qkv[: W * pieces, 1:], 1)
    qkv, st = lax.optimization_barrier((qkv, st))
    at = exchange(regroup(st), ("grp", "zl"))
    acc, top, stat = attend_own(base, key_blocks, block_count, qkv, frames)
    to, stat = lax.optimization_barrier((temporal_attend(y, at), stat))
    tr = exchange(to, loop_axes)
    so = attend_near(base, key_blocks, block_count, stat, qkv, less, more, acc, top, frames)
    sr = exchange(so, block_axes)
    return assemble(head_order, tr, sr, rows, width)


def solution(mesh):
    grp, seq = mesh.shape["grp"], mesh.shape["seq"]
    fine = Mesh(mesh.devices.reshape(grp, seq // 16, 2, 2, 4), ("grp", "yh", "yl", "zl", "x"))
    tokens = P(("grp", "yh", "yl", "zl", "x"), None)
    return jax.shard_map(
        local,
        mesh=fine,
        in_specs=(tokens, tokens, tokens, P(), P(), P()),
        out_specs=tokens,
        check_vma=False,
    )
```

```python
import functools
import math

import jax
import jax.numpy as jnp
from jax import lax
from jax.experimental import pallas as pl
from jax.experimental.pallas import tpu as pltpu
from jax.sharding import Mesh
from jax.sharding import PartitionSpec as P

HT = 8
W = 3
NB = 6
BLOCK = 4
DEPTH = 128
LANES = 128
BF = jnp.bfloat16
F32 = jnp.float32
VMEM = pl.BlockSpec(memory_space=pltpu.VMEM)
SMEM = pl.BlockSpec(memory_space=pltpu.SMEM)
ANY = pl.BlockSpec(memory_space=pl.ANY)
PARAMS = pltpu.CompilerParams(vmem_limit_bytes=40 * 1024 * 1024)
PACK_PARAMS = pltpu.CompilerParams(vmem_limit_bytes=58 * 1024 * 1024)


def estimate(gigaflops):
    return pl.CostEstimate(flops=gigaflops * 10**9, bytes_accessed=1 << 20, transcendentals=1 << 20)


def columns_of(order_ref, slot):
    return pl.ds(pl.multiple_of(order_ref[slot] * DEPTH, DEPTH), DEPTH)


def run_copies(copies):
    for copy in copies:
        copy.start()
    for copy in copies:
        copy.wait()


def pack_spatial_kernel(order_ref, *refs):
    dst, sems = refs[-2:]
    copies = []
    for which, src in enumerate(refs[:-2]):
        for head in range(dst.shape[0]):
            column = columns_of(order_ref, HT + head)
            copies.append(
                pltpu.make_async_copy(src.at[:, column], dst.at[head, which], sems.at[which, head])
            )
    run_copies(copies)


def pack_spatial(order, arrays):
    rows, width = arrays[0].shape
    heads = width // DEPTH - HT
    return pl.pallas_call(
        pack_spatial_kernel,
        out_shape=jax.ShapeDtypeStruct((heads, len(arrays), rows, DEPTH), BF),
        in_specs=[SMEM] + [ANY] * len(arrays),
        out_specs=VMEM,
        scratch_shapes=[pltpu.SemaphoreType.DMA((len(arrays), heads))],
        compiler_params=PACK_PARAMS,
    )(order, *arrays)


def pack_temporal_kernel(items, order_ref, q_ref, k_ref, v_ref, out_ref):
    pieces = q_ref.shape[0] // items
    for which, src in enumerate((q_ref, k_ref, v_ref)):
        for head in range(HT):
            block = src[:, columns_of(order_ref, head)]
            out_ref[head * pieces : (head + 1) * pieces, which] = block.reshape(pieces, items, DEPTH)


def pack_temporal(order, q, k, v, items):
    dests = HT * q.shape[0] // items
    return pl.pallas_call(
        functools.partial(pack_temporal_kernel, items),
        out_shape=jax.ShapeDtypeStruct((dests, 3, items, DEPTH), BF),
        in_specs=[SMEM] + [VMEM] * 3,
        out_specs=VMEM,
        compiler_params=PARAMS,
    )(order, q, k, v)


def temporal_kernel(in_ref, out_ref):
    frames, _, items, depth = in_ref.shape
    total = frames * items
    step = 256
    factor = depth ** (-0.5) * math.log2(math.e)
    k = in_ref[:, 1].reshape(total, depth)
    v = in_ref[:, 2].reshape(total, depth)
    row_item = lax.broadcasted_iota(jnp.int32, (step, total), 0) % items
    col_item = lax.broadcasted_iota(jnp.int32, (step, total), 1) % items
    same = row_item == col_item
    per = step // items
    for at in range(frames // per):
        q = in_ref[at * per : (at + 1) * per, 0].reshape(step, depth)
        s = lax.dot_general(q, k, (((1,), (1,)), ((), ())), preferred_element_type=F32)
        s = jnp.where(same, s * factor, -jnp.inf)
        p = jnp.exp2(s - jnp.max(s, axis=1, keepdims=True))
        total_p = jnp.sum(p, axis=1, keepdims=True)
        o = jnp.dot(p.astype(BF), v, preferred_element_type=F32) / total_p
        out_ref[at * per : (at + 1) * per] = o.astype(BF).reshape(per, items, depth)


def temporal_attend(arrived):
    frames, _, items, depth = arrived.shape
    return pl.pallas_call(
        temporal_kernel,
        out_shape=jax.ShapeDtypeStruct((frames, items, depth), BF),
        in_specs=[VMEM],
        out_specs=VMEM,
        compiler_params=PARAMS,
        cost_estimate=estimate(50),
    )(arrived)


def row_norm(blocks):
    ones = jnp.ones((DEPTH, LANES), BF)
    best = None
    for block in blocks:
        norms = jnp.dot(block * block, ones, preferred_element_type=F32)
        most = jnp.max(norms.reshape(-1, 8, LANES), axis=0)
        best = most if best is None else jnp.maximum(best, most)
    return jnp.max(best)


def used_slot(frames, base, kb_ref, bc_ref, mine, slot):
    frame = base + mine
    target = lax.rem(base + slot + frames, frames)
    hit = False
    for n in range(NB):
        hit = hit | ((kb_ref[frame, n] == target) & (bc_ref[frame] > n))
    return hit


def score_factor():
    return DEPTH ** (-0.5) * math.log2(math.e)


def products(q, k):
    return lax.dot_general(q, k, (((1,), (1,)), ((), ())), preferred_element_type=F32)


def add_frames(acc, q, pairs):
    for k, v, hit in pairs:
        p = jnp.exp2(products(q, k) * score_factor()).astype(BF)
        weight = jnp.where(hit, 1.0, 0.0).astype(BF)
        wide = jnp.concatenate([v * weight, jnp.full(v.shape, weight)], axis=1)
        add = jnp.dot(p, wide, preferred_element_type=F32)
        acc = add if acc is None else acc + add
    return acc


def fold_frame(q, k, v, acc_ref, m_ref):
    wide = jnp.concatenate([v, jnp.ones_like(v)], axis=1)
    s = products(q, k) * score_factor()
    old = m_ref[...]
    new = jnp.maximum(old, jnp.max(s, axis=1, keepdims=True))
    p = jnp.exp2(s - new[:, :1]).astype(BF)
    alpha = jnp.exp2(old - new)
    both = jnp.concatenate([alpha, alpha], axis=1)
    acc_ref[...] = acc_ref[...] * both + jnp.dot(p, wide, preferred_element_type=F32)
    m_ref[...] = new


def small_scores(q_norm, k_norm):
    factor = score_factor() * 1.02
    return q_norm * k_norm * (factor * factor) <= 1e4


def frame_at(ref, which, at, pieces):
    block = ref[pl.ds(at * pieces, pieces), which]
    return block.reshape(pieces * block.shape[1], DEPTH)


def own_kernel(frames, base_ref, kb_ref, bc_ref, q_ref, kv_ref, acc_ref, m_ref, stat_ref):
    pieces = q_ref.shape[0] // BLOCK
    size = pieces * q_ref.shape[2]
    base = base_ref[0]

    def part(which, at):
        return frame_at(kv_ref, which - 1, at, pieces) if which else frame_at(q_ref, 0, at, pieces)

    q_norm = row_norm([part(0, at) for at in range(BLOCK)])
    k_norm = row_norm([part(1, at) for at in range(BLOCK)])
    fast = small_scores(q_norm, k_norm)
    stat_ref[0] = q_norm
    stat_ref[1] = jnp.where(fast, 1.0, 0.0)

    def used(mine, slot):
        return used_slot(frames, base, kb_ref, bc_ref, mine, slot)

    @pl.when(fast)
    def _():
        def frame(mine, carry):
            pairs = [(part(1, slot), part(2, slot), used(mine, slot)) for slot in range(BLOCK)]
            acc_ref[mine] = add_frames(None, part(0, mine), pairs)
            m_ref[mine] = jnp.zeros((size, LANES), F32)
            return carry

        lax.fori_loop(0, BLOCK, frame, 0)

    @pl.when(jnp.logical_not(fast))
    def _():
        def pair(at, carry):
            mine, slot = at // BLOCK, lax.rem(at, BLOCK)

            @pl.when(slot == 0)
            def _():
                acc_ref[mine] = jnp.zeros((size, 2 * DEPTH), F32)
                m_ref[mine] = jnp.full((size, LANES), -jnp.inf, F32)

            @pl.when(used(mine, slot))
            def _():
                fold_frame(part(0, mine), part(1, slot), part(2, slot), acc_ref.at[mine], m_ref.at[mine])

            return carry

        lax.fori_loop(0, BLOCK * BLOCK, pair, 0)


def near_kernel(
    frames, base_ref, kb_ref, bc_ref, stat_ref, q_ref, less_ref, more_ref, acc_hbm, m_hbm, o_ref,
    acc_ref, m_ref, near_ref, sems, acc_sems, m_sem
):
    pieces = q_ref.shape[0] // BLOCK
    rows = q_ref.shape[2]
    base = base_ref[0]
    sums = [
        pltpu.make_async_copy(acc_hbm.at[mine], acc_ref.at[mine], acc_sems.at[mine])
        for mine in range(BLOCK)
    ]
    frames_in = [
        pltpu.make_async_copy(less_ref, near_ref.at[pl.ds(0, W * pieces)], sems.at[0]),
        pltpu.make_async_copy(more_ref, near_ref.at[pl.ds(W * pieces, W * pieces)], sems.at[1]),
    ]
    for copy in frames_in + sums:
        copy.start()
    for copy in frames_in:
        copy.wait()
    part = functools.partial(frame_at, near_ref, pieces=pieces)
    k_norm = row_norm([part(0, at) for at in range(2 * W)])
    fast = small_scores(stat_ref[0], k_norm) & (stat_ref[1] > 0.5)
    for copy in sums:
        copy.wait()

    def query(mine):
        return frame_at(q_ref, 0, mine, pieces)

    def used(mine, at):
        slot = jnp.where(at < W, at - W, at - W + BLOCK)
        return used_slot(frames, base, kb_ref, bc_ref, mine, slot)

    def finish(mine, acc):
        o = (acc[:, :DEPTH] / acc[:, DEPTH:]).astype(BF)
        o_ref[pl.ds(mine * pieces, pieces)] = o.reshape(pieces, rows, DEPTH)

    @pl.when(fast)
    def _():
        def frame(mine, carry):
            pairs = [
                (part(0, mine + j), part(1, mine + j), used(mine, mine + j)) for j in range(W)
            ]
            finish(mine, add_frames(acc_ref[mine], query(mine), pairs))
            return carry

        lax.fori_loop(0, BLOCK, frame, 0)

    @pl.when(jnp.logical_not(fast))
    def _():
        def frame(mine, carry):
            run_copies([pltpu.make_async_copy(m_hbm.at[mine], m_ref, m_sem)])

            def pair(j, inner):
                @pl.when(used(mine, mine + j))
                def _():
                    fold_frame(query(mine), part(0, mine + j), part(1, mine + j), acc_ref.at[mine], m_ref)

                return inner

            lax.fori_loop(0, W, pair, 0)
            finish(mine, acc_ref[mine])
            return carry

        lax.fori_loop(0, BLOCK, frame, 0)


def attend_own(base, kb, bc, q, kv, frames):
    dests, _, rows, depth = q.shape
    size = dests // BLOCK * rows
    return pl.pallas_call(
        functools.partial(own_kernel, frames),
        out_shape=[
            jax.ShapeDtypeStruct((BLOCK, size, 2 * depth), F32),
            jax.ShapeDtypeStruct((BLOCK, size, LANES), F32),
            jax.ShapeDtypeStruct((2,), F32),
        ],
        in_specs=[SMEM] * 3 + [VMEM] * 2,
        out_specs=[VMEM, VMEM, SMEM],
        compiler_params=PARAMS,
        cost_estimate=estimate(10),
    )(base, kb, bc, q, kv)


def attend_near(base, kb, bc, stat, q, less, more, acc, top, frames):
    dests, _, rows, depth = q.shape
    size = dests // BLOCK * rows
    return pl.pallas_call(
        functools.partial(near_kernel, frames),
        out_shape=jax.ShapeDtypeStruct((dests, rows, depth), BF),
        in_specs=[SMEM] * 4 + [VMEM] + [ANY] * 4,
        out_specs=VMEM,
        scratch_shapes=[
            pltpu.VMEM((BLOCK, size, 2 * depth), F32),
            pltpu.VMEM((size, LANES), F32),
            pltpu.VMEM((2 * less.shape[0], *less.shape[1:]), BF),
            pltpu.SemaphoreType.DMA((2,)),
            pltpu.SemaphoreType.DMA((BLOCK,)),
            pltpu.SemaphoreType.DMA,
        ],
        compiler_params=PARAMS,
    )(base, kb, bc, stat, q, less, more, acc, top)


def assemble_kernel(order_ref, t_ref, s_ref, out_ref):
    rows = out_ref.shape[0]
    pieces = t_ref.shape[0] // HT
    for head in range(HT):
        block = t_ref[head * pieces : (head + 1) * pieces].reshape(rows, DEPTH)
        out_ref[:, columns_of(order_ref, head)] = block
    for head in range(s_ref.shape[0]):
        out_ref[:, columns_of(order_ref, HT + head)] = s_ref[head]


def assemble(order, temporal, spatial, rows, width):
    return pl.pallas_call(
        assemble_kernel,
        out_shape=jax.ShapeDtypeStruct((rows, width), BF),
        in_specs=[SMEM, VMEM, VMEM],
        out_specs=VMEM,
        compiler_params=PARAMS,
    )(order, temporal, spatial)


def exchange(array, axes):
    return lax.all_to_all(array, axes, 0, 0, tiled=True)


def from_block(array, by):
    count = lax.axis_size("grp") * lax.axis_size("yh")
    return lax.ppermute(array, ("grp", "yh"), [((i + by) % count, i) for i in range(count)])


def local(queries, keys, values, head_order, key_blocks, block_count):
    rows, width = queries.shape
    blocks = lax.axis_size("grp") * lax.axis_size("yh")
    frames = blocks * BLOCK
    items = HT * rows // frames
    base = (lax.axis_index("grp") * lax.axis_size("yh") + lax.axis_index("yh")) * BLOCK
    base = base.astype(jnp.int32).reshape(1)

    block_axes = ("yl", "zl", "x")
    loop_axes = ("grp", "yh", "yl", "zl")
    st = pack_temporal(head_order, queries, keys, values, items)
    sq = pack_spatial(head_order, (queries,))
    kv = exchange(pack_spatial(head_order, (keys, values)), block_axes)
    pieces = kv.shape[0] // BLOCK
    less = from_block(kv[(BLOCK - W) * pieces :], -1)
    more = from_block(kv[: W * pieces], 1)
    kv, st = lax.optimization_barrier((kv, st))
    at = exchange(st, loop_axes)
    at, sq = lax.optimization_barrier((at, sq))
    q = exchange(sq, block_axes)
    to, q = lax.optimization_barrier((temporal_attend(at), q))
    tr = exchange(to, loop_axes)
    acc, top, stat = attend_own(base, key_blocks, block_count, q, kv, frames)
    so = attend_near(base, key_blocks, block_count, stat, q, less, more, acc, top, frames)
    sr = exchange(so, block_axes)
    return assemble(head_order, tr, sr, rows, width)


def solution(mesh):
    grp, seq = mesh.shape["grp"], mesh.shape["seq"]
    fine = Mesh(mesh.devices.reshape(grp, seq // 16, 2, 2, 4), ("grp", "yh", "yl", "zl", "x"))
    tokens = P(("grp", "yh", "yl", "zl", "x"), None)
    return jax.shard_map(
        local,
        mesh=fine,
        in_specs=(tokens, tokens, tokens, P(), P(), P()),
        out_specs=tokens,
        check_vma=False,
    )
```

```python
import functools
import math

import jax
import jax.numpy as jnp
from jax import lax
from jax.experimental import pallas as pl
from jax.experimental.pallas import tpu as pltpu
from jax.sharding import Mesh
from jax.sharding import PartitionSpec as P

HT = 8
W = 3
NB = 6
BLOCK = 4
DEPTH = 128
LANES = 128
BF = jnp.bfloat16
F32 = jnp.float32
VMEM = pl.BlockSpec(memory_space=pltpu.VMEM)
SMEM = pl.BlockSpec(memory_space=pltpu.SMEM)
ANY = pl.BlockSpec(memory_space=pl.ANY)
PARAMS = pltpu.CompilerParams(vmem_limit_bytes=40 * 1024 * 1024)
PACK_PARAMS = pltpu.CompilerParams(vmem_limit_bytes=58 * 1024 * 1024)


def estimate(gigaflops):
    return pl.CostEstimate(flops=gigaflops * 10**9, bytes_accessed=1 << 20, transcendentals=1 << 20)


def columns_of(order_ref, slot):
    return pl.ds(pl.multiple_of(order_ref[slot] * DEPTH, DEPTH), DEPTH)


def run_copies(copies):
    for copy in copies:
        copy.start()
    for copy in copies:
        copy.wait()


def pack_spatial_kernel(order_ref, *refs):
    dst, sems = refs[-2:]
    copies = []
    for which, src in enumerate(refs[:-2]):
        for head in range(dst.shape[0]):
            column = columns_of(order_ref, HT + head)
            copies.append(
                pltpu.make_async_copy(src.at[:, column], dst.at[head, which], sems.at[which, head])
            )
    run_copies(copies)


def pack_spatial(order, arrays):
    rows, width = arrays[0].shape
    heads = width // DEPTH - HT
    return pl.pallas_call(
        pack_spatial_kernel,
        out_shape=jax.ShapeDtypeStruct((heads, len(arrays), rows, DEPTH), BF),
        in_specs=[SMEM] + [ANY] * len(arrays),
        out_specs=VMEM,
        scratch_shapes=[pltpu.SemaphoreType.DMA((len(arrays), heads))],
        compiler_params=PACK_PARAMS,
    )(order, *arrays)


def pack_temporal_kernel(items, core_ref, order_ref, q_ref, k_ref, v_ref, mine_ref, other_ref):
    pieces = q_ref.shape[0] // items
    for out, core in ((mine_ref, core_ref[0]), (other_ref, 1 - core_ref[0])):
        for which, src in enumerate((q_ref, k_ref, v_ref)):
            for pair in range(HT // 2):
                block = src[:, columns_of(order_ref, 2 * pair + core)]
                out[pair * pieces : (pair + 1) * pieces, which] = block.reshape(pieces, items, DEPTH)


def pack_temporal(order, core, q, k, v, items):
    out = jax.ShapeDtypeStruct((HT // 2 * q.shape[0] // items, 3, items, DEPTH), BF)
    return pl.pallas_call(
        functools.partial(pack_temporal_kernel, items),
        out_shape=[out, out],
        in_specs=[SMEM, SMEM] + [VMEM] * 3,
        out_specs=[VMEM, VMEM],
        compiler_params=PARAMS,
    )(core, order, q, k, v)


def join_kernel(a_ref, b_ref, out_ref):
    out_ref[:, 0] = a_ref[...]
    out_ref[:, 1] = b_ref[...]


def join(mine, other):
    return pl.pallas_call(
        join_kernel,
        out_shape=jax.ShapeDtypeStruct((mine.shape[0], 2, *mine.shape[1:]), BF),
        in_specs=[VMEM] * 2,
        out_specs=VMEM,
        compiler_params=PARAMS,
    )(mine, other)


def temporal_kernel(core_ref, in_ref, out_ref):
    places, cores, _, items, depth = in_ref.shape
    total = places * cores * items
    per = 16
    step = per * cores * items
    inner = out_ref.shape[0] // HT
    k = in_ref[:, :, 1].reshape(total, depth)
    v = in_ref[:, :, 2].reshape(total, depth)
    row_item = lax.broadcasted_iota(jnp.int32, (step, total), 0) % items
    col_item = lax.broadcasted_iota(jnp.int32, (step, total), 1) % items
    same = row_item == col_item
    for at in range(places // per):
        q = in_ref[at * per : (at + 1) * per, :, 0].reshape(step, depth)
        s = jnp.where(same, products(q, k) * score_factor(), -jnp.inf)
        p = jnp.exp2(s - jnp.max(s, axis=1, keepdims=True))
        total_p = jnp.sum(p, axis=1, keepdims=True)
        o = jnp.dot(p.astype(BF), v, preferred_element_type=F32) / total_p
        o = o.astype(BF).reshape(per, cores, items, depth)
        high, low = divmod(at * per, inner)
        for which, core in enumerate((core_ref[0], 1 - core_ref[0])):
            first = (high * cores + core) * inner + low
            out_ref[pl.ds(first, per)] = o[:, which]


def temporal_attend(core, arrived):
    places, cores, _, items, depth = arrived.shape
    return pl.pallas_call(
        temporal_kernel,
        out_shape=jax.ShapeDtypeStruct((places * cores, items, depth), BF),
        in_specs=[SMEM, VMEM],
        out_specs=VMEM,
        compiler_params=PARAMS,
        cost_estimate=estimate(50),
    )(core, arrived)


def row_norm(blocks):
    ones = jnp.ones((DEPTH, LANES), BF)
    best = None
    for block in blocks:
        norms = jnp.dot(block * block, ones, preferred_element_type=F32)
        most = jnp.max(norms.reshape(-1, 8, LANES), axis=0)
        best = most if best is None else jnp.maximum(best, most)
    return jnp.max(best)


def used_slot(frames, base, kb_ref, bc_ref, mine, slot):
    frame = base + mine
    target = lax.rem(base + slot + frames, frames)
    hit = False
    for n in range(NB):
        hit = hit | ((kb_ref[frame, n] == target) & (bc_ref[frame] > n))
    return hit


def score_factor():
    return DEPTH ** (-0.5) * math.log2(math.e)


def products(q, k):
    return lax.dot_general(q, k, (((1,), (1,)), ((), ())), preferred_element_type=F32)


def add_frames(acc, q, pairs):
    for k, v, hit in pairs:
        p = jnp.exp2(products(q, k) * score_factor()).astype(BF)
        weight = jnp.where(hit, 1.0, 0.0).astype(BF)
        wide = jnp.concatenate([v * weight, jnp.full(v.shape, weight)], axis=1)
        add = jnp.dot(p, wide, preferred_element_type=F32)
        acc = add if acc is None else acc + add
    return acc


def fold_frame(q, k, v, acc_ref, m_ref):
    wide = jnp.concatenate([v, jnp.ones_like(v)], axis=1)
    s = products(q, k) * score_factor()
    old = m_ref[...]
    new = jnp.maximum(old, jnp.max(s, axis=1, keepdims=True))
    p = jnp.exp2(s - new[:, :1]).astype(BF)
    alpha = jnp.exp2(old - new)
    both = jnp.concatenate([alpha, alpha], axis=1)
    acc_ref[...] = acc_ref[...] * both + jnp.dot(p, wide, preferred_element_type=F32)
    m_ref[...] = new


def small_scores(q_norm, k_norm):
    factor = score_factor() * 1.02
    return q_norm * k_norm * (factor * factor) <= 1e4


def frame_at(ref, which, at, pieces):
    block = ref[pl.ds(at * pieces, pieces), which]
    return block.reshape(pieces * block.shape[1], DEPTH)


def own_kernel(frames, base_ref, kb_ref, bc_ref, in_ref, acc_ref, m_ref, stat_ref):
    pieces = in_ref.shape[0] // BLOCK
    size = pieces * in_ref.shape[2]
    base = base_ref[0]
    part = functools.partial(frame_at, in_ref, pieces=pieces)
    q_norm = row_norm([part(0, at) for at in range(BLOCK)])
    k_norm = row_norm([part(1, at) for at in range(BLOCK)])
    fast = small_scores(q_norm, k_norm)
    stat_ref[0] = q_norm
    stat_ref[1] = jnp.where(fast, 1.0, 0.0)

    def used(mine, slot):
        return used_slot(frames, base, kb_ref, bc_ref, mine, slot)

    @pl.when(fast)
    def _():
        def frame(mine, carry):
            pairs = [(part(1, slot), part(2, slot), used(mine, slot)) for slot in range(BLOCK)]
            acc_ref[mine] = add_frames(None, part(0, mine), pairs)
            m_ref[mine] = jnp.zeros((size, LANES), F32)
            return carry

        lax.fori_loop(0, BLOCK, frame, 0)

    @pl.when(jnp.logical_not(fast))
    def _():
        def pair(at, carry):
            mine, slot = at // BLOCK, lax.rem(at, BLOCK)

            @pl.when(slot == 0)
            def _():
                acc_ref[mine] = jnp.zeros((size, 2 * DEPTH), F32)
                m_ref[mine] = jnp.full((size, LANES), -jnp.inf, F32)

            @pl.when(used(mine, slot))
            def _():
                fold_frame(part(0, mine), part(1, slot), part(2, slot), acc_ref.at[mine], m_ref.at[mine])

            return carry

        lax.fori_loop(0, BLOCK * BLOCK, pair, 0)


def near_kernel(
    frames, base_ref, kb_ref, bc_ref, stat_ref, q_ref, less_ref, more_ref, acc_hbm, m_hbm, o_ref,
    acc_ref, m_ref, near_ref, sems, acc_sems, m_sem
):
    pieces = q_ref.shape[0] // BLOCK
    rows = q_ref.shape[2]
    base = base_ref[0]
    sums = [
        pltpu.make_async_copy(acc_hbm.at[mine], acc_ref.at[mine], acc_sems.at[mine])
        for mine in range(BLOCK)
    ]
    frames_in = [
        pltpu.make_async_copy(less_ref, near_ref.at[pl.ds(0, W * pieces)], sems.at[0]),
        pltpu.make_async_copy(more_ref, near_ref.at[pl.ds(W * pieces, W * pieces)], sems.at[1]),
    ]
    for copy in frames_in + sums:
        copy.start()
    for copy in frames_in:
        copy.wait()
    part = functools.partial(frame_at, near_ref, pieces=pieces)
    k_norm = row_norm([part(0, at) for at in range(2 * W)])
    fast = small_scores(stat_ref[0], k_norm) & (stat_ref[1] > 0.5)
    for copy in sums:
        copy.wait()

    def query(mine):
        return frame_at(q_ref, 0, mine, pieces)

    def used(mine, at):
        slot = jnp.where(at < W, at - W, at - W + BLOCK)
        return used_slot(frames, base, kb_ref, bc_ref, mine, slot)

    def finish(mine, acc):
        o = (acc[:, :DEPTH] / acc[:, DEPTH:]).astype(BF)
        o_ref[pl.ds(mine * pieces, pieces)] = o.reshape(pieces, rows, DEPTH)

    @pl.when(fast)
    def _():
        def frame(mine, carry):
            pairs = [
                (part(0, mine + j), part(1, mine + j), used(mine, mine + j)) for j in range(W)
            ]
            finish(mine, add_frames(acc_ref[mine], query(mine), pairs))
            return carry

        lax.fori_loop(0, BLOCK, frame, 0)

    @pl.when(jnp.logical_not(fast))
    def _():
        def frame(mine, carry):
            run_copies([pltpu.make_async_copy(m_hbm.at[mine], m_ref, m_sem)])

            def pair(j, inner):
                @pl.when(used(mine, mine + j))
                def _():
                    fold_frame(query(mine), part(0, mine + j), part(1, mine + j), acc_ref.at[mine], m_ref)

                return inner

            lax.fori_loop(0, W, pair, 0)
            finish(mine, acc_ref[mine])
            return carry

        lax.fori_loop(0, BLOCK, frame, 0)


def attend_own(base, kb, bc, arrived, frames):
    dests, _, rows, depth = arrived.shape
    size = dests // BLOCK * rows
    return pl.pallas_call(
        functools.partial(own_kernel, frames),
        out_shape=[
            jax.ShapeDtypeStruct((BLOCK, size, 2 * depth), F32),
            jax.ShapeDtypeStruct((BLOCK, size, LANES), F32),
            jax.ShapeDtypeStruct((2,), F32),
        ],
        in_specs=[SMEM] * 3 + [VMEM],
        out_specs=[VMEM, VMEM, SMEM],
        compiler_params=PARAMS,
        cost_estimate=estimate(10),
    )(base, kb, bc, arrived)


def attend_near(base, kb, bc, stat, q, less, more, acc, top, frames):
    dests, _, rows, depth = q.shape
    size = dests // BLOCK * rows
    return pl.pallas_call(
        functools.partial(near_kernel, frames),
        out_shape=jax.ShapeDtypeStruct((dests, rows, depth), BF),
        in_specs=[SMEM] * 4 + [VMEM] + [ANY] * 4,
        out_specs=VMEM,
        scratch_shapes=[
            pltpu.VMEM((BLOCK, size, 2 * depth), F32),
            pltpu.VMEM((size, LANES), F32),
            pltpu.VMEM((2 * less.shape[0], *less.shape[1:]), BF),
            pltpu.SemaphoreType.DMA((2,)),
            pltpu.SemaphoreType.DMA((BLOCK,)),
            pltpu.SemaphoreType.DMA,
        ],
        compiler_params=PARAMS,
    )(base, kb, bc, stat, q, less, more, acc, top)


def assemble_kernel(order_ref, t_ref, s_ref, out_ref):
    rows = out_ref.shape[0]
    pieces = t_ref.shape[0] // HT
    for head in range(HT):
        block = t_ref[head * pieces : (head + 1) * pieces].reshape(rows, DEPTH)
        out_ref[:, columns_of(order_ref, head)] = block
    for head in range(s_ref.shape[0]):
        out_ref[:, columns_of(order_ref, HT + head)] = s_ref[head]


def assemble(order, temporal, spatial, rows, width):
    return pl.pallas_call(
        assemble_kernel,
        out_shape=jax.ShapeDtypeStruct((rows, width), BF),
        in_specs=[SMEM, VMEM, VMEM],
        out_specs=VMEM,
        compiler_params=PARAMS,
    )(order, temporal, spatial)


def exchange(array, axes):
    return lax.all_to_all(array, axes, 0, 0, tiled=True)


def from_block(array, by):
    count = lax.axis_size("zh") * lax.axis_size("core") * lax.axis_size("yh")
    return lax.ppermute(array, ("zh", "core", "yh"), [((i + by) % count, i) for i in range(count)])


def local(queries, keys, values, head_order, key_blocks, block_count):
    rows, width = queries.shape
    blocks = lax.axis_size("zh") * lax.axis_size("core") * lax.axis_size("yh")
    frames = blocks * BLOCK
    items = HT * rows // frames
    base = lax.axis_index(("zh", "core", "yh")) * BLOCK
    base = base.astype(jnp.int32).reshape(1)

    block_axes = ("yl", "zl", "x")
    loop_axes = ("zh", "core", "yh", "yl", "zl")
    core = lax.axis_index("core").astype(jnp.int32).reshape(1)
    mine, other = pack_temporal(head_order, core, queries, keys, values, items)
    st = join(mine, lax.ppermute(other, "core", [(0, 1), (1, 0)]))
    qkv = exchange(pack_spatial(head_order, (queries, keys, values)), block_axes)
    pieces = qkv.shape[0] // BLOCK
    less = from_block(qkv[(BLOCK - W) * pieces :, 1:], -1)
    more = from_block(qkv[: W * pieces, 1:], 1)
    qkv, st = lax.optimization_barrier((qkv, st))
    at = exchange(st, ("zh", "yh", "yl", "zl"))
    acc, top, stat = attend_own(base, key_blocks, block_count, qkv, frames)
    to, stat = lax.optimization_barrier((temporal_attend(core, at), stat))
    tr = exchange(to, loop_axes)
    so = attend_near(base, key_blocks, block_count, stat, qkv, less, more, acc, top, frames)
    sr = exchange(so, block_axes)
    return assemble(head_order, tr, sr, rows, width)


def solution(mesh):
    grp, seq = mesh.shape["grp"], mesh.shape["seq"]
    names = ("zh", "core", "yh", "yl", "zl", "x")
    fine = Mesh(mesh.devices.reshape(grp // 2, 2, seq // 16, 2, 2, 4), names)
    tokens = P(names, None)
    return jax.shard_map(
        local,
        mesh=fine,
        in_specs=(tokens, tokens, tokens, P(), P(), P()),
        out_specs=tokens,
        check_vma=False,
    )
```

```python
import functools
import math

import jax
import jax.numpy as jnp
from jax import lax
from jax.experimental import pallas as pl
from jax.experimental.pallas import tpu as pltpu
from jax.sharding import Mesh
from jax.sharding import PartitionSpec as P

HT = 8
W = 3
NB = 6
BLOCK = 4
DEPTH = 128
LANES = 128
BF = jnp.bfloat16
F32 = jnp.float32
VMEM = pl.BlockSpec(memory_space=pltpu.VMEM)
SMEM = pl.BlockSpec(memory_space=pltpu.SMEM)
ANY = pl.BlockSpec(memory_space=pl.ANY)
PARAMS = pltpu.CompilerParams(vmem_limit_bytes=40 * 1024 * 1024)
PACK_PARAMS = pltpu.CompilerParams(vmem_limit_bytes=58 * 1024 * 1024)


def estimate(gigaflops):
    return pl.CostEstimate(flops=gigaflops * 10**9, bytes_accessed=1 << 20, transcendentals=1 << 20)


def columns_of(order_ref, slot):
    return pl.ds(pl.multiple_of(order_ref[slot] * DEPTH, DEPTH), DEPTH)


def run_copies(copies):
    for copy in copies:
        copy.start()
    for copy in copies:
        copy.wait()


def pack_spatial_kernel(order_ref, *refs):
    dst, sems = refs[-2:]
    copies = []
    for which, src in enumerate(refs[:-2]):
        for head in range(dst.shape[0]):
            column = columns_of(order_ref, HT + head)
            copies.append(
                pltpu.make_async_copy(src.at[:, column], dst.at[head, which], sems.at[which, head])
            )
    run_copies(copies)


def pack_spatial(order, arrays):
    rows, width = arrays[0].shape
    heads = width // DEPTH - HT
    return pl.pallas_call(
        pack_spatial_kernel,
        out_shape=jax.ShapeDtypeStruct((heads, len(arrays), rows, DEPTH), BF),
        in_specs=[SMEM] + [ANY] * len(arrays),
        out_specs=VMEM,
        scratch_shapes=[pltpu.SemaphoreType.DMA((len(arrays), heads))],
        compiler_params=PACK_PARAMS,
    )(order, *arrays)


def pack_temporal_kernel(items, core_ref, order_ref, q_ref, k_ref, v_ref, mine_ref, other_ref):
    pieces = q_ref.shape[0] // items
    for out, core in ((mine_ref, core_ref[0]), (other_ref, 1 - core_ref[0])):
        for which, src in enumerate((q_ref, k_ref, v_ref)):
            for pair in range(HT // 2):
                block = src[:, columns_of(order_ref, 2 * pair + core)]
                out[pair * pieces : (pair + 1) * pieces, which] = block.reshape(pieces, items, DEPTH)


def pack_temporal(order, core, q, k, v, items):
    out = jax.ShapeDtypeStruct((HT // 2 * q.shape[0] // items, 3, items, DEPTH), BF)
    return pl.pallas_call(
        functools.partial(pack_temporal_kernel, items),
        out_shape=[out, out],
        in_specs=[SMEM, SMEM] + [VMEM] * 3,
        out_specs=[VMEM, VMEM],
        compiler_params=PARAMS,
    )(core, order, q, k, v)


def part_kernel(low_ref, a_ref, b_ref, mine_ref, other_ref):
    for out, low in ((mine_ref, low_ref[0]), (other_ref, 1 - low_ref[0])):
        for which, src in enumerate((a_ref, b_ref)):
            out[:, pl.ds(which, 1)] = src[:, pl.ds(low, 1)]


def part(low, a, b):
    out = jax.ShapeDtypeStruct(a.shape, BF)
    return pl.pallas_call(
        part_kernel,
        out_shape=[out, out],
        in_specs=[SMEM, VMEM, VMEM],
        out_specs=[VMEM, VMEM],
        compiler_params=PARAMS,
    )(low, a, b)


def join_kernel(a_ref, b_ref, out_ref):
    out_ref[:, 0] = a_ref[...]
    out_ref[:, 1] = b_ref[...]


def join(mine, other):
    return pl.pallas_call(
        join_kernel,
        out_shape=jax.ShapeDtypeStruct((mine.shape[0], 2, *mine.shape[1:]), BF),
        in_specs=[VMEM] * 2,
        out_specs=VMEM,
        compiler_params=PARAMS,
    )(mine, other)


def temporal_kernel(core_ref, low_ref, in_ref, out_ref):
    places, lows, cores, _, items, depth = in_ref.shape
    total = places * lows * cores * items
    per = out_ref.shape[1]
    step = per * lows * cores * items
    k = in_ref[:, :, :, 1].reshape(total, depth)
    v = in_ref[:, :, :, 2].reshape(total, depth)
    row_item = lax.broadcasted_iota(jnp.int32, (step, total), 0) % items
    col_item = lax.broadcasted_iota(jnp.int32, (step, total), 1) % items
    same = row_item == col_item
    for high in range(places // per):
        q = in_ref[high * per : (high + 1) * per, :, :, 0].reshape(step, depth)
        s = jnp.where(same, products(q, k) * score_factor(), -jnp.inf)
        p = jnp.exp2(s - jnp.max(s, axis=1, keepdims=True))
        total_p = jnp.sum(p, axis=1, keepdims=True)
        o = jnp.dot(p.astype(BF), v, preferred_element_type=F32) / total_p
        o = o.astype(BF).reshape(per, lows, cores, items, depth)
        for i, low in enumerate((low_ref[0], 1 - low_ref[0])):
            for j, core in enumerate((core_ref[0], 1 - core_ref[0])):
                out_ref[pl.ds(high * cores + core, 1), :, pl.ds(low, 1)] = o[:, i, j][None, :, None]


def temporal_attend(core, low, arrived, ys):
    places, lows, cores, _, items, depth = arrived.shape
    frames = places * lows * cores
    out = pl.pallas_call(
        temporal_kernel,
        out_shape=jax.ShapeDtypeStruct((frames // (ys * lows), ys, lows, items, depth), BF),
        in_specs=[SMEM, SMEM, VMEM],
        out_specs=VMEM,
        compiler_params=PARAMS,
        cost_estimate=estimate(50),
    )(core, low, arrived)
    return out.reshape(frames, items, depth)


def row_norm(blocks):
    ones = jnp.ones((DEPTH, LANES), BF)
    best = None
    for block in blocks:
        norms = jnp.dot(block * block, ones, preferred_element_type=F32)
        most = jnp.max(norms.reshape(-1, 8, LANES), axis=0)
        best = most if best is None else jnp.maximum(best, most)
    return jnp.max(best)


def used_slot(frames, base, kb_ref, bc_ref, mine, slot):
    frame = base + mine
    target = lax.rem(base + slot + frames, frames)
    hit = False
    for n in range(NB):
        hit = hit | ((kb_ref[frame, n] == target) & (bc_ref[frame] > n))
    return hit


def score_factor():
    return DEPTH ** (-0.5) * math.log2(math.e)


def products(q, k):
    return lax.dot_general(q, k, (((1,), (1,)), ((), ())), preferred_element_type=F32)


def add_frames(acc, q, pairs):
    for k, v, hit in pairs:
        p = jnp.exp2(products(q, k) * score_factor()).astype(BF)
        weight = jnp.where(hit, 1.0, 0.0).astype(BF)
        wide = jnp.concatenate([v * weight, jnp.full(v.shape, weight)], axis=1)
        add = jnp.dot(p, wide, preferred_element_type=F32)
        acc = add if acc is None else acc + add
    return acc


def fold_frame(q, k, v, acc_ref, m_ref):
    wide = jnp.concatenate([v, jnp.ones_like(v)], axis=1)
    s = products(q, k) * score_factor()
    old = m_ref[...]
    new = jnp.maximum(old, jnp.max(s, axis=1, keepdims=True))
    p = jnp.exp2(s - new[:, :1]).astype(BF)
    alpha = jnp.exp2(old - new)
    both = jnp.concatenate([alpha, alpha], axis=1)
    acc_ref[...] = acc_ref[...] * both + jnp.dot(p, wide, preferred_element_type=F32)
    m_ref[...] = new


def small_scores(q_norm, k_norm):
    factor = score_factor() * 1.02
    return q_norm * k_norm * (factor * factor) <= 1e4


def frame_at(ref, which, at, pieces):
    block = ref[pl.ds(at * pieces, pieces), which]
    return block.reshape(pieces * block.shape[1], DEPTH)


def own_kernel(frames, base_ref, kb_ref, bc_ref, in_ref, acc_ref, m_ref, stat_ref):
    pieces = in_ref.shape[0] // BLOCK
    size = pieces * in_ref.shape[2]
    base = base_ref[0]
    part = functools.partial(frame_at, in_ref, pieces=pieces)
    q_norm = row_norm([part(0, at) for at in range(BLOCK)])
    k_norm = row_norm([part(1, at) for at in range(BLOCK)])
    fast = small_scores(q_norm, k_norm)
    stat_ref[0] = q_norm
    stat_ref[1] = jnp.where(fast, 1.0, 0.0)

    def used(mine, slot):
        return used_slot(frames, base, kb_ref, bc_ref, mine, slot)

    @pl.when(fast)
    def _():
        def frame(mine, carry):
            pairs = [(part(1, slot), part(2, slot), used(mine, slot)) for slot in range(BLOCK)]
            acc_ref[mine] = add_frames(None, part(0, mine), pairs)
            m_ref[mine] = jnp.zeros((size, LANES), F32)
            return carry

        lax.fori_loop(0, BLOCK, frame, 0)

    @pl.when(jnp.logical_not(fast))
    def _():
        def pair(at, carry):
            mine, slot = at // BLOCK, lax.rem(at, BLOCK)

            @pl.when(slot == 0)
            def _():
                acc_ref[mine] = jnp.zeros((size, 2 * DEPTH), F32)
                m_ref[mine] = jnp.full((size, LANES), -jnp.inf, F32)

            @pl.when(used(mine, slot))
            def _():
                fold_frame(part(0, mine), part(1, slot), part(2, slot), acc_ref.at[mine], m_ref.at[mine])

            return carry

        lax.fori_loop(0, BLOCK * BLOCK, pair, 0)


def near_kernel(
    frames, base_ref, kb_ref, bc_ref, stat_ref, in_ref, less_ref, more_ref, acc_hbm, m_hbm, o_ref,
    acc_ref, m_ref, near_ref, q_ref, sems, acc_sems, m_sem
):
    pieces = in_ref.shape[0] // BLOCK
    rows = in_ref.shape[2]
    base = base_ref[0]
    sums = [
        pltpu.make_async_copy(acc_hbm.at[mine], acc_ref.at[mine], acc_sems.at[mine])
        for mine in range(BLOCK)
    ]
    frames_in = [
        pltpu.make_async_copy(less_ref, near_ref.at[pl.ds(0, W * pieces)], sems.at[0]),
        pltpu.make_async_copy(more_ref, near_ref.at[pl.ds(W * pieces, W * pieces)], sems.at[1]),
        pltpu.make_async_copy(in_ref.at[:, pl.ds(0, 1)], q_ref, sems.at[2]),
    ]
    for copy in frames_in + sums:
        copy.start()
    for copy in frames_in:
        copy.wait()
    part = functools.partial(frame_at, near_ref, pieces=pieces)
    k_norm = row_norm([part(0, at) for at in range(2 * W)])
    fast = small_scores(stat_ref[0], k_norm) & (stat_ref[1] > 0.5)
    for copy in sums:
        copy.wait()

    def query(mine):
        return frame_at(q_ref, 0, mine, pieces)

    def used(mine, at):
        slot = jnp.where(at < W, at - W, at - W + BLOCK)
        return used_slot(frames, base, kb_ref, bc_ref, mine, slot)

    def finish(mine, acc):
        o = (acc[:, :DEPTH] / acc[:, DEPTH:]).astype(BF)
        o_ref[pl.ds(mine * pieces, pieces)] = o.reshape(pieces, rows, DEPTH)

    @pl.when(fast)
    def _():
        def frame(mine, carry):
            pairs = [
                (part(0, mine + j), part(1, mine + j), used(mine, mine + j)) for j in range(W)
            ]
            finish(mine, add_frames(acc_ref[mine], query(mine), pairs))
            return carry

        lax.fori_loop(0, BLOCK, frame, 0)

    @pl.when(jnp.logical_not(fast))
    def _():
        def frame(mine, carry):
            run_copies([pltpu.make_async_copy(m_hbm.at[mine], m_ref, m_sem)])

            def pair(j, inner):
                @pl.when(used(mine, mine + j))
                def _():
                    fold_frame(query(mine), part(0, mine + j), part(1, mine + j), acc_ref.at[mine], m_ref)

                return inner

            lax.fori_loop(0, W, pair, 0)
            finish(mine, acc_ref[mine])
            return carry

        lax.fori_loop(0, BLOCK, frame, 0)


def attend_own(base, kb, bc, arrived, frames):
    dests, _, rows, depth = arrived.shape
    size = dests // BLOCK * rows
    return pl.pallas_call(
        functools.partial(own_kernel, frames),
        out_shape=[
            jax.ShapeDtypeStruct((BLOCK, size, 2 * depth), F32),
            jax.ShapeDtypeStruct((BLOCK, size, LANES), F32),
            jax.ShapeDtypeStruct((2,), F32),
        ],
        in_specs=[SMEM] * 3 + [VMEM],
        out_specs=[VMEM, VMEM, SMEM],
        compiler_params=PARAMS,
        cost_estimate=estimate(10),
    )(base, kb, bc, arrived)


def attend_near(base, kb, bc, stat, q, less, more, acc, top, frames):
    dests, _, rows, depth = q.shape
    size = dests // BLOCK * rows
    return pl.pallas_call(
        functools.partial(near_kernel, frames),
        out_shape=jax.ShapeDtypeStruct((dests, rows, depth), BF),
        in_specs=[SMEM] * 4 + [ANY] * 5,
        out_specs=VMEM,
        scratch_shapes=[
            pltpu.VMEM((BLOCK, size, 2 * depth), F32),
            pltpu.VMEM((size, LANES), F32),
            pltpu.VMEM((2 * less.shape[0], *less.shape[1:]), BF),
            pltpu.VMEM((dests, 1, rows, depth), BF),
            pltpu.SemaphoreType.DMA((3,)),
            pltpu.SemaphoreType.DMA((BLOCK,)),
            pltpu.SemaphoreType.DMA,
        ],
        compiler_params=PARAMS,
    )(base, kb, bc, stat, q, less, more, acc, top)


def assemble_kernel(order_ref, t_ref, s_ref, out_ref):
    rows = out_ref.shape[0]
    pieces = t_ref.shape[0] // HT
    for head in range(HT):
        block = t_ref[head * pieces : (head + 1) * pieces].reshape(rows, DEPTH)
        out_ref[:, columns_of(order_ref, head)] = block
    for head in range(s_ref.shape[0]):
        out_ref[:, columns_of(order_ref, HT + head)] = s_ref[head]


def assemble(order, temporal, spatial, rows, width):
    return pl.pallas_call(
        assemble_kernel,
        out_shape=jax.ShapeDtypeStruct((rows, width), BF),
        in_specs=[SMEM, VMEM, VMEM],
        out_specs=VMEM,
        compiler_params=PARAMS,
    )(order, temporal, spatial)


def exchange(array, axes):
    return lax.all_to_all(array, axes, 0, 0, tiled=True)


def from_block(array, by):
    count = lax.axis_size("zh") * lax.axis_size("core") * lax.axis_size("yh")
    return lax.ppermute(array, ("zh", "core", "yh"), [((i + by) % count, i) for i in range(count)])


def local(queries, keys, values, head_order, key_blocks, block_count):
    rows, width = queries.shape
    blocks = lax.axis_size("zh") * lax.axis_size("core") * lax.axis_size("yh")
    frames = blocks * BLOCK
    items = HT * rows // frames
    base = lax.axis_index(("zh", "core", "yh")) * BLOCK
    base = base.astype(jnp.int32).reshape(1)

    block_axes = ("yl", "zl", "x")
    loop_axes = ("zh", "core", "yh", "yl", "zl")
    core = lax.axis_index("core").astype(jnp.int32).reshape(1)
    low = lax.axis_index("zl").astype(jnp.int32).reshape(1)
    ys = lax.axis_size("yh") * lax.axis_size("yl")
    mine, other = pack_temporal(head_order, core, queries, keys, values, items)
    other = lax.ppermute(other, "core", [(0, 1), (1, 0)])
    by_low = (mine.shape[0] // 2, 2, *mine.shape[1:])
    mine, other = part(low, mine.reshape(by_low), other.reshape(by_low))
    st = join(mine, lax.ppermute(other, "zl", [(0, 1), (1, 0)]))
    qkv = exchange(pack_spatial(head_order, (queries, keys, values)), block_axes)
    pieces = qkv.shape[0] // BLOCK
    less = from_block(qkv[(BLOCK - W) * pieces :, 1:], -1)
    more = from_block(qkv[: W * pieces, 1:], 1)
    qkv, st = lax.optimization_barrier((qkv, st))
    at = exchange(st, ("zh", "yh", "yl"))
    acc, top, stat = attend_own(base, key_blocks, block_count, qkv, frames)
    to, stat = lax.optimization_barrier((temporal_attend(core, low, at, ys), stat))
    tr = exchange(to, loop_axes)
    so = attend_near(base, key_blocks, block_count, stat, qkv, less, more, acc, top, frames)
    sr = exchange(so, block_axes)
    return assemble(head_order, tr, sr, rows, width)


def solution(mesh):
    grp, seq = mesh.shape["grp"], mesh.shape["seq"]
    names = ("zh", "core", "yh", "yl", "zl", "x")
    fine = Mesh(mesh.devices.reshape(grp // 2, 2, seq // 16, 2, 2, 4), names)
    tokens = P(names, None)
    return jax.shard_map(
        local,
        mesh=fine,
        in_specs=(tokens, tokens, tokens, P(), P(), P()),
        out_specs=tokens,
        check_vma=False,
    )
```

```python
import functools
import math

import jax
import jax.numpy as jnp
from jax import lax
from jax.experimental import pallas as pl
from jax.experimental.pallas import tpu as pltpu
from jax.sharding import Mesh
from jax.sharding import PartitionSpec as P

HT = 8
W = 3
NB = 6
BLOCK = 4
DEPTH = 128
LANES = 128
BF = jnp.bfloat16
F32 = jnp.float32
VMEM = pl.BlockSpec(memory_space=pltpu.VMEM)
SMEM = pl.BlockSpec(memory_space=pltpu.SMEM)
ANY = pl.BlockSpec(memory_space=pl.ANY)
PARAMS = pltpu.CompilerParams(vmem_limit_bytes=40 * 1024 * 1024)
PACK_PARAMS = pltpu.CompilerParams(vmem_limit_bytes=58 * 1024 * 1024)


def estimate(gigaflops):
    return pl.CostEstimate(flops=gigaflops * 10**9, bytes_accessed=1 << 20, transcendentals=1 << 20)


def columns_of(order_ref, slot):
    return pl.ds(pl.multiple_of(order_ref[slot] * DEPTH, DEPTH), DEPTH)


def run_copies(copies):
    for copy in copies:
        copy.start()
    for copy in copies:
        copy.wait()


def pack_spatial_kernel(order_ref, *refs):
    dst, sems = refs[-2:]
    copies = []
    for which, src in enumerate(refs[:-2]):
        for head in range(dst.shape[0]):
            column = columns_of(order_ref, HT + head)
            copies.append(
                pltpu.make_async_copy(src.at[:, column], dst.at[head, which], sems.at[which, head])
            )
    run_copies(copies)


def pack_spatial(order, arrays):
    rows, width = arrays[0].shape
    heads = width // DEPTH - HT
    return pl.pallas_call(
        pack_spatial_kernel,
        out_shape=jax.ShapeDtypeStruct((heads, len(arrays), rows, DEPTH), BF),
        in_specs=[SMEM] + [ANY] * len(arrays),
        out_specs=VMEM,
        scratch_shapes=[pltpu.SemaphoreType.DMA((len(arrays), heads))],
        compiler_params=PACK_PARAMS,
    )(order, *arrays)


def pack_temporal_kernel(items, core_ref, order_ref, q_ref, k_ref, v_ref, mine_ref, other_ref):
    pieces = q_ref.shape[0] // items
    for out, core in ((mine_ref, core_ref[0]), (other_ref, 1 - core_ref[0])):
        for which, src in enumerate((q_ref, k_ref, v_ref)):
            for pair in range(HT // 2):
                block = src[:, columns_of(order_ref, 2 * pair + core)]
                out[pair * pieces : (pair + 1) * pieces, which] = block.reshape(pieces, items, DEPTH)


def pack_temporal(order, core, q, k, v, items):
    out = jax.ShapeDtypeStruct((HT // 2 * q.shape[0] // items, 3, items, DEPTH), BF)
    return pl.pallas_call(
        functools.partial(pack_temporal_kernel, items),
        out_shape=[out, out],
        in_specs=[SMEM, SMEM] + [VMEM] * 3,
        out_specs=[VMEM, VMEM],
        compiler_params=PARAMS,
    )(core, order, q, k, v)


def join_kernel(a_ref, b_ref, out_ref):
    out_ref[:, 0] = a_ref[...]
    out_ref[:, 1] = b_ref[...]


def join(mine, other):
    return pl.pallas_call(
        join_kernel,
        out_shape=jax.ShapeDtypeStruct((mine.shape[0], 2, *mine.shape[1:]), BF),
        in_specs=[VMEM] * 2,
        out_specs=VMEM,
        compiler_params=PARAMS,
    )(mine, other)


def temporal_kernel(core_ref, in_ref, out_ref):
    places, cores, _, items, depth = in_ref.shape
    total = places * cores * items
    per = 16
    step = per * cores * items
    inner = out_ref.shape[0] // HT
    k = in_ref[:, :, 1].reshape(total, depth)
    v = in_ref[:, :, 2].reshape(total, depth)
    row_item = lax.broadcasted_iota(jnp.int32, (step, total), 0) % items
    col_item = lax.broadcasted_iota(jnp.int32, (step, total), 1) % items
    same = row_item == col_item
    for at in range(places // per):
        q = in_ref[at * per : (at + 1) * per, :, 0].reshape(step, depth)
        s = jnp.where(same, products(q, k) * score_factor(), -jnp.inf)
        p = jnp.exp2(s - jnp.max(s, axis=1, keepdims=True))
        total_p = jnp.sum(p, axis=1, keepdims=True)
        o = jnp.dot(p.astype(BF), v, preferred_element_type=F32) / total_p
        o = o.astype(BF).reshape(per, cores, items, depth)
        high, low = divmod(at * per, inner)
        for which, core in enumerate((core_ref[0], 1 - core_ref[0])):
            first = (high * cores + core) * inner + low
            out_ref[pl.ds(first, per)] = o[:, which]


def temporal_attend(core, arrived):
    places, cores, _, items, depth = arrived.shape
    return pl.pallas_call(
        temporal_kernel,
        out_shape=jax.ShapeDtypeStruct((places * cores, items, depth), BF),
        in_specs=[SMEM, VMEM],
        out_specs=VMEM,
        compiler_params=PARAMS,
        cost_estimate=estimate(50),
    )(core, arrived)


def row_norm(blocks):
    ones = jnp.ones((DEPTH, LANES), BF)
    best = None
    for block in blocks:
        norms = jnp.dot(block * block, ones, preferred_element_type=F32)
        most = jnp.max(norms.reshape(-1, 8, LANES), axis=0)
        best = most if best is None else jnp.maximum(best, most)
    return jnp.max(best)


def used_slot(frames, base, kb_ref, bc_ref, mine, slot):
    frame = base + mine
    target = lax.rem(base + slot + frames, frames)
    hit = False
    for n in range(NB):
        hit = hit | ((kb_ref[frame, n] == target) & (bc_ref[frame] > n))
    return hit


def score_factor():
    return DEPTH ** (-0.5) * math.log2(math.e)


def products(q, k):
    return lax.dot_general(q, k, (((1,), (1,)), ((), ())), preferred_element_type=F32)


def add_frames(acc, q, pairs):
    for k, v, hit in pairs:
        p = jnp.exp2(products(q, k) * score_factor()).astype(BF)
        weight = jnp.where(hit, 1.0, 0.0).astype(BF)
        wide = jnp.concatenate([v * weight, jnp.full(v.shape, weight)], axis=1)
        add = jnp.dot(p, wide, preferred_element_type=F32)
        acc = add if acc is None else acc + add
    return acc


def fold_frame(q, k, v, acc_ref, m_ref):
    wide = jnp.concatenate([v, jnp.ones_like(v)], axis=1)
    s = products(q, k) * score_factor()
    old = m_ref[...]
    new = jnp.maximum(old, jnp.max(s, axis=1, keepdims=True))
    p = jnp.exp2(s - new[:, :1]).astype(BF)
    alpha = jnp.exp2(old - new)
    both = jnp.concatenate([alpha, alpha], axis=1)
    acc_ref[...] = acc_ref[...] * both + jnp.dot(p, wide, preferred_element_type=F32)
    m_ref[...] = new


def small_scores(q_norm, k_norm):
    factor = score_factor() * 1.02
    return q_norm * k_norm * (factor * factor) <= 1e4


def frame_at(ref, which, at, pieces):
    block = ref[pl.ds(at * pieces, pieces), which]
    return block.reshape(pieces * block.shape[1], DEPTH)


def upper_lanes(rows):
    return lax.broadcasted_iota(jnp.int32, (rows, LANES), 1) >= LANES // 2


def own_kernel(frames, base_ref, kb_ref, bc_ref, in_ref, acc_ref, side_ref, q_ref, stat_ref, both_ref, m_ref):
    pieces = in_ref.shape[0] // BLOCK
    size = pieces * in_ref.shape[2]
    base = base_ref[0]
    part = functools.partial(frame_at, in_ref, pieces=pieces)
    q_ref[...] = in_ref[:, pl.ds(0, 1)]
    q_norm = row_norm([part(0, at) for at in range(BLOCK)])
    k_norm = row_norm([part(1, at) for at in range(BLOCK)])
    fast = small_scores(q_norm, k_norm)
    stat_ref[0] = q_norm
    stat_ref[1] = jnp.where(fast, 1.0, 0.0)

    def used(mine, slot):
        return used_slot(frames, base, kb_ref, bc_ref, mine, slot)

    @pl.when(fast)
    def _():
        def frame(mine, carry):
            pairs = [(part(1, slot), part(2, slot), used(mine, slot)) for slot in range(BLOCK)]
            acc = add_frames(None, part(0, mine), pairs)
            acc_ref[mine] = acc[:, :DEPTH]
            side_ref[mine] = acc[:, DEPTH:]
            return carry

        lax.fori_loop(0, BLOCK, frame, 0)

    @pl.when(jnp.logical_not(fast))
    def _():
        def pair(at, carry):
            mine, slot = at // BLOCK, lax.rem(at, BLOCK)

            @pl.when(slot == 0)
            def _():
                both_ref[...] = jnp.zeros((size, 2 * DEPTH), F32)
                m_ref[...] = jnp.full((size, LANES), -jnp.inf, F32)

            @pl.when(used(mine, slot))
            def _():
                fold_frame(part(0, mine), part(1, slot), part(2, slot), both_ref, m_ref)

            @pl.when(slot == BLOCK - 1)
            def _():
                acc_ref[mine] = both_ref[:, :DEPTH]
                side_ref[mine] = jnp.where(upper_lanes(size), m_ref[...], both_ref[:, DEPTH:])

            return carry

        lax.fori_loop(0, BLOCK * BLOCK, pair, 0)


def near_kernel(
    frames, base_ref, kb_ref, bc_ref, stat_ref, q_ref, less_ref, more_ref, acc_in, side_in, o_ref,
    acc_ref, m_ref, near_ref, sems
):
    pieces = q_ref.shape[0] // BLOCK
    rows = q_ref.shape[2]
    size = pieces * rows
    base = base_ref[0]
    run_copies(
        [
            pltpu.make_async_copy(less_ref, near_ref.at[pl.ds(0, W * pieces)], sems.at[0]),
            pltpu.make_async_copy(more_ref, near_ref.at[pl.ds(W * pieces, W * pieces)], sems.at[1]),
        ]
    )
    part = functools.partial(frame_at, near_ref, pieces=pieces)
    k_norm = row_norm([part(0, at) for at in range(2 * W)])
    fast = small_scores(stat_ref[0], k_norm) & (stat_ref[1] > 0.5)

    def query(mine):
        return frame_at(q_ref, 0, mine, pieces)

    def used(mine, at):
        slot = jnp.where(at < W, at - W, at - W + BLOCK)
        return used_slot(frames, base, kb_ref, bc_ref, mine, slot)

    def finish(mine, acc):
        o = (acc[:, :DEPTH] / acc[:, DEPTH:]).astype(BF)
        o_ref[pl.ds(mine * pieces, pieces)] = o.reshape(pieces, rows, DEPTH)

    @pl.when(fast)
    def _():
        def frame(mine, carry):
            pairs = [
                (part(0, mine + j), part(1, mine + j), used(mine, mine + j)) for j in range(W)
            ]
            acc = jnp.concatenate([acc_in[mine], side_in[mine]], axis=1)
            finish(mine, add_frames(acc, query(mine), pairs))
            return carry

        lax.fori_loop(0, BLOCK, frame, 0)

    @pl.when(jnp.logical_not(fast))
    def _():
        def frame(mine, carry):
            side = side_in[mine]
            quick = jnp.full((size, LANES), stat_ref[1], F32) > 0.5
            top = jnp.broadcast_to(side[:, LANES - 1 :], (size, LANES))
            m_ref[...] = jnp.where(quick, 0.0, top)
            acc_ref[:, :DEPTH] = acc_in[mine]
            acc_ref[:, DEPTH:] = jnp.broadcast_to(side[:, :1], (size, LANES))

            def pair(j, inner):
                @pl.when(used(mine, mine + j))
                def _():
                    fold_frame(query(mine), part(0, mine + j), part(1, mine + j), acc_ref, m_ref)

                return inner

            lax.fori_loop(0, W, pair, 0)
            finish(mine, acc_ref[...])
            return carry

        lax.fori_loop(0, BLOCK, frame, 0)


def attend_own(base, kb, bc, arrived, frames):
    dests, _, rows, depth = arrived.shape
    size = dests // BLOCK * rows
    return pl.pallas_call(
        functools.partial(own_kernel, frames),
        out_shape=[
            jax.ShapeDtypeStruct((BLOCK, size, depth), F32),
            jax.ShapeDtypeStruct((BLOCK, size, LANES), F32),
            jax.ShapeDtypeStruct((dests, 1, rows, depth), BF),
            jax.ShapeDtypeStruct((2,), F32),
        ],
        in_specs=[SMEM] * 3 + [VMEM],
        out_specs=[VMEM, VMEM, VMEM, SMEM],
        scratch_shapes=[pltpu.VMEM((size, 2 * depth), F32), pltpu.VMEM((size, LANES), F32)],
        compiler_params=PARAMS,
        cost_estimate=estimate(10),
    )(base, kb, bc, arrived)


def attend_near(base, kb, bc, stat, q, less, more, sums, frames):
    dests, _, rows, depth = q.shape
    size = dests // BLOCK * rows
    return pl.pallas_call(
        functools.partial(near_kernel, frames),
        out_shape=jax.ShapeDtypeStruct((dests, rows, depth), BF),
        in_specs=[SMEM] * 4 + [VMEM, ANY, ANY, VMEM, VMEM],
        out_specs=VMEM,
        scratch_shapes=[
            pltpu.VMEM((size, 2 * depth), F32),
            pltpu.VMEM((size, LANES), F32),
            pltpu.VMEM((2 * less.shape[0], *less.shape[1:]), BF),
            pltpu.SemaphoreType.DMA((2,)),
        ],
        compiler_params=PARAMS,
    )(base, kb, bc, stat, q, less, more, *sums)


def assemble_kernel(order_ref, t_ref, s_ref, out_ref):
    rows = out_ref.shape[0]
    pieces = t_ref.shape[0] // HT
    for head in range(HT):
        block = t_ref[head * pieces : (head + 1) * pieces].reshape(rows, DEPTH)
        out_ref[:, columns_of(order_ref, head)] = block
    for head in range(s_ref.shape[0]):
        out_ref[:, columns_of(order_ref, HT + head)] = s_ref[head]


def assemble(order, temporal, spatial, rows, width):
    return pl.pallas_call(
        assemble_kernel,
        out_shape=jax.ShapeDtypeStruct((rows, width), BF),
        in_specs=[SMEM, VMEM, VMEM],
        out_specs=VMEM,
        compiler_params=PARAMS,
    )(order, temporal, spatial)


def exchange(array, axes):
    return lax.all_to_all(array, axes, 0, 0, tiled=True)


def from_block(array, by):
    count = lax.axis_size("zh") * lax.axis_size("core") * lax.axis_size("yh")
    return lax.ppermute(array, ("zh", "core", "yh"), [((i + by) % count, i) for i in range(count)])


def local(queries, keys, values, head_order, key_blocks, block_count):
    rows, width = queries.shape
    blocks = lax.axis_size("zh") * lax.axis_size("core") * lax.axis_size("yh")
    frames = blocks * BLOCK
    items = HT * rows // frames
    base = lax.axis_index(("zh", "core", "yh")) * BLOCK
    base = base.astype(jnp.int32).reshape(1)

    block_axes = ("yl", "zl", "x")
    loop_axes = ("zh", "core", "yh", "yl", "zl")
    core = lax.axis_index("core").astype(jnp.int32).reshape(1)
    mine, other = pack_temporal(head_order, core, queries, keys, values, items)
    st = join(mine, lax.ppermute(other, "core", [(0, 1), (1, 0)]))
    qkv = exchange(pack_spatial(head_order, (queries, keys, values)), block_axes)
    pieces = qkv.shape[0] // BLOCK
    less = from_block(qkv[(BLOCK - W) * pieces :, 1:], -1)
    more = from_block(qkv[: W * pieces, 1:], 1)
    qkv, st = lax.optimization_barrier((qkv, st))
    at = exchange(st, ("zh", "yh", "yl", "zl"))
    *sums, q, stat = attend_own(base, key_blocks, block_count, qkv, frames)
    to, stat = lax.optimization_barrier((temporal_attend(core, at), stat))
    tr = exchange(to, loop_axes)
    so = attend_near(base, key_blocks, block_count, stat, q, less, more, sums, frames)
    sr = exchange(so, block_axes)
    return assemble(head_order, tr, sr, rows, width)


def solution(mesh):
    grp, seq = mesh.shape["grp"], mesh.shape["seq"]
    names = ("zh", "core", "yh", "yl", "zl", "x")
    fine = Mesh(mesh.devices.reshape(grp // 2, 2, seq // 16, 2, 2, 4), names)
    tokens = P(names, None)
    return jax.shard_map(
        local,
        mesh=fine,
        in_specs=(tokens, tokens, tokens, P(), P(), P()),
        out_specs=tokens,
        check_vma=False,
    )
```

```python
import functools
import math

import jax
import jax.numpy as jnp
from jax import lax
from jax.experimental import pallas as pl
from jax.experimental.pallas import tpu as pltpu
from jax.sharding import Mesh
from jax.sharding import PartitionSpec as P

HT = 8
W = 3
NB = 6
BLOCK = 4
DEPTH = 128
LANES = 128
BF = jnp.bfloat16
F32 = jnp.float32
VMEM = pl.BlockSpec(memory_space=pltpu.VMEM)
SMEM = pl.BlockSpec(memory_space=pltpu.SMEM)
ANY = pl.BlockSpec(memory_space=pl.ANY)
PARAMS = pltpu.CompilerParams(vmem_limit_bytes=40 * 1024 * 1024)
PACK_PARAMS = pltpu.CompilerParams(vmem_limit_bytes=58 * 1024 * 1024)


def estimate(gigaflops):
    return pl.CostEstimate(flops=gigaflops * 10**9, bytes_accessed=1 << 20, transcendentals=1 << 20)


def columns_of(order_ref, slot):
    return pl.ds(pl.multiple_of(order_ref[slot] * DEPTH, DEPTH), DEPTH)


def run_copies(copies):
    for copy in copies:
        copy.start()
    for copy in copies:
        copy.wait()


def pack_spatial_kernel(order_ref, *refs):
    dst, held, sems, out_sems = refs[-4:]
    heads = range(dst.shape[0])
    inward = [
        [
            pltpu.make_async_copy(
                src.at[:, columns_of(order_ref, HT + head)], held.at[head, which], sems.at[which, head]
            )
            for which, src in enumerate(refs[:-4])
        ]
        for head in heads
    ]
    outward = [pltpu.make_async_copy(held.at[head], dst.at[head], out_sems.at[head]) for head in heads]
    for group in inward:
        for copy in group:
            copy.start()
    for group, out in zip(inward, outward):
        for copy in group:
            copy.wait()
        out.start()
    for out in outward:
        out.wait()


def pack_spatial(order, arrays):
    rows, width = arrays[0].shape
    heads = width // DEPTH - HT
    shape = (heads, len(arrays), rows, DEPTH)
    return pl.pallas_call(
        pack_spatial_kernel,
        out_shape=jax.ShapeDtypeStruct(shape, BF),
        in_specs=[SMEM] + [ANY] * len(arrays),
        out_specs=ANY,
        scratch_shapes=[
            pltpu.VMEM(shape, BF),
            pltpu.SemaphoreType.DMA((len(arrays), heads)),
            pltpu.SemaphoreType.DMA((heads,)),
        ],
        compiler_params=PACK_PARAMS,
    )(order, *arrays)


def pack_temporal_kernel(items, core_ref, order_ref, q_ref, k_ref, v_ref, mine_ref, other_ref):
    pieces = q_ref.shape[0] // items
    for out, core in ((mine_ref, core_ref[0]), (other_ref, 1 - core_ref[0])):
        for which, src in enumerate((q_ref, k_ref, v_ref)):
            for pair in range(HT // 2):
                block = src[:, columns_of(order_ref, 2 * pair + core)]
                out[pair * pieces : (pair + 1) * pieces, which] = block.reshape(pieces, items, DEPTH)


def pack_temporal(order, core, q, k, v, items):
    out = jax.ShapeDtypeStruct((HT // 2 * q.shape[0] // items, 3, items, DEPTH), BF)
    return pl.pallas_call(
        functools.partial(pack_temporal_kernel, items),
        out_shape=[out, out],
        in_specs=[SMEM, SMEM] + [VMEM] * 3,
        out_specs=[VMEM, VMEM],
        compiler_params=PARAMS,
    )(core, order, q, k, v)


def join_kernel(a_ref, b_ref, out_ref):
    out_ref[:, 0] = a_ref[...]
    out_ref[:, 1] = b_ref[...]


def join(mine, other):
    return pl.pallas_call(
        join_kernel,
        out_shape=jax.ShapeDtypeStruct((mine.shape[0], 2, *mine.shape[1:]), BF),
        in_specs=[VMEM] * 2,
        out_specs=VMEM,
        compiler_params=PARAMS,
    )(mine, other)


def temporal_kernel(core_ref, in_ref, out_ref):
    places, cores, _, items, depth = in_ref.shape
    total = places * cores * items
    per = 16
    step = per * cores * items
    inner = out_ref.shape[0] // HT
    k = in_ref[:, :, 1].reshape(total, depth)
    v = in_ref[:, :, 2].reshape(total, depth)
    row_item = lax.broadcasted_iota(jnp.int32, (step, total), 0) % items
    col_item = lax.broadcasted_iota(jnp.int32, (step, total), 1) % items
    same = row_item == col_item
    for at in range(places // per):
        q = in_ref[at * per : (at + 1) * per, :, 0].reshape(step, depth)
        s = jnp.where(same, products(q, k) * score_factor(), -jnp.inf)
        p = jnp.exp2(s - jnp.max(s, axis=1, keepdims=True))
        total_p = jnp.sum(p, axis=1, keepdims=True)
        o = jnp.dot(p.astype(BF), v, preferred_element_type=F32) / total_p
        o = o.astype(BF).reshape(per, cores, items, depth)
        high, low = divmod(at * per, inner)
        for which, core in enumerate((core_ref[0], 1 - core_ref[0])):
            first = (high * cores + core) * inner + low
            out_ref[pl.ds(first, per)] = o[:, which]


def temporal_attend(core, arrived):
    places, cores, _, items, depth = arrived.shape
    return pl.pallas_call(
        temporal_kernel,
        out_shape=jax.ShapeDtypeStruct((places * cores, items, depth), BF),
        in_specs=[SMEM, VMEM],
        out_specs=VMEM,
        compiler_params=PARAMS,
        cost_estimate=estimate(50),
    )(core, arrived)


def row_norm(blocks):
    ones = jnp.ones((DEPTH, LANES), BF)
    best = None
    for block in blocks:
        norms = jnp.dot(block * block, ones, preferred_element_type=F32)
        most = jnp.max(norms.reshape(-1, 8, LANES), axis=0)
        best = most if best is None else jnp.maximum(best, most)
    return jnp.max(best)


def used_slot(frames, base, kb_ref, bc_ref, mine, slot):
    frame = base + mine
    target = lax.rem(base + slot + frames, frames)
    hit = False
    for n in range(NB):
        hit = hit | ((kb_ref[frame, n] == target) & (bc_ref[frame] > n))
    return hit


def score_factor():
    return DEPTH ** (-0.5) * math.log2(math.e)


def products(q, k):
    return lax.dot_general(q, k, (((1,), (1,)), ((), ())), preferred_element_type=F32)


def add_frames(acc, q, pairs):
    for k, v, hit in pairs:
        p = jnp.exp2(products(q, k) * score_factor()).astype(BF)
        weight = jnp.where(hit, 1.0, 0.0).astype(BF)
        wide = jnp.concatenate([v * weight, jnp.full(v.shape, weight)], axis=1)
        add = jnp.dot(p, wide, preferred_element_type=F32)
        acc = add if acc is None else acc + add
    return acc


def fold_frame(q, k, v, acc_ref, m_ref):
    wide = jnp.concatenate([v, jnp.ones_like(v)], axis=1)
    s = products(q, k) * score_factor()
    old = m_ref[...]
    new = jnp.maximum(old, jnp.max(s, axis=1, keepdims=True))
    p = jnp.exp2(s - new[:, :1]).astype(BF)
    alpha = jnp.exp2(old - new)
    both = jnp.concatenate([alpha, alpha], axis=1)
    acc_ref[...] = acc_ref[...] * both + jnp.dot(p, wide, preferred_element_type=F32)
    m_ref[...] = new


def small_scores(q_norm, k_norm):
    factor = score_factor() * 1.02
    return q_norm * k_norm * (factor * factor) <= 1e4


def frame_at(ref, which, at, pieces):
    block = ref[pl.ds(at * pieces, pieces), which]
    return block.reshape(pieces * block.shape[1], DEPTH)


def upper_lanes(rows):
    return lax.broadcasted_iota(jnp.int32, (rows, LANES), 1) >= LANES // 2


def own_kernel(frames, base_ref, kb_ref, bc_ref, in_ref, acc_ref, side_ref, q_ref, stat_ref, both_ref, m_ref):
    pieces = in_ref.shape[0] // BLOCK
    size = pieces * in_ref.shape[2]
    base = base_ref[0]
    part = functools.partial(frame_at, in_ref, pieces=pieces)
    q_ref[...] = in_ref[:, pl.ds(0, 1)]
    q_norm = row_norm([part(0, at) for at in range(BLOCK)])
    k_norm = row_norm([part(1, at) for at in range(BLOCK)])
    fast = small_scores(q_norm, k_norm)
    stat_ref[0] = q_norm
    stat_ref[1] = jnp.where(fast, 1.0, 0.0)

    def used(mine, slot):
        return used_slot(frames, base, kb_ref, bc_ref, mine, slot)

    @pl.when(fast)
    def _():
        def frame(mine, carry):
            pairs = [(part(1, slot), part(2, slot), used(mine, slot)) for slot in range(BLOCK)]
            acc = add_frames(None, part(0, mine), pairs)
            acc_ref[mine] = acc[:, :DEPTH]
            side_ref[mine] = acc[:, DEPTH:]
            return carry

        lax.fori_loop(0, BLOCK, frame, 0)

    @pl.when(jnp.logical_not(fast))
    def _():
        def pair(at, carry):
            mine, slot = at // BLOCK, lax.rem(at, BLOCK)

            @pl.when(slot == 0)
            def _():
                both_ref[...] = jnp.zeros((size, 2 * DEPTH), F32)
                m_ref[...] = jnp.full((size, LANES), -jnp.inf, F32)

            @pl.when(used(mine, slot))
            def _():
                fold_frame(part(0, mine), part(1, slot), part(2, slot), both_ref, m_ref)

            @pl.when(slot == BLOCK - 1)
            def _():
                acc_ref[mine] = both_ref[:, :DEPTH]
                side_ref[mine] = jnp.where(upper_lanes(size), m_ref[...], both_ref[:, DEPTH:])

            return carry

        lax.fori_loop(0, BLOCK * BLOCK, pair, 0)


def near_kernel(
    frames, base_ref, kb_ref, bc_ref, stat_ref, q_ref, less_ref, more_ref, acc_in, side_in, o_ref,
    acc_ref, m_ref, near_ref, sems
):
    pieces = q_ref.shape[0] // BLOCK
    rows = q_ref.shape[2]
    size = pieces * rows
    base = base_ref[0]
    run_copies(
        [
            pltpu.make_async_copy(less_ref, near_ref.at[pl.ds(0, W * pieces)], sems.at[0]),
            pltpu.make_async_copy(more_ref, near_ref.at[pl.ds(W * pieces, W * pieces)], sems.at[1]),
        ]
    )
    part = functools.partial(frame_at, near_ref, pieces=pieces)
    k_norm = row_norm([part(0, at) for at in range(2 * W)])
    fast = small_scores(stat_ref[0], k_norm) & (stat_ref[1] > 0.5)

    def query(mine):
        return frame_at(q_ref, 0, mine, pieces)

    def used(mine, at):
        slot = jnp.where(at < W, at - W, at - W + BLOCK)
        return used_slot(frames, base, kb_ref, bc_ref, mine, slot)

    def finish(mine, acc):
        o = (acc[:, :DEPTH] / acc[:, DEPTH:]).astype(BF)
        o_ref[pl.ds(mine * pieces, pieces)] = o.reshape(pieces, rows, DEPTH)

    @pl.when(fast)
    def _():
        def frame(mine, carry):
            pairs = [
                (part(0, mine + j), part(1, mine + j), used(mine, mine + j)) for j in range(W)
            ]
            acc = jnp.concatenate([acc_in[mine], side_in[mine]], axis=1)
            finish(mine, add_frames(acc, query(mine), pairs))
            return carry

        lax.fori_loop(0, BLOCK, frame, 0)

    @pl.when(jnp.logical_not(fast))
    def _():
        def frame(mine, carry):
            side = side_in[mine]
            quick = jnp.full((size, LANES), stat_ref[1], F32) > 0.5
            top = jnp.broadcast_to(side[:, LANES - 1 :], (size, LANES))
            m_ref[...] = jnp.where(quick, 0.0, top)
            acc_ref[:, :DEPTH] = acc_in[mine]
            acc_ref[:, DEPTH:] = jnp.broadcast_to(side[:, :1], (size, LANES))

            def pair(j, inner):
                @pl.when(used(mine, mine + j))
                def _():
                    fold_frame(query(mine), part(0, mine + j), part(1, mine + j), acc_ref, m_ref)

                return inner

            lax.fori_loop(0, W, pair, 0)
            finish(mine, acc_ref[...])
            return carry

        lax.fori_loop(0, BLOCK, frame, 0)


def attend_own(base, kb, bc, arrived, frames):
    dests, _, rows, depth = arrived.shape
    size = dests // BLOCK * rows
    return pl.pallas_call(
        functools.partial(own_kernel, frames),
        out_shape=[
            jax.ShapeDtypeStruct((BLOCK, size, depth), F32),
            jax.ShapeDtypeStruct((BLOCK, size, LANES), F32),
            jax.ShapeDtypeStruct((dests, 1, rows, depth), BF),
            jax.ShapeDtypeStruct((2,), F32),
        ],
        in_specs=[SMEM] * 3 + [VMEM],
        out_specs=[VMEM, VMEM, VMEM, SMEM],
        scratch_shapes=[pltpu.VMEM((size, 2 * depth), F32), pltpu.VMEM((size, LANES), F32)],
        compiler_params=PARAMS,
        cost_estimate=estimate(10),
    )(base, kb, bc, arrived)


def attend_near(base, kb, bc, stat, q, less, more, sums, frames):
    dests, _, rows, depth = q.shape
    size = dests // BLOCK * rows
    return pl.pallas_call(
        functools.partial(near_kernel, frames),
        out_shape=jax.ShapeDtypeStruct((dests, rows, depth), BF),
        in_specs=[SMEM] * 4 + [VMEM, ANY, ANY, VMEM, VMEM],
        out_specs=VMEM,
        scratch_shapes=[
            pltpu.VMEM((size, 2 * depth), F32),
            pltpu.VMEM((size, LANES), F32),
            pltpu.VMEM((2 * less.shape[0], *less.shape[1:]), BF),
            pltpu.SemaphoreType.DMA((2,)),
        ],
        compiler_params=PARAMS,
    )(base, kb, bc, stat, q, less, more, *sums)


def place_kernel(first, order_ref, src_ref, *refs):
    out, sems = refs[-2:]
    run_copies(
        [
            pltpu.make_async_copy(
                src_ref.at[head], out.at[:, :, columns_of(order_ref, first + head)], sems.at[head]
            )
            for head in range(src_ref.shape[0])
        ]
    )


def place(order, blocks, first, rows, width, before=()):
    heads, pieces, items, _ = blocks.shape
    return pl.pallas_call(
        functools.partial(place_kernel, first),
        out_shape=jax.ShapeDtypeStruct((pieces, items, width), BF),
        in_specs=[SMEM, VMEM] + [ANY] * len(before),
        out_specs=ANY,
        scratch_shapes=[pltpu.SemaphoreType.DMA((heads,))],
        input_output_aliases={2: 0} if before else {},
        compiler_params=PARAMS if before else PACK_PARAMS,
    )(order, blocks, *before)


def exchange(array, axes):
    return lax.all_to_all(array, axes, 0, 0, tiled=True)


def from_block(array, by):
    count = lax.axis_size("zh") * lax.axis_size("core") * lax.axis_size("yh")
    return lax.ppermute(array, ("zh", "core", "yh"), [((i + by) % count, i) for i in range(count)])


def local(queries, keys, values, head_order, key_blocks, block_count):
    rows, width = queries.shape
    blocks = lax.axis_size("zh") * lax.axis_size("core") * lax.axis_size("yh")
    frames = blocks * BLOCK
    items = HT * rows // frames
    base = lax.axis_index(("zh", "core", "yh")) * BLOCK
    base = base.astype(jnp.int32).reshape(1)

    block_axes = ("yl", "zl", "x")
    loop_axes = ("zh", "core", "yh", "yl", "zl")
    core = lax.axis_index("core").astype(jnp.int32).reshape(1)
    mine, other = pack_temporal(head_order, core, queries, keys, values, items)
    st = join(mine, lax.ppermute(other, "core", [(0, 1), (1, 0)]))
    qkv = exchange(pack_spatial(head_order, (queries, keys, values)), block_axes)
    pieces = qkv.shape[0] // BLOCK
    less = from_block(qkv[(BLOCK - W) * pieces :, 1:], -1)
    more = from_block(qkv[: W * pieces, 1:], 1)
    qkv, st = lax.optimization_barrier((qkv, st))
    at = exchange(st, ("zh", "yh", "yl", "zl"))
    *sums, q, stat = attend_own(base, key_blocks, block_count, qkv, frames)
    to, stat = lax.optimization_barrier((temporal_attend(core, at), stat))
    tr = exchange(to, loop_axes)
    so = attend_near(base, key_blocks, block_count, stat, q, less, more, sums, frames)
    sr = exchange(so, block_axes)
    by_head = (-1, rows // items, items, DEPTH)
    partial = place(head_order, tr.reshape(by_head), 0, rows, width)
    whole = place(head_order, sr.reshape(by_head), HT, rows, width, (partial,))
    return whole.reshape(rows, width)


def solution(mesh):
    grp, seq = mesh.shape["grp"], mesh.shape["seq"]
    names = ("zh", "core", "yh", "yl", "zl", "x")
    fine = Mesh(mesh.devices.reshape(grp // 2, 2, seq // 16, 2, 2, 4), names)
    tokens = P(names, None)
    return jax.shard_map(
        local,
        mesh=fine,
        in_specs=(tokens, tokens, tokens, P(), P(), P()),
        out_specs=tokens,
        check_vma=False,
    )
```

```python
import functools
import math

import jax
import jax.numpy as jnp
from jax import lax
from jax.experimental import pallas as pl
from jax.experimental.pallas import tpu as pltpu
from jax.sharding import Mesh
from jax.sharding import PartitionSpec as P

HT = 8
W = 3
NB = 6
BLOCK = 4
DEPTH = 128
LANES = 128
BF = jnp.bfloat16
F32 = jnp.float32
VMEM = pl.BlockSpec(memory_space=pltpu.VMEM)
SMEM = pl.BlockSpec(memory_space=pltpu.SMEM)
ANY = pl.BlockSpec(memory_space=pl.ANY)
PARAMS = pltpu.CompilerParams(vmem_limit_bytes=40 * 1024 * 1024)
PACK_PARAMS = pltpu.CompilerParams(vmem_limit_bytes=58 * 1024 * 1024)


def estimate(gigaflops):
    return pl.CostEstimate(flops=gigaflops * 10**9, bytes_accessed=1 << 20, transcendentals=1 << 20)


def columns_of(order_ref, slot):
    return pl.ds(pl.multiple_of(order_ref[slot] * DEPTH, DEPTH), DEPTH)


def run_copies(copies):
    for copy in copies:
        copy.start()
    for copy in copies:
        copy.wait()


def pack_spatial_kernel(order_ref, *refs):
    dst, held, sems, out_sems = refs[-4:]
    heads = range(dst.shape[0])
    inward = [
        [
            pltpu.make_async_copy(
                src.at[:, columns_of(order_ref, HT + head)], held.at[head, which], sems.at[which, head]
            )
            for which, src in enumerate(refs[:-4])
        ]
        for head in heads
    ]
    outward = [pltpu.make_async_copy(held.at[head], dst.at[head], out_sems.at[head]) for head in heads]
    for group in inward:
        for copy in group:
            copy.start()
    for group, out in zip(inward, outward):
        for copy in group:
            copy.wait()
        out.start()
    for out in outward:
        out.wait()


def pack_spatial(order, arrays):
    rows, width = arrays[0].shape
    heads = width // DEPTH - HT
    shape = (heads, len(arrays), rows, DEPTH)
    return pl.pallas_call(
        pack_spatial_kernel,
        out_shape=jax.ShapeDtypeStruct(shape, BF),
        in_specs=[SMEM] + [ANY] * len(arrays),
        out_specs=ANY,
        scratch_shapes=[
            pltpu.VMEM(shape, BF),
            pltpu.SemaphoreType.DMA((len(arrays), heads)),
            pltpu.SemaphoreType.DMA((heads,)),
        ],
        compiler_params=PACK_PARAMS,
    )(order, *arrays)


def pack_temporal_kernel(items, core_ref, order_ref, q_ref, k_ref, v_ref, mine_ref, other_ref):
    pieces = q_ref.shape[0] // items
    for out, core in ((mine_ref, core_ref[0]), (other_ref, 1 - core_ref[0])):
        for which, src in enumerate((q_ref, k_ref, v_ref)):
            for pair in range(HT // 2):
                block = src[:, columns_of(order_ref, 2 * pair + core)]
                out[pair * pieces : (pair + 1) * pieces, which] = block.reshape(pieces, items, DEPTH)


def pack_temporal(order, core, q, k, v, items):
    out = jax.ShapeDtypeStruct((HT // 2 * q.shape[0] // items, 3, items, DEPTH), BF)
    return pl.pallas_call(
        functools.partial(pack_temporal_kernel, items),
        out_shape=[out, out],
        in_specs=[SMEM, SMEM] + [VMEM] * 3,
        out_specs=[VMEM, VMEM],
        compiler_params=PARAMS,
    )(core, order, q, k, v)


def join_kernel(a_ref, b_ref, out_ref):
    out_ref[:, 0] = a_ref[...]
    out_ref[:, 1] = b_ref[...]


def join(mine, other):
    return pl.pallas_call(
        join_kernel,
        out_shape=jax.ShapeDtypeStruct((mine.shape[0], 2, *mine.shape[1:]), BF),
        in_specs=[VMEM] * 2,
        out_specs=VMEM,
        compiler_params=PARAMS,
    )(mine, other)


def temporal_kernel(core_ref, in_ref, out_ref):
    places, cores, _, items, depth = in_ref.shape
    total = places * cores * items
    per = 16
    step = per * cores * items
    inner = out_ref.shape[0] // HT
    k = in_ref[:, :, 1].reshape(total, depth)
    v = in_ref[:, :, 2].reshape(total, depth)
    row_item = lax.broadcasted_iota(jnp.int32, (step, total), 0) % items
    col_item = lax.broadcasted_iota(jnp.int32, (step, total), 1) % items
    same = row_item == col_item
    for at in range(places // per):
        q = in_ref[at * per : (at + 1) * per, :, 0].reshape(step, depth)
        s = jnp.where(same, products(q, k) * score_factor(), -jnp.inf)
        p = jnp.exp2(s - jnp.max(s, axis=1, keepdims=True))
        total_p = jnp.sum(p, axis=1, keepdims=True)
        o = jnp.dot(p.astype(BF), v, preferred_element_type=F32) / total_p
        o = o.astype(BF).reshape(per, cores, items, depth)
        high, low = divmod(at * per, inner)
        for which, core in enumerate((core_ref[0], 1 - core_ref[0])):
            first = (high * cores + core) * inner + low
            out_ref[pl.ds(first, per)] = o[:, which]


def temporal_attend(core, arrived):
    places, cores, _, items, depth = arrived.shape
    return pl.pallas_call(
        temporal_kernel,
        out_shape=jax.ShapeDtypeStruct((places * cores, items, depth), BF),
        in_specs=[SMEM, VMEM],
        out_specs=VMEM,
        compiler_params=PARAMS,
        cost_estimate=estimate(50),
    )(core, arrived)


def row_norm(blocks):
    ones = jnp.ones((DEPTH, LANES), BF)
    best = None
    for block in blocks:
        norms = jnp.dot(block * block, ones, preferred_element_type=F32)
        most = jnp.max(norms.reshape(-1, 8, LANES), axis=0)
        best = most if best is None else jnp.maximum(best, most)
    return jnp.max(best)


def used_slot(frames, base, kb_ref, bc_ref, mine, slot):
    frame = base + mine
    target = lax.rem(base + slot + frames, frames)
    hit = False
    for n in range(NB):
        hit = hit | ((kb_ref[frame, n] == target) & (bc_ref[frame] > n))
    return hit


def score_factor():
    return DEPTH ** (-0.5) * math.log2(math.e)


def products(q, k):
    return lax.dot_general(q, k, (((1,), (1,)), ((), ())), preferred_element_type=F32)


def add_frames(acc, q, pairs):
    for k, v, hit in pairs:
        p = jnp.exp2(products(q, k) * score_factor()).astype(BF)
        weight = jnp.where(hit, 1.0, 0.0).astype(BF)
        wide = jnp.concatenate([v * weight, jnp.full(v.shape, weight)], axis=1)
        add = jnp.dot(p, wide, preferred_element_type=F32)
        acc = add if acc is None else acc + add
    return acc


def fold_frame(q, k, v, acc_ref, m_ref):
    wide = jnp.concatenate([v, jnp.ones_like(v)], axis=1)
    s = products(q, k) * score_factor()
    old = m_ref[...]
    new = jnp.maximum(old, jnp.max(s, axis=1, keepdims=True))
    p = jnp.exp2(s - new[:, :1]).astype(BF)
    alpha = jnp.exp2(old - new)
    both = jnp.concatenate([alpha, alpha], axis=1)
    acc_ref[...] = acc_ref[...] * both + jnp.dot(p, wide, preferred_element_type=F32)
    m_ref[...] = new


def small_scores(q_norm, k_norm):
    factor = score_factor() * 1.02
    return q_norm * k_norm * (factor * factor) <= 1e4


def frame_at(ref, which, at, pieces):
    block = ref[pl.ds(at * pieces, pieces), which]
    return block.reshape(pieces * block.shape[1], DEPTH)


def upper_lanes(rows):
    return lax.broadcasted_iota(jnp.int32, (rows, LANES), 1) >= LANES // 2


def own_kernel(frames, base_ref, kb_ref, bc_ref, in_ref, acc_ref, side_ref, q_ref, stat_ref, both_ref, m_ref):
    pieces = in_ref.shape[0] // BLOCK
    size = pieces * in_ref.shape[2]
    base = base_ref[0]
    part = functools.partial(frame_at, in_ref, pieces=pieces)
    q_ref[...] = in_ref[:, pl.ds(0, 1)]
    q_norm = row_norm([part(0, at) for at in range(BLOCK)])
    k_norm = row_norm([part(1, at) for at in range(BLOCK)])
    fast = small_scores(q_norm, k_norm)
    stat_ref[0] = q_norm
    stat_ref[1] = jnp.where(fast, 1.0, 0.0)

    def used(mine, slot):
        return used_slot(frames, base, kb_ref, bc_ref, mine, slot)

    @pl.when(fast)
    def _():
        def frame(mine, carry):
            pairs = [(part(1, slot), part(2, slot), used(mine, slot)) for slot in range(BLOCK)]
            acc = add_frames(None, part(0, mine), pairs)
            acc_ref[mine] = acc[:, :DEPTH]
            side_ref[mine] = acc[:, DEPTH:]
            return carry

        lax.fori_loop(0, BLOCK, frame, 0)

    @pl.when(jnp.logical_not(fast))
    def _():
        def pair(at, carry):
            mine, slot = at // BLOCK, lax.rem(at, BLOCK)

            @pl.when(slot == 0)
            def _():
                both_ref[...] = jnp.zeros((size, 2 * DEPTH), F32)
                m_ref[...] = jnp.full((size, LANES), -jnp.inf, F32)

            @pl.when(used(mine, slot))
            def _():
                fold_frame(part(0, mine), part(1, slot), part(2, slot), both_ref, m_ref)

            @pl.when(slot == BLOCK - 1)
            def _():
                acc_ref[mine] = both_ref[:, :DEPTH]
                side_ref[mine] = jnp.where(upper_lanes(size), m_ref[...], both_ref[:, DEPTH:])

            return carry

        lax.fori_loop(0, BLOCK * BLOCK, pair, 0)


def near_kernel(
    frames, base_ref, kb_ref, bc_ref, stat_ref, q_ref, less_ref, more_ref, acc_in, side_in, o_ref,
    acc_ref, m_ref, near_ref, held_ref, sems, held_sems
):
    pieces = q_ref.shape[0] // BLOCK
    rows = q_ref.shape[2]
    size = pieces * rows
    base = base_ref[0]
    arriving = [
        pltpu.make_async_copy(src, near_ref.at[pl.ds(at * W * pieces, W * pieces)], sems.at[at])
        for at, src in enumerate((less_ref, more_ref))
    ]
    holding = [
        pltpu.make_async_copy(src, held_ref.at[:, :, pl.ds(at * LANES, LANES)], held_sems.at[at])
        for at, src in enumerate((acc_in, side_in))
    ]
    for copy in arriving + holding:
        copy.start()
    part = functools.partial(frame_at, near_ref, pieces=pieces)
    arriving[0].wait()
    less_norm = row_norm([part(0, at) for at in range(W)])
    arriving[1].wait()
    k_norm = jnp.maximum(less_norm, row_norm([part(0, at) for at in range(W, 2 * W)]))
    fast = small_scores(stat_ref[0], k_norm) & (stat_ref[1] > 0.5)
    for copy in holding:
        copy.wait()

    def query(mine):
        return frame_at(q_ref, 0, mine, pieces)

    def used(mine, at):
        slot = jnp.where(at < W, at - W, at - W + BLOCK)
        return used_slot(frames, base, kb_ref, bc_ref, mine, slot)

    def finish(mine, acc):
        o = (acc[:, :DEPTH] / acc[:, DEPTH:]).astype(BF)
        o_ref[pl.ds(mine * pieces, pieces)] = o.reshape(pieces, rows, DEPTH)

    @pl.when(fast)
    def _():
        def frame(mine, carry):
            pairs = [
                (part(0, mine + j), part(1, mine + j), used(mine, mine + j)) for j in range(W)
            ]
            finish(mine, add_frames(held_ref[mine], query(mine), pairs))
            return carry

        lax.fori_loop(0, BLOCK, frame, 0)

    @pl.when(jnp.logical_not(fast))
    def _():
        def frame(mine, carry):
            side = held_ref[mine, :, LANES:]
            quick = jnp.full((size, LANES), stat_ref[1], F32) > 0.5
            top = jnp.broadcast_to(side[:, LANES - 1 :], (size, LANES))
            m_ref[...] = jnp.where(quick, 0.0, top)
            acc_ref[:, :DEPTH] = held_ref[mine, :, :LANES]
            acc_ref[:, DEPTH:] = jnp.broadcast_to(side[:, :1], (size, LANES))

            def pair(j, inner):
                @pl.when(used(mine, mine + j))
                def _():
                    fold_frame(query(mine), part(0, mine + j), part(1, mine + j), acc_ref, m_ref)

                return inner

            lax.fori_loop(0, W, pair, 0)
            finish(mine, acc_ref[...])
            return carry

        lax.fori_loop(0, BLOCK, frame, 0)


def attend_own(base, kb, bc, arrived, frames):
    dests, _, rows, depth = arrived.shape
    size = dests // BLOCK * rows
    return pl.pallas_call(
        functools.partial(own_kernel, frames),
        out_shape=[
            jax.ShapeDtypeStruct((BLOCK, size, depth), F32),
            jax.ShapeDtypeStruct((BLOCK, size, LANES), F32),
            jax.ShapeDtypeStruct((dests, 1, rows, depth), BF),
            jax.ShapeDtypeStruct((2,), F32),
        ],
        in_specs=[SMEM] * 3 + [VMEM],
        out_specs=[VMEM, VMEM, VMEM, SMEM],
        scratch_shapes=[pltpu.VMEM((size, 2 * depth), F32), pltpu.VMEM((size, LANES), F32)],
        compiler_params=PARAMS,
        cost_estimate=estimate(10),
    )(base, kb, bc, arrived)


def attend_near(base, kb, bc, stat, q, less, more, sums, frames):
    dests, _, rows, depth = q.shape
    size = dests // BLOCK * rows
    return pl.pallas_call(
        functools.partial(near_kernel, frames),
        out_shape=jax.ShapeDtypeStruct((dests, rows, depth), BF),
        in_specs=[SMEM] * 4 + [VMEM] + [ANY] * 4,
        out_specs=VMEM,
        scratch_shapes=[
            pltpu.VMEM((size, 2 * depth), F32),
            pltpu.VMEM((size, LANES), F32),
            pltpu.VMEM((2 * less.shape[0], *less.shape[1:]), BF),
            pltpu.VMEM((BLOCK, size, 2 * LANES), F32),
            pltpu.SemaphoreType.DMA((2,)),
            pltpu.SemaphoreType.DMA((2,)),
        ],
        compiler_params=PARAMS,
    )(base, kb, bc, stat, q, less, more, *sums)


def place_kernel(first, order_ref, src_ref, *refs):
    out, sems = refs[-2:]
    run_copies(
        [
            pltpu.make_async_copy(
                src_ref.at[head], out.at[:, :, columns_of(order_ref, first + head)], sems.at[head]
            )
            for head in range(src_ref.shape[0])
        ]
    )


def place(order, blocks, first, rows, width, before=()):
    heads, pieces, items, _ = blocks.shape
    return pl.pallas_call(
        functools.partial(place_kernel, first),
        out_shape=jax.ShapeDtypeStruct((pieces, items, width), BF),
        in_specs=[SMEM, VMEM] + [ANY] * len(before),
        out_specs=ANY,
        scratch_shapes=[pltpu.SemaphoreType.DMA((heads,))],
        input_output_aliases={2: 0} if before else {},
        compiler_params=PARAMS if before else PACK_PARAMS,
    )(order, blocks, *before)


def exchange(array, axes):
    return lax.all_to_all(array, axes, 0, 0, tiled=True)


def from_block(array, by):
    count = lax.axis_size("zh") * lax.axis_size("core") * lax.axis_size("yh")
    return lax.ppermute(array, ("zh", "core", "yh"), [((i + by) % count, i) for i in range(count)])


def local(queries, keys, values, head_order, key_blocks, block_count):
    rows, width = queries.shape
    blocks = lax.axis_size("zh") * lax.axis_size("core") * lax.axis_size("yh")
    frames = blocks * BLOCK
    items = HT * rows // frames
    base = lax.axis_index(("zh", "core", "yh")) * BLOCK
    base = base.astype(jnp.int32).reshape(1)

    block_axes = ("yl", "zl", "x")
    loop_axes = ("zh", "core", "yh", "yl", "zl")
    core = lax.axis_index("core").astype(jnp.int32).reshape(1)
    mine, other = pack_temporal(head_order, core, queries, keys, values, items)
    st = join(mine, lax.ppermute(other, "core", [(0, 1), (1, 0)]))
    qkv = exchange(pack_spatial(head_order, (queries, keys, values)), block_axes)
    pieces = qkv.shape[0] // BLOCK
    less = from_block(qkv[(BLOCK - W) * pieces :, 1:], -1)
    more = from_block(qkv[: W * pieces, 1:], 1)
    qkv, st = lax.optimization_barrier((qkv, st))
    at = exchange(st, ("zh", "yh", "yl", "zl"))
    *sums, q, stat = attend_own(base, key_blocks, block_count, qkv, frames)
    to, stat = lax.optimization_barrier((temporal_attend(core, at), stat))
    tr = exchange(to, loop_axes)
    so = attend_near(base, key_blocks, block_count, stat, q, less, more, sums, frames)
    sr = exchange(so, block_axes)
    by_head = (-1, rows // items, items, DEPTH)
    partial = place(head_order, tr.reshape(by_head), 0, rows, width)
    whole = place(head_order, sr.reshape(by_head), HT, rows, width, (partial,))
    return whole.reshape(rows, width)


def solution(mesh):
    grp, seq = mesh.shape["grp"], mesh.shape["seq"]
    names = ("zh", "core", "yh", "yl", "zl", "x")
    fine = Mesh(mesh.devices.reshape(grp // 2, 2, seq // 16, 2, 2, 4), names)
    tokens = P(names, None)
    return jax.shard_map(
        local,
        mesh=fine,
        in_specs=(tokens, tokens, tokens, P(), P(), P()),
        out_specs=tokens,
        check_vma=False,
    )
```

```python
import functools
import math

import jax
import jax.numpy as jnp
from jax import lax
from jax.experimental import pallas as pl
from jax.experimental.pallas import tpu as pltpu
from jax.sharding import Mesh
from jax.sharding import PartitionSpec as P

HT = 8
W = 3
NB = 6
BLOCK = 4
DEPTH = 128
LANES = 128
BF = jnp.bfloat16
F32 = jnp.float32
VMEM = pl.BlockSpec(memory_space=pltpu.VMEM)
SMEM = pl.BlockSpec(memory_space=pltpu.SMEM)
ANY = pl.BlockSpec(memory_space=pl.ANY)
PARAMS = pltpu.CompilerParams(vmem_limit_bytes=40 * 1024 * 1024)
PACK_PARAMS = pltpu.CompilerParams(vmem_limit_bytes=58 * 1024 * 1024)


def estimate(gigaflops):
    return pl.CostEstimate(flops=gigaflops * 10**9, bytes_accessed=1 << 20, transcendentals=1 << 20)


def columns_of(order_ref, slot):
    return pl.ds(pl.multiple_of(order_ref[slot] * DEPTH, DEPTH), DEPTH)


def run_copies(copies):
    for copy in copies:
        copy.start()
    for copy in copies:
        copy.wait()


def pack_spatial_kernel(order_ref, *refs):
    dst, held, sems, out_sems = refs[-4:]
    heads = range(dst.shape[0])
    inward = [
        [
            pltpu.make_async_copy(
                src.at[:, columns_of(order_ref, HT + head)], held.at[head, which], sems.at[which, head]
            )
            for which, src in enumerate(refs[:-4])
        ]
        for head in heads
    ]
    outward = [pltpu.make_async_copy(held.at[head], dst.at[head], out_sems.at[head]) for head in heads]
    for group in inward:
        for copy in group:
            copy.start()
    for group, out in zip(inward, outward):
        for copy in group:
            copy.wait()
        out.start()
    for out in outward:
        out.wait()


def pack_spatial(order, arrays):
    rows, width = arrays[0].shape
    heads = width // DEPTH - HT
    shape = (heads, len(arrays), rows, DEPTH)
    return pl.pallas_call(
        pack_spatial_kernel,
        out_shape=jax.ShapeDtypeStruct(shape, BF),
        in_specs=[SMEM] + [ANY] * len(arrays),
        out_specs=ANY,
        scratch_shapes=[
            pltpu.VMEM(shape, BF),
            pltpu.SemaphoreType.DMA((len(arrays), heads)),
            pltpu.SemaphoreType.DMA((heads,)),
        ],
        compiler_params=PACK_PARAMS,
    )(order, *arrays)


def pack_temporal_kernel(items, core_ref, order_ref, q_ref, k_ref, v_ref, mine_ref, other_ref):
    pieces = q_ref.shape[0] // items
    for out, core in ((mine_ref, core_ref[0]), (other_ref, 1 - core_ref[0])):
        for which, src in enumerate((q_ref, k_ref, v_ref)):
            for pair in range(HT // 2):
                block = src[:, columns_of(order_ref, 2 * pair + core)]
                out[pair * pieces : (pair + 1) * pieces, which] = block.reshape(pieces, items, DEPTH)


def pack_temporal(order, core, q, k, v, items):
    out = jax.ShapeDtypeStruct((HT // 2 * q.shape[0] // items, 3, items, DEPTH), BF)
    return pl.pallas_call(
        functools.partial(pack_temporal_kernel, items),
        out_shape=[out, out],
        in_specs=[SMEM, SMEM] + [VMEM] * 3,
        out_specs=[VMEM, VMEM],
        compiler_params=PARAMS,
    )(core, order, q, k, v)


def join_kernel(a_ref, b_ref, out_ref):
    out_ref[:, 0] = a_ref[...]
    out_ref[:, 1] = b_ref[...]


def join(mine, other):
    return pl.pallas_call(
        join_kernel,
        out_shape=jax.ShapeDtypeStruct((mine.shape[0], 2, *mine.shape[1:]), BF),
        in_specs=[VMEM] * 2,
        out_specs=VMEM,
        compiler_params=PARAMS,
    )(mine, other)


def temporal_kernel(core_ref, in_ref, out_ref):
    places, cores, _, items, depth = in_ref.shape
    total = places * cores * items
    per = 16
    step = per * cores * items
    inner = out_ref.shape[0] // HT
    k = in_ref[:, :, 1].reshape(total, depth)
    v = in_ref[:, :, 2].reshape(total, depth)
    row_item = lax.broadcasted_iota(jnp.int32, (step, total), 0) % items
    col_item = lax.broadcasted_iota(jnp.int32, (step, total), 1) % items
    same = row_item == col_item
    for at in range(places // per):
        q = in_ref[at * per : (at + 1) * per, :, 0].reshape(step, depth)
        s = jnp.where(same, products(q, k) * score_factor(), -jnp.inf)
        p = jnp.exp2(s - jnp.max(s, axis=1, keepdims=True))
        total_p = jnp.sum(p, axis=1, keepdims=True)
        o = jnp.dot(p.astype(BF), v, preferred_element_type=F32) / total_p
        o = o.astype(BF).reshape(per, cores, items, depth)
        high, low = divmod(at * per, inner)
        for which, core in enumerate((core_ref[0], 1 - core_ref[0])):
            first = (high * cores + core) * inner + low
            out_ref[pl.ds(first, per)] = o[:, which]


def temporal_attend(core, arrived):
    places, cores, _, items, depth = arrived.shape
    return pl.pallas_call(
        temporal_kernel,
        out_shape=jax.ShapeDtypeStruct((places * cores, items, depth), BF),
        in_specs=[SMEM, VMEM],
        out_specs=VMEM,
        compiler_params=PARAMS,
        cost_estimate=estimate(50),
    )(core, arrived)


def row_norm(blocks):
    ones = jnp.ones((DEPTH, LANES), BF)
    best = None
    for block in blocks:
        norms = jnp.dot(block * block, ones, preferred_element_type=F32)
        most = jnp.max(norms.reshape(-1, 8, LANES), axis=0)
        best = most if best is None else jnp.maximum(best, most)
    return jnp.max(best)


def used_slot(frames, base, kb_ref, bc_ref, mine, slot):
    frame = base + mine
    target = lax.rem(base + slot + frames, frames)
    hit = False
    for n in range(NB):
        hit = hit | ((kb_ref[frame, n] == target) & (bc_ref[frame] > n))
    return hit


def score_factor():
    return DEPTH ** (-0.5) * math.log2(math.e)


def products(q, k):
    return lax.dot_general(q, k, (((1,), (1,)), ((), ())), preferred_element_type=F32)


def add_frames(acc, q, pairs):
    for k, v, hit in pairs:
        p = jnp.exp2(products(q, k) * score_factor()).astype(BF)
        weight = jnp.where(hit, 1.0, 0.0).astype(BF)
        wide = jnp.concatenate([v * weight, jnp.full(v.shape, weight)], axis=1)
        add = jnp.dot(p, wide, preferred_element_type=F32)
        acc = add if acc is None else acc + add
    return acc


def fold_frame(q, k, v, acc_ref, m_ref):
    wide = jnp.concatenate([v, jnp.ones_like(v)], axis=1)
    s = products(q, k) * score_factor()
    old = m_ref[...]
    new = jnp.maximum(old, jnp.max(s, axis=1, keepdims=True))
    p = jnp.exp2(s - new[:, :1]).astype(BF)
    alpha = jnp.exp2(old - new)
    both = jnp.concatenate([alpha, alpha], axis=1)
    acc_ref[...] = acc_ref[...] * both + jnp.dot(p, wide, preferred_element_type=F32)
    m_ref[...] = new


def small_scores(q_norm, k_norm):
    factor = score_factor() * 1.02
    return q_norm * k_norm * (factor * factor) <= 1e4


def frame_at(ref, which, at, pieces):
    block = ref[pl.ds(at * pieces, pieces), which]
    return block.reshape(pieces * block.shape[1], DEPTH)


def upper_lanes(rows):
    return lax.broadcasted_iota(jnp.int32, (rows, LANES), 1) >= LANES // 2


def own_kernel(frames, base_ref, kb_ref, bc_ref, in_ref, acc_ref, side_ref, q_ref, stat_ref, both_ref, m_ref):
    pieces = in_ref.shape[0] // BLOCK
    size = pieces * in_ref.shape[2]
    base = base_ref[0]
    part = functools.partial(frame_at, in_ref, pieces=pieces)
    q_ref[...] = in_ref[:, pl.ds(0, 1)]
    q_norm = row_norm([part(0, at) for at in range(BLOCK)])
    k_norm = row_norm([part(1, at) for at in range(BLOCK)])
    fast = small_scores(q_norm, k_norm)
    stat_ref[0] = q_norm
    stat_ref[1] = jnp.where(fast, 1.0, 0.0)

    def used(mine, slot):
        return used_slot(frames, base, kb_ref, bc_ref, mine, slot)

    @pl.when(fast)
    def _():
        def frame(mine, carry):
            pairs = [(part(1, slot), part(2, slot), used(mine, slot)) for slot in range(BLOCK)]
            acc = add_frames(None, part(0, mine), pairs)
            acc_ref[mine] = acc[:, :DEPTH]
            side_ref[mine] = acc[:, DEPTH:]
            return carry

        lax.fori_loop(0, BLOCK, frame, 0)

    @pl.when(jnp.logical_not(fast))
    def _():
        def pair(at, carry):
            mine, slot = at // BLOCK, lax.rem(at, BLOCK)

            @pl.when(slot == 0)
            def _():
                both_ref[...] = jnp.zeros((size, 2 * DEPTH), F32)
                m_ref[...] = jnp.full((size, LANES), -jnp.inf, F32)

            @pl.when(used(mine, slot))
            def _():
                fold_frame(part(0, mine), part(1, slot), part(2, slot), both_ref, m_ref)

            @pl.when(slot == BLOCK - 1)
            def _():
                acc_ref[mine] = both_ref[:, :DEPTH]
                side_ref[mine] = jnp.where(upper_lanes(size), m_ref[...], both_ref[:, DEPTH:])

            return carry

        lax.fori_loop(0, BLOCK * BLOCK, pair, 0)


def near_kernel(
    frames, base_ref, kb_ref, bc_ref, stat_ref, q_ref, less_ref, more_ref, acc_in, side_in, o_ref,
    acc_ref, m_ref, near_ref, sems
):
    pieces = q_ref.shape[0] // BLOCK
    rows = q_ref.shape[2]
    size = pieces * rows
    base = base_ref[0]
    run_copies(
        [
            pltpu.make_async_copy(less_ref, near_ref.at[pl.ds(0, W * pieces)], sems.at[0]),
            pltpu.make_async_copy(more_ref, near_ref.at[pl.ds(W * pieces, W * pieces)], sems.at[1]),
        ]
    )
    part = functools.partial(frame_at, near_ref, pieces=pieces)
    k_norm = row_norm([part(0, at) for at in range(2 * W)])
    fast = small_scores(stat_ref[0], k_norm) & (stat_ref[1] > 0.5)

    def query(mine):
        return frame_at(q_ref, 0, mine, pieces)

    def used(mine, at):
        slot = jnp.where(at < W, at - W, at - W + BLOCK)
        return used_slot(frames, base, kb_ref, bc_ref, mine, slot)

    def finish(mine, acc):
        o = (acc[:, :DEPTH] / acc[:, DEPTH:]).astype(BF)
        o_ref[pl.ds(mine * pieces, pieces)] = o.reshape(pieces, rows, DEPTH)

    @pl.when(fast)
    def _():
        def frame(mine, carry):
            pairs = [
                (part(0, mine + j), part(1, mine + j), used(mine, mine + j)) for j in range(W)
            ]
            acc = jnp.concatenate([acc_in[mine], side_in[mine]], axis=1)
            finish(mine, add_frames(acc, query(mine), pairs))
            return carry

        lax.fori_loop(0, BLOCK, frame, 0, unroll=True)

    @pl.when(jnp.logical_not(fast))
    def _():
        def frame(mine, carry):
            side = side_in[mine]
            quick = jnp.full((size, LANES), stat_ref[1], F32) > 0.5
            top = jnp.broadcast_to(side[:, LANES - 1 :], (size, LANES))
            m_ref[...] = jnp.where(quick, 0.0, top)
            acc_ref[:, :DEPTH] = acc_in[mine]
            acc_ref[:, DEPTH:] = jnp.broadcast_to(side[:, :1], (size, LANES))

            def pair(j, inner):
                @pl.when(used(mine, mine + j))
                def _():
                    fold_frame(query(mine), part(0, mine + j), part(1, mine + j), acc_ref, m_ref)

                return inner

            lax.fori_loop(0, W, pair, 0)
            finish(mine, acc_ref[...])
            return carry

        lax.fori_loop(0, BLOCK, frame, 0)


def attend_own(base, kb, bc, arrived, frames):
    dests, _, rows, depth = arrived.shape
    size = dests // BLOCK * rows
    return pl.pallas_call(
        functools.partial(own_kernel, frames),
        out_shape=[
            jax.ShapeDtypeStruct((BLOCK, size, depth), F32),
            jax.ShapeDtypeStruct((BLOCK, size, LANES), F32),
            jax.ShapeDtypeStruct((dests, 1, rows, depth), BF),
            jax.ShapeDtypeStruct((2,), F32),
        ],
        in_specs=[SMEM] * 3 + [VMEM],
        out_specs=[VMEM, VMEM, VMEM, SMEM],
        scratch_shapes=[pltpu.VMEM((size, 2 * depth), F32), pltpu.VMEM((size, LANES), F32)],
        compiler_params=PARAMS,
        cost_estimate=estimate(10),
    )(base, kb, bc, arrived)


def attend_near(base, kb, bc, stat, q, less, more, sums, frames):
    dests, _, rows, depth = q.shape
    size = dests // BLOCK * rows
    return pl.pallas_call(
        functools.partial(near_kernel, frames),
        out_shape=jax.ShapeDtypeStruct((dests, rows, depth), BF),
        in_specs=[SMEM] * 4 + [VMEM, ANY, ANY, VMEM, VMEM],
        out_specs=VMEM,
        scratch_shapes=[
            pltpu.VMEM((size, 2 * depth), F32),
            pltpu.VMEM((size, LANES), F32),
            pltpu.VMEM((2 * less.shape[0], *less.shape[1:]), BF),
            pltpu.SemaphoreType.DMA((2,)),
        ],
        compiler_params=PARAMS,
    )(base, kb, bc, stat, q, less, more, *sums)


def place_kernel(first, order_ref, src_ref, *refs):
    out, sems = refs[-2:]
    run_copies(
        [
            pltpu.make_async_copy(
                src_ref.at[head], out.at[:, :, columns_of(order_ref, first + head)], sems.at[head]
            )
            for head in range(src_ref.shape[0])
        ]
    )


def place(order, blocks, first, rows, width, before=()):
    heads, pieces, items, _ = blocks.shape
    return pl.pallas_call(
        functools.partial(place_kernel, first),
        out_shape=jax.ShapeDtypeStruct((pieces, items, width), BF),
        in_specs=[SMEM, VMEM] + [ANY] * len(before),
        out_specs=ANY,
        scratch_shapes=[pltpu.SemaphoreType.DMA((heads,))],
        input_output_aliases={2: 0} if before else {},
        compiler_params=PARAMS if before else PACK_PARAMS,
    )(order, blocks, *before)


def exchange(array, axes):
    return lax.all_to_all(array, axes, 0, 0, tiled=True)


def from_block(array, by):
    count = lax.axis_size("zh") * lax.axis_size("core") * lax.axis_size("yh")
    return lax.ppermute(array, ("zh", "core", "yh"), [((i + by) % count, i) for i in range(count)])


def local(queries, keys, values, head_order, key_blocks, block_count):
    rows, width = queries.shape
    blocks = lax.axis_size("zh") * lax.axis_size("core") * lax.axis_size("yh")
    frames = blocks * BLOCK
    items = HT * rows // frames
    base = lax.axis_index(("zh", "core", "yh")) * BLOCK
    base = base.astype(jnp.int32).reshape(1)

    block_axes = ("yl", "zl", "x")
    loop_axes = ("zh", "core", "yh", "yl", "zl")
    core = lax.axis_index("core").astype(jnp.int32).reshape(1)
    mine, other = pack_temporal(head_order, core, queries, keys, values, items)
    st = join(mine, lax.ppermute(other, "core", [(0, 1), (1, 0)]))
    qkv = exchange(pack_spatial(head_order, (queries, keys, values)), block_axes)
    pieces = qkv.shape[0] // BLOCK
    less = from_block(qkv[(BLOCK - W) * pieces :, 1:], -1)
    more = from_block(qkv[: W * pieces, 1:], 1)
    qkv, st = lax.optimization_barrier((qkv, st))
    at = exchange(st, ("zh", "yh", "yl", "zl"))
    *sums, q, stat = attend_own(base, key_blocks, block_count, qkv, frames)
    to, stat = lax.optimization_barrier((temporal_attend(core, at), stat))
    tr = exchange(to, loop_axes)
    so = attend_near(base, key_blocks, block_count, stat, q, less, more, sums, frames)
    sr = exchange(so, block_axes)
    by_head = (-1, rows // items, items, DEPTH)
    partial = place(head_order, tr.reshape(by_head), 0, rows, width)
    whole = place(head_order, sr.reshape(by_head), HT, rows, width, (partial,))
    return whole.reshape(rows, width)


def solution(mesh):
    grp, seq = mesh.shape["grp"], mesh.shape["seq"]
    names = ("zh", "core", "yh", "yl", "zl", "x")
    fine = Mesh(mesh.devices.reshape(grp // 2, 2, seq // 16, 2, 2, 4), names)
    tokens = P(names, None)
    return jax.shard_map(
        local,
        mesh=fine,
        in_specs=(tokens, tokens, tokens, P(), P(), P()),
        out_specs=tokens,
        check_vma=False,
    )
```
